32 devices in a mesh: feeder: 8 (over z, x), node: 4 (over y, core).
Axes of the slice: x: 2, y: 2, z: 4, core: 2. Of those that a mesh axis runs over, the one named last changes fastest.
Arguments:
- factors: bfloat16 [2048, 256], P('node'), may hold values from -6 to 6
- loadings: bfloat16 [4096, 256], P(('feeder', 'node')), may hold values from -0.35355339 to 0.5
- parents: int32 [4096], P(('feeder', 'node')), may hold values from -1 to 126, as said below
- load_base: float32 [2, 4096], P(None, ('feeder', 'node')), may hold values from 1.953125e-05 to 0.00390625, as said below
- lateral_z: float32 [2, 4096], P(None, ('feeder', 'node')), may hold values from 0.000875 to 0.021875, as said below
- trunk_z: float32 [2, 8, 4], P(None, 'feeder', 'node'), may hold values from 0.00275 to 0.04875, as said below
Outputs:
- volt_real: float32 [2048, 4096], P(None, ('feeder', 'node'))
- volt_imag: float32 [2048, 4096], P(None, ('feeder', 'node'))
The draws below stay inside these ranges and needn't reach their ends.
Inputs may be any that keep to these rules, and one draw needn't show every extreme that they name: `parents`: within each aligned run of 128 nodes (one lateral), a node's entry is the position of its parent in the same lateral, which comes before it, or -1 for a branch from the section's head node; the first node of every lateral has -1 and the last node's parent is the node just before it. `load_base`: with unit = 1 / 1024, row 0 lies between 1 and 4 units and row 1 between 0.02 and 0.08 units. `lateral_z`: with unit = 128 * 8 / 128^2, row 0 lies between 0.014 and 0.056 units and row 1 between 0.087 and 0.35 units. `trunk_z`: with unit = 1 / 8, row 0 lies between 0.022 and 0.066 units and row 1 between 0.13 and 0.39 units.
All inputs are finite; a program needn't handle non-finite values.
Results may differ from the reference program's by a relative error of at most 0.0003.
Values may be sent and summed in bfloat16 or wider, within the bound.
No kernel may reach another device: no remote copies, remote signals or barrier semaphores. Data moves between devices by JAX's collectives and lax.ppermute only.
A program may use at most 64 MiB of HBM per device.

```python
import jax
import jax.numpy as jnp
from jax import lax

R = 256
LAT_NODES = 128
LAT_DEV = 1
SCEN = 2048
SWEEPS = 3
NODES_DEV = 128
SECTIONS = 8
CIRCUITS = 4
NODES = 4096


def draw_factors(key, part):
    common = jax.random.uniform(jax.random.fold_in(key, 61), (SCEN, 1), jnp.float32, -6.0, 6.0)
    others = jnp.clip(jax.random.normal(jax.random.fold_in(key, 67), (SCEN, R - 1), jnp.float32), -6.0, 6.0)
    return jnp.concatenate([common, others], axis=1).astype(jnp.bfloat16)


def draw_loadings(key, part):
    spread = (R // 2) ** (-0.5)
    common = jax.random.uniform(jax.random.fold_in(key, 71), (NODES, 1), jnp.float32, 0.3, 0.5)
    others = spread * jnp.clip(jax.random.normal(jax.random.fold_in(key, 73), (NODES, R - 1), jnp.float32), -4.0, 4.0)
    return jnp.concatenate([common, others], axis=1).astype(jnp.bfloat16)


def draw_parents(key, part):
    position = jnp.arange(NODES, dtype=jnp.int32) % LAT_NODES
    stride = jax.random.randint(jax.random.fold_in(key, 17), (NODES,), 1, 5, dtype=jnp.int32)
    parent_pos = position - stride
    parent_pos = jnp.where(parent_pos < -1, -1, parent_pos)
    parent_pos = jnp.where(position == 0, -1, parent_pos)
    parent_pos = jnp.where(position == LAT_NODES - 1, LAT_NODES - 2, parent_pos)
    return parent_pos.astype(jnp.int32)


def log_between(key, shape, low, high):
    unit_draw = jax.random.uniform(key, shape, jnp.float32)
    return low * jnp.exp(unit_draw * jnp.log(high / low))


def draw_load_base(key, part):
    scale = 1.0 / (NODES_DEV * SECTIONS)
    active = log_between(jax.random.fold_in(key, 31), (NODES,), scale, 4.0 * scale)
    reactive = log_between(jax.random.fold_in(key, 37), (NODES,), 0.02 * scale, 0.08 * scale)
    return jnp.stack([active, reactive]).astype(jnp.float32)


def draw_lateral_z(key, part):
    scale = NODES_DEV * SECTIONS / (LAT_NODES * LAT_NODES)
    resist = log_between(jax.random.fold_in(key, 41), (NODES,), 0.014 * scale, 0.056 * scale)
    react = log_between(jax.random.fold_in(key, 43), (NODES,), 0.087 * scale, 0.35 * scale)
    return jnp.stack([resist, react]).astype(jnp.float32)


def draw_trunk_z(key, part):
    scale = 1.0 / SECTIONS
    resist = log_between(jax.random.fold_in(key, 47), (SECTIONS, CIRCUITS), 0.022 * scale, 0.066 * scale)
    react = log_between(jax.random.fold_in(key, 53), (SECTIONS, CIRCUITS), 0.13 * scale, 0.39 * scale)
    return jnp.stack([resist, react]).astype(jnp.float32)


def setup_inputs(seed: int = 0) -> dict:
    key_of = jax.random.split(jax.random.key(seed), 7)
    factors = draw_factors(jax.random.fold_in(key_of[6], 71), 0)
    loadings = draw_loadings(jax.random.fold_in(key_of[6], 71), 0)
    parents = draw_parents(jax.random.fold_in(key_of[6], 71), 0)
    load_base = draw_load_base(jax.random.fold_in(key_of[6], 71), 0)
    lateral_z = draw_lateral_z(jax.random.fold_in(key_of[6], 71), 0)
    trunk_z = draw_trunk_z(jax.random.fold_in(key_of[6], 71), 0)
    return {"factors": factors, "loadings": loadings, "parents": parents, "load_base": load_base, "lateral_z": lateral_z, "trunk_z": trunk_z}


HIGHEST = lax.Precision.HIGHEST


def path_matrix(parent_rows):
    laterals, width = parent_rows.shape
    column = jnp.arange(width, dtype=jnp.int32)
    adjacency = (parent_rows[:, :, None] == column[None, None, :]).astype(jnp.float32)
    identity = jnp.eye(width, dtype=jnp.float32)
    paths = identity[None] + adjacency
    power = adjacency
    for turn in range((width - 1).bit_length() - 1):
        power = jnp.einsum("alm,amn->aln", power, power, precision=HIGHEST)
        paths = paths + jnp.einsum("alm,amn->aln", paths, power, precision=HIGHEST)
    return paths


def node_currents(active, reactive, real_part, imag_part):
    magnitude = real_part * real_part + imag_part * imag_part
    return (active * real_part + reactive * imag_part) / magnitude, (active * imag_part - reactive * real_part) / magnitude


def reference(factors, loadings, parents, load_base, lateral_z, trunk_z):
    level = jnp.dot(factors, loadings.T, preferred_element_type=jnp.float32).astype(jnp.bfloat16)
    width = NODES_DEV * CIRCUITS
    scen = factors.shape[0]
    lat_count = CIRCUITS * LAT_DEV
    section_data = []
    for section_index in range(SECTIONS):
        lower = section_index * width
        swing = 1.0 + 0.5 * jnp.tanh(level[:, lower:lower + width].astype(jnp.float32))
        active = load_base[0, lower:lower + width][None, :] * swing
        reactive = load_base[1, lower:lower + width][None, :] * swing
        paths = path_matrix(parents[lower:lower + width].reshape(lat_count, LAT_NODES))
        resist = lateral_z[0, lower:lower + width].reshape(lat_count, LAT_NODES)
        react = lateral_z[1, lower:lower + width].reshape(lat_count, LAT_NODES)
        section_data.append((active, reactive, paths, resist, react))
    volts = [(jnp.ones((scen, width), jnp.float32), jnp.zeros((scen, width), jnp.float32)) for section_index in range(SECTIONS)]
    for sweep_index in range(SWEEPS):
        currents = []
        inject_real = []
        inject_imag = []
        for section_index in range(SECTIONS):
            active, reactive, paths, resist, react = section_data[section_index]
            current_real, current_imag = node_currents(active, reactive, volts[section_index][0], volts[section_index][1])
            currents.append((current_real, current_imag))
            inject_real.append(jnp.sum(current_real.reshape(scen, CIRCUITS, NODES_DEV), axis=2))
            inject_imag.append(jnp.sum(current_imag.reshape(scen, CIRCUITS, NODES_DEV), axis=2))
        inject_real = jnp.stack(inject_real)
        inject_imag = jnp.stack(inject_imag)
        trunk_real = jnp.flip(jnp.cumsum(jnp.flip(inject_real, 0), 0), 0)
        trunk_imag = jnp.flip(jnp.cumsum(jnp.flip(inject_imag, 0), 0), 0)
        resist_trunk = trunk_z[0][:, None, :]
        react_trunk = trunk_z[1][:, None, :]
        drop_real = resist_trunk * trunk_real - react_trunk * trunk_imag
        drop_imag = resist_trunk * trunk_imag + react_trunk * trunk_real
        head_real = 1.0 - jnp.cumsum(drop_real, 0)
        head_imag = -jnp.cumsum(drop_imag, 0)
        new_volts = []
        for section_index in range(SECTIONS):
            active, reactive, paths, resist, react = section_data[section_index]
            current_real, current_imag = currents[section_index]
            stacked = jnp.stack([current_real, current_imag]).reshape(2, scen, lat_count, LAT_NODES)
            branch = jnp.einsum("csal,alm->csam", stacked, paths, precision=HIGHEST)
            weighted = jnp.stack([resist * branch[0] - react * branch[1], resist * branch[1] + react * branch[0]])
            drops = jnp.einsum("csam,alm->csal", weighted, paths, precision=HIGHEST).reshape(2, scen, width)
            base_real = jnp.repeat(head_real[section_index], NODES_DEV, axis=1)
            base_imag = jnp.repeat(head_imag[section_index], NODES_DEV, axis=1)
            new_volts.append((base_real - drops[0], base_imag - drops[1]))
        volts = new_volts
    volt_real = jnp.concatenate([volts[section_index][0] for section_index in range(SECTIONS)], axis=1)
    volt_imag = jnp.concatenate([volts[section_index][1] for section_index in range(SECTIONS)], axis=1)
    return volt_real, volt_imag
```

```python
import jax
import jax.numpy as jnp
from jax import lax
from jax.sharding import PartitionSpec as P

LAT_NODES = 128
SWEEPS = 3


HIGHEST = lax.Precision.HIGHEST


def path_matrix(parent_rows):
    laterals, width = parent_rows.shape
    column = jnp.arange(width, dtype=jnp.int32)
    adjacency = (parent_rows[:, :, None] == column[None, None, :]).astype(jnp.bfloat16)
    identity = jnp.eye(width, dtype=jnp.bfloat16)
    paths = identity[None] + adjacency
    power = adjacency
    for turn in range((width - 1).bit_length() - 1):
        power = jnp.einsum("alm,amn->aln", power, power)
        paths = paths + jnp.einsum("alm,amn->aln", paths, power)
    return paths


def node_currents(active, reactive, real_part, imag_part):
    magnitude = real_part * real_part + imag_part * imag_part
    return (
        (active * real_part + reactive * imag_part) / magnitude,
        (active * imag_part - reactive * real_part) / magnitude,
    )


def lateral_products(stacked, table):
    high = stacked.astype(jnp.bfloat16)
    low = (stacked - high.astype(jnp.float32)).astype(jnp.bfloat16)
    both = jnp.concatenate([high, low], axis=1)
    return jnp.dot(both, jnp.concatenate([table, table]), preferred_element_type=jnp.float32)


def xor_gather(block, axis, size):
    held = block[None]
    step = 1
    while step < size:
        other = lax.ppermute(held, axis, [(i, i ^ step) for i in range(size)])
        held = jnp.concatenate([held, other])
        step *= 2
    return held


def trunk_table(z_all, index):
    size = z_all.shape[0]
    section = index ^ jnp.arange(size, dtype=jnp.int32)
    shared = (section[None, :] <= jnp.minimum(index, section)[:, None]).astype(jnp.float32)
    return jnp.sum(shared[:, :, None] * z_all[None], axis=1)


def local(feeders, nodes, factors, loadings, parents, load_base, lateral_z, trunk_z):
    node = lax.axis_index("node")
    feeder = lax.axis_index("feeder")
    rows = factors.shape[0]
    scen = rows * nodes
    held = factors[None]
    order = [0]
    step = nodes // 2
    while step >= 1:
        other = lax.ppermute(held, "node", [(i, i ^ step) for i in range(nodes)])
        held = jnp.concatenate([held, other])
        order = order + [o ^ step for o in order]
        step //= 2
    whole = jnp.zeros((scen, factors.shape[1]), factors.dtype)
    for place, offset in enumerate(order):
        whole = lax.dynamic_update_slice(whole, held[place], ((node ^ offset) * rows, 0))
    levels = jnp.einsum("sr,nr->sn", whole, loadings, preferred_element_type=jnp.float32).astype(jnp.bfloat16)
    nodes_here = levels.shape[1]
    swing = 1.0 + 0.5 * jnp.tanh(levels.astype(jnp.float32))
    active = load_base[0][None, :] * swing
    reactive = load_base[1][None, :] * swing
    paths = path_matrix(parents.reshape(1, LAT_NODES))[0]
    resist = lateral_z[0][None, :]
    react = lateral_z[1][None, :]
    volts = None
    table = None
    for sweep_index in range(SWEEPS):
        if volts is None:
            current_real, current_imag = active, -reactive
        else:
            current_real, current_imag = node_currents(active, reactive, volts[:scen], volts[scen:])
        current = jnp.concatenate([current_real, current_imag])
        inject = jnp.sum(current, axis=1).reshape(2, scen // 128, 128)
        if table is None:
            extra = jnp.broadcast_to(trunk_z.reshape(2, 1, 1), (2, 8, 128))
            every = xor_gather(jnp.concatenate([inject, extra], axis=1), "feeder", feeders)
            table = trunk_table(every[:, :, scen // 128, 0], feeder)
            every = every[:, :, : scen // 128]
        else:
            every = xor_gather(inject, "feeder", feeders)
        branch = lateral_products(current, paths)
        branch_real = branch[:scen]
        branch_imag = branch[scen:]
        weighted = jnp.concatenate(
            [resist * branch_real - react * branch_imag, resist * branch_imag + react * branch_real]
        )
        drops = lateral_products(weighted, paths.T)
        r = table[:, 0, None, None]
        x = table[:, 1, None, None]
        head_real = 1.0 - jnp.sum(r * every[:, 0] - x * every[:, 1], axis=0).reshape(scen)
        head_imag = -jnp.sum(r * every[:, 1] + x * every[:, 0], axis=0).reshape(scen)
        volts = jnp.concatenate(
            [head_real[:, None] - drops[:scen], head_imag[:, None] - drops[scen:]]
        )
    return (volts[:scen], volts[scen:])


def solution(mesh):
    feeders = mesh.shape["feeder"]
    nodes = mesh.shape["node"]

    def part(*args):
        return local(feeders, nodes, *args)

    return jax.shard_map(
        part,
        mesh=mesh,
        in_specs=(
            P("node", None),
            P(("feeder", "node"), None),
            P(("feeder", "node")),
            P(None, ("feeder", "node")),
            P(None, ("feeder", "node")),
            P(None, "feeder", "node"),
        ),
        out_specs=(P(None, ("feeder", "node")), P(None, ("feeder", "node"))),
        check_vma=False,
    )
```

```python
import jax
import jax.numpy as jnp
from jax import lax
from jax.sharding import PartitionSpec as P

LAT_NODES = 128
SWEEPS = 3


HIGHEST = lax.Precision.HIGHEST


def path_matrix(parent_rows):
    laterals, width = parent_rows.shape
    column = jnp.arange(width, dtype=jnp.int32)
    adjacency = (parent_rows[:, :, None] == column[None, None, :]).astype(jnp.bfloat16)
    identity = jnp.eye(width, dtype=jnp.bfloat16)
    paths = identity[None] + adjacency
    power = adjacency
    for turn in range((width - 1).bit_length() - 1):
        power = jnp.einsum("alm,amn->aln", power, power)
        paths = paths + jnp.einsum("alm,amn->aln", paths, power)
    return paths


def node_currents(active, reactive, real_part, imag_part):
    magnitude = real_part * real_part + imag_part * imag_part
    return (
        (active * real_part + reactive * imag_part) / magnitude,
        (active * imag_part - reactive * real_part) / magnitude,
    )


def lateral_products(stacked, table):
    high = stacked.astype(jnp.bfloat16)
    low = (stacked - high.astype(jnp.float32)).astype(jnp.bfloat16)
    both = jnp.concatenate([high, low], axis=1)
    return jnp.dot(both, jnp.concatenate([table, table]), preferred_element_type=jnp.float32)


def spread_gather(block, axis, size):
    return lax.all_to_all(jnp.broadcast_to(block[None], (size, *block.shape)), axis, 0, 0, tiled=True)


def trunk_table(z_all, index):
    size = z_all.shape[0]
    section = jnp.arange(size, dtype=jnp.int32)
    shared = (section[None, :] <= jnp.minimum(index, section)[:, None]).astype(jnp.float32)
    return jnp.sum(shared[:, :, None] * z_all[None], axis=1)


def local(feeders, nodes, factors, loadings, parents, load_base, lateral_z, trunk_z):
    node = lax.axis_index("node")
    feeder = lax.axis_index("feeder")
    rows = factors.shape[0]
    scen = rows * nodes
    held = factors[None]
    order = [0]
    step = nodes // 2
    while step >= 1:
        other = lax.ppermute(held, "node", [(i, i ^ step) for i in range(nodes)])
        held = jnp.concatenate([held, other])
        order = order + [o ^ step for o in order]
        step //= 2
    whole = jnp.zeros((scen, factors.shape[1]), factors.dtype)
    for place, offset in enumerate(order):
        whole = lax.dynamic_update_slice(whole, held[place], ((node ^ offset) * rows, 0))
    levels = jnp.einsum("sr,nr->sn", whole, loadings, preferred_element_type=jnp.float32).astype(jnp.bfloat16)
    nodes_here = levels.shape[1]
    swing = 1.0 + 0.5 * jnp.tanh(levels.astype(jnp.float32))
    active = load_base[0][None, :] * swing
    reactive = load_base[1][None, :] * swing
    paths = path_matrix(parents.reshape(1, LAT_NODES))[0]
    resist = lateral_z[0][None, :]
    react = lateral_z[1][None, :]
    volts = None
    table = None
    for sweep_index in range(SWEEPS):
        if volts is None:
            current_real, current_imag = active, -reactive
        else:
            current_real, current_imag = node_currents(active, reactive, volts[:scen], volts[scen:])
        current = jnp.concatenate([current_real, current_imag])
        inject = jnp.sum(current, axis=1).reshape(2, scen // 128, 128)
        if table is None:
            extra = jnp.broadcast_to(trunk_z.reshape(2, 1, 1), (2, 8, 128))
            every = spread_gather(jnp.concatenate([inject, extra], axis=1), "feeder", feeders)
            table = trunk_table(every[:, :, scen // 128, 0], feeder)
            every = every[:, :, : scen // 128]
        else:
            every = spread_gather(inject, "feeder", feeders)
        branch = lateral_products(current, paths)
        branch_real = branch[:scen]
        branch_imag = branch[scen:]
        weighted = jnp.concatenate(
            [resist * branch_real - react * branch_imag, resist * branch_imag + react * branch_real]
        )
        drops = lateral_products(weighted, paths.T)
        r = table[:, 0, None, None]
        x = table[:, 1, None, None]
        head_real = 1.0 - jnp.sum(r * every[:, 0] - x * every[:, 1], axis=0).reshape(scen)
        head_imag = -jnp.sum(r * every[:, 1] + x * every[:, 0], axis=0).reshape(scen)
        volts = jnp.concatenate(
            [head_real[:, None] - drops[:scen], head_imag[:, None] - drops[scen:]]
        )
    return (volts[:scen], volts[scen:])


def solution(mesh):
    feeders = mesh.shape["feeder"]
    nodes = mesh.shape["node"]

    def part(*args):
        return local(feeders, nodes, *args)

    return jax.shard_map(
        part,
        mesh=mesh,
        in_specs=(
            P("node", None),
            P(("feeder", "node"), None),
            P(("feeder", "node")),
            P(None, ("feeder", "node")),
            P(None, ("feeder", "node")),
            P(None, "feeder", "node"),
        ),
        out_specs=(P(None, ("feeder", "node")), P(None, ("feeder", "node"))),
        check_vma=False,
    )
```

```python
import functools

import jax
import jax.numpy as jnp
from jax import lax
from jax.experimental import pallas as pl
from jax.experimental.pallas import tpu as pltpu
from jax.sharding import PartitionSpec as P

SWEEPS = 3
EXTRA = 16
LANES = 128

VMEM = pl.BlockSpec(memory_space=pltpu.VMEM)
SMEM = pl.BlockSpec(memory_space=pltpu.SMEM)


def split(x):
    high = x.astype(jnp.bfloat16)
    low = (x - high.astype(jnp.float32)).astype(jnp.bfloat16)
    return high, low


def product(left, right):
    return jnp.dot(left, right, preferred_element_type=jnp.float32)


def product_nt(left, right):
    return lax.dot_general(left, right, (((1,), (1,)), ((), ())), preferred_element_type=jnp.float32)


def wide(row, width):
    n = row.shape[1]
    if width <= n:
        return row[:, :width]
    return jnp.concatenate([row] * (width // n), axis=1)


def pack_kernel(feeders, trunk_ref, loadings_ref, parents_ref, base_ref, z_ref, out_ref, rows_ref, meta_ref):
    n = loadings_ref.shape[0]
    rows_ref[0:2, :] = base_ref[...]
    rows_ref[2:4, :] = z_ref[...]
    rows_ref[4:5, :] = jnp.full((1, n), trunk_ref[0], jnp.float32)
    rows_ref[5:6, :] = jnp.full((1, n), trunk_ref[1], jnp.float32)
    rows_ref[6:7, :] = parents_ref[...].astype(jnp.float32)
    rows_ref[7:8, :] = jnp.zeros((1, n), jnp.float32)
    rows = rows_ref[...]
    high = rows.astype(jnp.bfloat16).astype(jnp.float32)
    middle = (rows - high).astype(jnp.bfloat16).astype(jnp.float32)
    low = rows - high - middle
    meta_ref[0:8, 0:n] = high
    meta_ref[0:8, n : 2 * n] = middle
    meta_ref[8:16, 0:n] = low
    meta_ref[8:16, n : 2 * n] = jnp.zeros_like(low)
    meta = meta_ref[...].astype(jnp.bfloat16)
    loadings = loadings_ref[...]
    for to in range(feeders):
        out_ref[to, 0:n, :] = loadings
        out_ref[to, n : n + EXTRA, :] = meta


def section_matrix(parts, n):
    high, middle, low = parts[0:8, 0:n], parts[0:8, n : 2 * n], parts[8:16, 0:n]
    rows = high + middle + low
    row_ids = lax.broadcasted_iota(jnp.int32, (n, n), 0)
    lane_ids = lax.broadcasted_iota(jnp.int32, (n, n), 1)
    children = (jnp.broadcast_to(rows[6:7], (n, n)) == row_ids.astype(jnp.float32)).astype(jnp.bfloat16)
    identity = (row_ids == lane_ids).astype(jnp.bfloat16)
    power = product_nt(identity, children).astype(jnp.bfloat16)
    paths = identity + power
    reach = 2
    power = product(power, power).astype(jnp.bfloat16)
    while reach < n:
        if 2 * reach < n:
            both = product(power, jnp.concatenate([power, paths], axis=1))
            paths = paths + both[:, n:].astype(jnp.bfloat16)
            power = both[:, :n].astype(jnp.bfloat16)
        else:
            paths = paths + product(power, paths).astype(jnp.bfloat16)
        reach *= 2
    paths32 = paths.astype(jnp.float32)

    def scaled(index):
        return jnp.concatenate([paths32 * high[index : index + 1], paths32 * middle[index : index + 1]], axis=1)

    left = jnp.concatenate([scaled(2), scaled(3)], axis=0).astype(jnp.bfloat16)
    shared = product_nt(left, jnp.concatenate([paths, paths], axis=1))
    resist, react = shared[:n], shared[n:]
    base_active, base_reactive = rows[0:1], rows[1:2]
    real = resist * base_active + react * base_reactive
    imag = react * base_active - resist * base_reactive
    real_high, real_low = split(real)
    imag_high, imag_low = split(imag)
    pad_ids = lax.broadcasted_iota(jnp.int32, (EXTRA, 2 * n), 0)
    row_real = jnp.concatenate([base_active, base_reactive], axis=1)
    row_imag = jnp.concatenate([-base_reactive, base_active], axis=1)
    sums = jnp.where(pad_ids == 0, row_real, jnp.where(pad_ids == 1, row_imag, 0.0))
    sums_high, sums_low = split(sums)

    def whole(real_part, imag_part, sums_part):
        top = jnp.concatenate([real_part, -imag_part], axis=1)
        bottom = jnp.concatenate([imag_part, real_part], axis=1)
        return jnp.concatenate([top, bottom, sums_part], axis=0)

    return jnp.concatenate(
        [whole(real_high, imag_high, sums_high), whole(real_low, imag_low, sums_low)], axis=0
    )


def swing_of(loadings, factors):
    level = product_nt(loadings, factors).astype(jnp.bfloat16).astype(jnp.float32)
    return 1.0 + 0.5 * jnp.tanh(level)


def apply(matrix, high, low):
    half = matrix.shape[0] // 2
    first = product(matrix, high)
    return first[:half] + first[half:] + product(matrix[:half], low)


def scaled_volts(swing, real, imag):
    inverse = swing / (real * real + imag * imag)
    return jnp.concatenate([real * inverse, imag * inverse], axis=0)


def heads_kernel(
    feeders, pieces, place_ref, every_ref, *refs
):
    piece_refs, (head_ref, own_ref, factors_ref, matrix_ref, swing_ref, drop_ref, inject_ref) = refs[:pieces], refs[pieces:]
    rows = piece_refs[0].shape[0]
    width = factors_ref.shape[0]
    n = swing_ref.shape[1]
    span = 2 * n
    piece, offset = place_ref[0], place_ref[1]
    for index, piece_ref in enumerate(piece_refs):
        @pl.when(piece == index)
        def _(piece_ref=piece_ref):
            factors_ref[...] = piece_ref[pl.ds(pl.multiple_of(offset, width), width), :]
    group = min(feeders, 8)

    def sections(body):
        if group == feeders:
            for g in range(feeders):
                body(g)
        else:
            @pl.loop(0, feeders // group)
            def _(outer):
                for inner in range(group):
                    body(outer * group + inner)

    def first(g):
        matrix_ref[g] = section_matrix(every_ref[g, n : n + EXTRA, :].astype(jnp.float32), n)
        swing = swing_of(every_ref[g, 0:n, :], factors_ref[...])
        swing_ref[g] = swing
        high, low = split(swing)
        out = apply(matrix_ref[g][:, :n], high, low)
        drop_ref[g] = out[:span]
        inject_ref[g] = out[span:]

    sections(first)

    def trunk_row(g, index):
        parts = every_ref[g, n : n + EXTRA, :].astype(jnp.float32)
        row = parts[index : index + 1, 0:n] + parts[index : index + 1, n : 2 * n] + parts[index + 8 : index + 9, 0:n]
        return wide(row, width)

    trunk = [(trunk_row(g, 4), trunk_row(g, 5)) for g in range(feeders)]

    def heads(sweep):
        flows = [None] * feeders
        real = jnp.zeros((1, width), jnp.float32)
        imag = real
        for g in reversed(range(feeders)):
            real = real + inject_ref[g, 0:1, :]
            imag = imag + inject_ref[g, 1:2, :]
            flows[g] = (real, imag)
        head_real = jnp.ones((1, width), jnp.float32)
        head_imag = jnp.zeros((1, width), jnp.float32)
        for g in range(feeders):
            r, x = trunk[g]
            real, imag = flows[g]
            head_real = head_real - (r * real - x * imag)
            head_imag = head_imag - (r * imag + x * real)
            head_ref[g, 2 * sweep : 2 * sweep + 1, :] = head_real
            head_ref[g, 2 * sweep + 1 : 2 * sweep + 2, :] = head_imag

    heads(0)
    for sweep in range(1, SWEEPS):
        last = sweep == SWEEPS - 1

        def again(g, sweep=sweep, last=last):
            real = head_ref[g, 2 * sweep - 2 : 2 * sweep - 1, :] - drop_ref[g, 0:n, :]
            imag = head_ref[g, 2 * sweep - 1 : 2 * sweep, :] - drop_ref[g, n:span, :]
            high, low = split(scaled_volts(swing_ref[g], real, imag))
            if last:
                half = span + EXTRA
                row_high = matrix_ref[g, span:half, :]
                row_low = matrix_ref[g, half + span :, :]
                inject_ref[g] = product(row_high, high) + product(row_low, high) + product(row_high, low)
            else:
                out = apply(matrix_ref[g], high, low)
                drop_ref[g] = out[:span]
                inject_ref[g] = out[span:]

        sections(again)
        heads(sweep)
    for g in range(feeders):
        head_ref[g, 2 * SWEEPS :, :] = jnp.zeros((head_ref.shape[1] - 2 * SWEEPS, width), jnp.float32)
    own_ref[...] = matrix_ref[place_ref[2]]


def first_kernel(pieces, node_ref, matrix_ref, loadings_ref, *refs):
    piece_refs, (swing_ref, drop_ref) = refs[:pieces], refs[pieces:]
    n = loadings_ref.shape[0]
    width = swing_ref.shape[2]
    chunks = piece_refs[0].shape[0] // width
    loadings = loadings_ref[...]
    half = matrix_ref.shape[0] // 2
    matrix = jnp.concatenate([matrix_ref[0 : 2 * n, 0:n], matrix_ref[half : half + 2 * n, 0:n]], axis=0)
    for index, piece_ref in enumerate(piece_refs):
        for part in range(chunks):
            chunk = jnp.bitwise_xor(node_ref[0], index) * chunks + part
            swing = swing_of(loadings, piece_ref[part * width : (part + 1) * width, :])
            swing_ref[chunk] = swing
            high, low = split(swing)
            drop_ref[chunk] = apply(matrix, high, low)


def volts_kernel(matrix_ref, swing_ref, drop_ref, head_ref, real_ref, imag_ref):
    n = swing_ref.shape[1]
    width = swing_ref.shape[2]
    half = matrix_ref.shape[0] // 2
    matrix = jnp.concatenate([matrix_ref[0 : 2 * n, :], matrix_ref[half : half + 2 * n, :]], axis=0)
    for chunk in range(swing_ref.shape[0]):
        drop = drop_ref[chunk]
        for sweep in range(SWEEPS):
            real = head_ref[chunk, 2 * sweep : 2 * sweep + 1, :] - drop[:n]
            imag = head_ref[chunk, 2 * sweep + 1 : 2 * sweep + 2, :] - drop[n:]
            if sweep < SWEEPS - 1:
                high, low = split(scaled_volts(swing_ref[chunk], real, imag))
                drop = apply(matrix, high, low)
        real_ref[chunk * width : (chunk + 1) * width, :] = real.T
        imag_ref[chunk * width : (chunk + 1) * width, :] = imag.T


def limit(nbytes):
    return pltpu.CompilerParams(vmem_limit_bytes=min(60 << 20, int(nbytes) + (16 << 20)))


def local(feeders, nodes, factors, loadings, parents, load_base, lateral_z, trunk_z):
    node = lax.axis_index("node").astype(jnp.int32)
    feeder = lax.axis_index("feeder").astype(jnp.int32)
    rows, rank = factors.shape
    scen = rows * nodes
    n = loadings.shape[0]
    width = max(scen // feeders, LANES)
    share = feeders * width // scen
    f32, bf16 = jnp.float32, jnp.bfloat16
    matrix_rows = 2 * (2 * n + EXTRA)

    packed = pl.pallas_call(
        functools.partial(pack_kernel, feeders),
        out_shape=jax.ShapeDtypeStruct((feeders, n + EXTRA, rank), bf16),
        in_specs=[SMEM, VMEM, VMEM, VMEM, VMEM],
        out_specs=VMEM,
        scratch_shapes=[pltpu.VMEM((8, n), f32), pltpu.VMEM((EXTRA, rank), f32)],
        compiler_params=limit(feeders * (n + EXTRA) * rank * 2),
        name="pack",
    )(trunk_z.reshape(2), loadings, parents.reshape(1, n), load_base, lateral_z)
    every = lax.all_to_all(packed, "feeder", 0, 0, tiled=True)

    held = {0: factors}
    step = nodes // 2
    while step >= 1:
        pairs = [(i, i ^ step) for i in range(nodes)]
        for offset in list(held):
            held[offset ^ step] = lax.ppermute(held[offset], "node", pairs)
        step //= 2
    pieces = [held[offset] for offset in range(nodes)]

    start = (feeder // share) * width
    place = jnp.stack([(start // rows) ^ node, start % rows, feeder])
    heads, matrix = pl.pallas_call(
        functools.partial(heads_kernel, feeders, nodes),
        out_shape=(
            jax.ShapeDtypeStruct((feeders, 8, width), f32),
            jax.ShapeDtypeStruct((matrix_rows, 2 * n), bf16),
        ),
        in_specs=[SMEM] + [VMEM] * (1 + nodes),
        out_specs=(VMEM, VMEM),
        scratch_shapes=[
            pltpu.VMEM((width, rank), bf16),
            pltpu.VMEM((feeders, matrix_rows, 2 * n), bf16),
            pltpu.VMEM((feeders, n, width), f32),
            pltpu.VMEM((feeders, 2 * n, width), f32),
            pltpu.VMEM((feeders, EXTRA, width), f32),
        ],
        compiler_params=limit(feeders * (matrix_rows * 4 * n + 3 * n * width * 4 + EXTRA * width * 4 + (n + EXTRA) * rank * 2)),
        name="heads",
    )(place, every, *pieces)
    given = lax.all_to_all(heads, "feeder", 0, 0, tiled=True)
    given = given[::share]

    chunks = scen // width
    swing, drop = pl.pallas_call(
        functools.partial(first_kernel, nodes),
        out_shape=(
            jax.ShapeDtypeStruct((chunks, n, width), f32),
            jax.ShapeDtypeStruct((chunks, 2 * n, width), f32),
        ),
        in_specs=[SMEM] + [VMEM] * (2 + nodes),
        out_specs=(VMEM, VMEM),
        compiler_params=limit(3 * n * scen * 4 + scen * rank * 2),
        cost_estimate=pl.CostEstimate(flops=2 * scen * n * rank * 4, bytes_accessed=3 * n * scen * 4, transcendentals=scen * n),
        name="first",
    )(node.reshape(1), matrix, loadings, *pieces)
    return pl.pallas_call(
        volts_kernel,
        out_shape=(
            jax.ShapeDtypeStruct((scen, n), f32),
            jax.ShapeDtypeStruct((scen, n), f32),
        ),
        in_specs=[VMEM] * 4,
        out_specs=(VMEM, VMEM),
        compiler_params=limit(5 * n * scen * 4),
        name="volts",
    )(matrix, swing, drop, given)


def solution(mesh):
    feeders = mesh.shape["feeder"]
    nodes = mesh.shape["node"]
    return jax.shard_map(
        functools.partial(local, feeders, nodes),
        mesh=mesh,
        in_specs=(
            P("node", None),
            P(("feeder", "node"), None),
            P(("feeder", "node")),
            P(None, ("feeder", "node")),
            P(None, ("feeder", "node")),
            P(None, "feeder", "node"),
        ),
        out_specs=(P(None, ("feeder", "node")), P(None, ("feeder", "node"))),
        check_vma=False,
    )
```

```python
import functools

import jax
import jax.numpy as jnp
from jax import lax
from jax.experimental import pallas as pl
from jax.experimental.pallas import tpu as pltpu
from jax.sharding import PartitionSpec as P

SWEEPS = 3
EXTRA = 16
LANES = 128

VMEM = pl.BlockSpec(memory_space=pltpu.VMEM)
SMEM = pl.BlockSpec(memory_space=pltpu.SMEM)
HBM = pl.BlockSpec(memory_space=pltpu.HBM)


def split(x):
    high = x.astype(jnp.bfloat16)
    low = (x - high.astype(jnp.float32)).astype(jnp.bfloat16)
    return high, low


def product(left, right):
    return jnp.dot(left, right, preferred_element_type=jnp.float32)


def product_nt(left, right):
    return lax.dot_general(left, right, (((1,), (1,)), ((), ())), preferred_element_type=jnp.float32)


def wide(row, width):
    n = row.shape[1]
    if width <= n:
        return row[:, :width]
    return jnp.concatenate([row] * (width // n), axis=1)


def pack_kernel(
    feeders, trunk_ref, loadings_ref, parents_ref, base_ref, z_ref, out_ref, trunk, loads, owners, rows_ref, meta_ref, sems
):
    n = loadings_ref.shape[0]
    copies = [
        pltpu.make_async_copy(loadings_ref, loads, sems.at[0]),
        pltpu.make_async_copy(parents_ref, owners, sems.at[1]),
        pltpu.make_async_copy(base_ref, rows_ref.at[0], sems.at[2]),
        pltpu.make_async_copy(z_ref, rows_ref.at[1], sems.at[3]),
        pltpu.make_async_copy(trunk_ref, trunk, sems.at[4]),
    ]
    for copy in copies:
        copy.start()
    for copy in copies[1:]:
        copy.wait()
    pair_ids = lax.broadcasted_iota(jnp.int32, (2, n), 0)
    trunk_rows = jnp.where(pair_ids == 0, trunk[0], trunk[1])
    for index, rows in enumerate((rows_ref[0], rows_ref[1], trunk_rows)):
        high = rows.astype(jnp.bfloat16).astype(jnp.float32)
        middle = (rows - high).astype(jnp.bfloat16).astype(jnp.float32)
        meta_ref[2 * index : 2 * index + 2, 0:n] = high
        meta_ref[2 * index : 2 * index + 2, n : 2 * n] = middle
        meta_ref[8 + 2 * index : 10 + 2 * index, 0:n] = rows - high - middle
    meta_ref[6:8, 0:n] = jnp.broadcast_to(owners[...].astype(jnp.float32), (2, n))
    meta_ref[6:8, n : 2 * n] = jnp.zeros((2, n), jnp.float32)
    meta_ref[14:16, 0:n] = jnp.zeros((2, n), jnp.float32)
    meta_ref[8:16, n : 2 * n] = jnp.zeros((8, n), jnp.float32)
    meta = meta_ref[...].astype(jnp.bfloat16)
    copies[0].wait()
    loadings = loads[...]
    for to in range(feeders):
        out_ref[to, 0:n, :] = loadings
        out_ref[to, n : n + EXTRA, :] = meta


def section_matrices(metas, n):
    row_ids = lax.broadcasted_iota(jnp.int32, (n, n), 0).astype(jnp.float32)
    lane_ids = lax.broadcasted_iota(jnp.int32, (n, n), 1).astype(jnp.float32)
    identity = (row_ids == lane_ids).astype(jnp.bfloat16)
    pad_ids = lax.broadcasted_iota(jnp.int32, (EXTRA, 2 * n), 0)
    highs = [meta[0:8, 0:n] for meta in metas]
    middles = [meta[0:8, n : 2 * n] for meta in metas]
    rows = [high + middle + meta[8:16, 0:n] for high, middle, meta in zip(highs, middles, metas)]
    powers = [(jnp.broadcast_to(high[6:7], (n, n)) == row_ids).astype(jnp.bfloat16) for high in highs]
    powers = [product_nt(identity, power).astype(jnp.bfloat16) for power in powers]
    paths = [identity + power for power in powers]
    powers = [product(power, power).astype(jnp.bfloat16) for power in powers]
    reach = 2
    while reach < n:
        if 2 * reach < n:
            both = [product(x, jnp.concatenate([x, p], axis=1)) for x, p in zip(powers, paths)]
            paths = [p + b[:, n:].astype(jnp.bfloat16) for p, b in zip(paths, both)]
            powers = [b[:, :n].astype(jnp.bfloat16) for b in both]
        else:
            paths = [p + product(x, p).astype(jnp.bfloat16) for x, p in zip(powers, paths)]
        reach *= 2
    shared = []
    for path, high, middle in zip(paths, highs, middles):
        wide_path = path.astype(jnp.float32)

        def scaled(index):
            return jnp.concatenate([wide_path * high[index : index + 1], wide_path * middle[index : index + 1]], axis=1)

        left = jnp.concatenate([scaled(2), scaled(3)], axis=0).astype(jnp.bfloat16)
        shared.append(product_nt(left, jnp.concatenate([path, path], axis=1)))
    out = []
    for both, row in zip(shared, rows):
        resist, react = both[:n], both[n:]
        base_active, base_reactive = row[0:1], row[1:2]
        real_high, real_low = split(resist * base_active + react * base_reactive)
        imag_high, imag_low = split(react * base_active - resist * base_reactive)
        row_real = jnp.concatenate([base_active, base_reactive], axis=1)
        row_imag = jnp.concatenate([-base_reactive, base_active], axis=1)
        sums_high, sums_low = split(jnp.where(pad_ids == 0, row_real, jnp.where(pad_ids == 1, row_imag, 0.0)))

        def whole(real_part, imag_part, sums_part):
            top = jnp.concatenate([real_part, -imag_part], axis=1)
            bottom = jnp.concatenate([imag_part, real_part], axis=1)
            return jnp.concatenate([top, bottom, sums_part], axis=0)

        out.append(
            jnp.concatenate(
                [whole(real_high, imag_high, sums_high), whole(real_low, imag_low, sums_low)], axis=0
            )
        )
    return out


def swing_of(loadings, factors):
    level = product_nt(loadings, factors).astype(jnp.bfloat16).astype(jnp.float32)
    return 1.0 + 0.5 * jnp.tanh(level)


def apply(matrix, high, low):
    half = matrix.shape[0] // 2
    first = product(matrix, high)
    return first[:half] + first[half:] + product(matrix[:half], low)


def scaled_volts(swing, real, imag):
    inverse = swing / (real * real + imag * imag)
    return jnp.concatenate([real * inverse, imag * inverse], axis=0)


def heads_kernel(feeders, pieces, place_ref, every_ref, *refs):
    piece_refs = refs[:pieces]
    head_ref, own_ref, factors_ref, matrix_ref, swing_ref, drop_ref, inject_ref, sem = refs[pieces:]
    width = factors_ref.shape[0]
    n = swing_ref.shape[1]
    span = 2 * n
    piece, offset = place_ref[0], place_ref[1]
    for index, piece_ref in enumerate(piece_refs):
        @pl.when(piece == index)
        def _(piece_ref=piece_ref):
            rows = piece_ref.at[pl.ds(pl.multiple_of(offset, width), width), :]
            copy = pltpu.make_async_copy(rows, factors_ref, sem)
            copy.start()
            copy.wait()
    group = min(feeders, 8)

    def sections(body):
        if group == feeders:
            body(list(range(feeders)))
        else:
            @pl.loop(0, feeders // group)
            def _(outer):
                body([outer * group + inner for inner in range(group)])

    def keep(g, out):
        drop_ref[g] = out[:span]
        inject_ref[g] = out[span:]

    def first(gs):
        for g, matrix in zip(gs, section_matrices([every_ref[g, n : n + EXTRA, :].astype(jnp.float32) for g in gs], n)):
            matrix_ref[g] = matrix
        factors = factors_ref[...]
        for g in gs:
            swing = swing_of(every_ref[g, 0:n, :], factors)
            swing_ref[g] = swing
            high, low = split(swing)
            keep(g, apply(matrix_ref[g][:, :n], high, low))

    sections(first)

    def trunk_row(g, index):
        parts = every_ref[g, n : n + EXTRA, :].astype(jnp.float32)
        row = parts[index : index + 1, 0:n] + parts[index : index + 1, n : 2 * n] + parts[index + 8 : index + 9, 0:n]
        return wide(row, width)

    trunk = [(trunk_row(g, 4), trunk_row(g, 5)) for g in range(feeders)]

    def heads(sweep):
        flows = [None] * feeders
        real = jnp.zeros((1, width), jnp.float32)
        imag = real
        for g in reversed(range(feeders)):
            real = real + inject_ref[g, 0:1, :]
            imag = imag + inject_ref[g, 1:2, :]
            flows[g] = (real, imag)
        head_real = jnp.ones((1, width), jnp.float32)
        head_imag = jnp.zeros((1, width), jnp.float32)
        for g in range(feeders):
            r, x = trunk[g]
            real, imag = flows[g]
            head_real = head_real - (r * real - x * imag)
            head_imag = head_imag - (r * imag + x * real)
            head_ref[g, 2 * sweep : 2 * sweep + 1, :] = head_real
            head_ref[g, 2 * sweep + 1 : 2 * sweep + 2, :] = head_imag

    heads(0)
    for sweep in range(1, SWEEPS):
        def again(gs, sweep=sweep):
            for g in gs:
                real = head_ref[g, 2 * sweep - 2 : 2 * sweep - 1, :] - drop_ref[g, 0:n, :]
                imag = head_ref[g, 2 * sweep - 1 : 2 * sweep, :] - drop_ref[g, n:span, :]
                high, low = split(scaled_volts(swing_ref[g], real, imag))
                if sweep == SWEEPS - 1:
                    half = span + EXTRA
                    row_high = matrix_ref[g, span:half, :]
                    row_low = matrix_ref[g, half + span :, :]
                    inject_ref[g] = product(row_high, high) + product(row_low, high) + product(row_high, low)
                else:
                    keep(g, apply(matrix_ref[g], high, low))

        sections(again)
        heads(sweep)
    for g in range(feeders):
        head_ref[g, 2 * SWEEPS :, :] = jnp.zeros((head_ref.shape[1] - 2 * SWEEPS, width), jnp.float32)
    own_ref[...] = matrix_ref[place_ref[2]]


def drop_rows(matrix_ref, n):
    half = matrix_ref.shape[0] // 2
    return jnp.concatenate([matrix_ref[0 : 2 * n, :], matrix_ref[half : half + 2 * n, :]], axis=0)


def first_kernel(pieces, node_ref, matrix_ref, loadings_ref, *refs):
    piece_refs, (swing_ref, drop_ref, loads, factors_ref, sems) = refs[:pieces], refs[pieces:]
    n = loadings_ref.shape[0]
    width = swing_ref.shape[2]
    chunks = piece_refs[0].shape[0] // width
    copies = [
        pltpu.make_async_copy(loadings_ref, loads, sems.at[0]),
        pltpu.make_async_copy(piece_refs[0], factors_ref, sems.at[1]),
    ]
    for copy in copies:
        copy.start()
    matrix = drop_rows(matrix_ref, n)[:, 0:n]
    copies[0].wait()
    loadings = loads[...]
    for index in reversed(range(pieces)):
        piece_ref = piece_refs[index]
        if index == 0:
            copies[1].wait()
            piece_ref = factors_ref
        for part in range(chunks):
            chunk = jnp.bitwise_xor(node_ref[0], index) * chunks + part
            swing = swing_of(loadings, piece_ref[part * width : (part + 1) * width, :])
            swing_ref[chunk] = swing
            high, low = split(swing)
            drop_ref[chunk] = apply(matrix, high, low)


def volts_kernel(matrix_ref, swing_ref, drop_ref, head_ref, real_ref, imag_ref, out_ref, sems):
    n = swing_ref.shape[1]
    chunks, width = swing_ref.shape[0], swing_ref.shape[2]
    matrix = drop_rows(matrix_ref, n)
    drops = [None] * chunks
    copies = []
    for sweep in range(SWEEPS):
        for chunk in range(chunks):
            drop = drop_ref[chunk] if sweep == 0 else drops[chunk]
            real = head_ref[chunk, 2 * sweep : 2 * sweep + 1, :] - drop[:n]
            imag = head_ref[chunk, 2 * sweep + 1 : 2 * sweep + 2, :] - drop[n:]
            if sweep < SWEEPS - 1:
                high, low = split(scaled_volts(swing_ref[chunk], real, imag))
                drops[chunk] = apply(matrix, high, low)
            else:
                rows = slice(chunk * width, (chunk + 1) * width)
                for index, (part, to_ref) in enumerate(((real, real_ref), (imag, imag_ref))):
                    out_ref[index, rows, :] = part.T
                    copy = pltpu.make_async_copy(out_ref.at[index, rows, :], to_ref.at[rows, :], sems.at[index, chunk])
                    copy.start()
                    copies.append(copy)
    for copy in copies:
        copy.wait()


def in_hbm(*arrays):
    return [pltpu.with_memory_space_constraint(array, pltpu.HBM) for array in arrays]


def limit(nbytes):
    return pltpu.CompilerParams(vmem_limit_bytes=min(60 << 20, int(nbytes) + (16 << 20)))


def local(feeders, nodes, factors, loadings, parents, load_base, lateral_z, trunk_z):
    node = lax.axis_index("node").astype(jnp.int32)
    feeder = lax.axis_index("feeder").astype(jnp.int32)
    rows, rank = factors.shape
    scen = rows * nodes
    n = loadings.shape[0]
    width = max(scen // feeders, LANES)
    share = feeders * width // scen
    f32, bf16 = jnp.float32, jnp.bfloat16
    matrix_rows = 2 * (2 * n + EXTRA)

    packed = pl.pallas_call(
        functools.partial(pack_kernel, feeders),
        out_shape=jax.ShapeDtypeStruct((feeders, n + EXTRA, rank), bf16),
        in_specs=[HBM] * 5,
        out_specs=VMEM,
        scratch_shapes=[
            pltpu.SMEM((2,), f32),
            pltpu.VMEM((n, rank), bf16),
            pltpu.VMEM((1, n), jnp.int32),
            pltpu.VMEM((2, 2, n), f32),
            pltpu.VMEM((EXTRA, rank), f32),
            pltpu.SemaphoreType.DMA((5,)),
        ],
        compiler_params=limit(feeders * (n + EXTRA) * rank * 2),
        name="pack",
    )(*in_hbm(trunk_z.reshape(2), loadings, parents.reshape(1, n), load_base, lateral_z))
    every = lax.all_to_all(packed, "feeder", 0, 0, tiled=True)

    held = {0: factors}
    step = nodes // 2
    while step >= 1:
        pairs = [(i, i ^ step) for i in range(nodes)]
        for offset in list(held):
            held[offset ^ step] = lax.ppermute(held[offset], "node", pairs)
        step //= 2
    pieces = [held[offset] for offset in range(nodes)]

    start = (feeder // share) * width
    place = jnp.stack([(start // rows) ^ node, start % rows, feeder])
    heads, matrix = pl.pallas_call(
        functools.partial(heads_kernel, feeders, nodes),
        out_shape=(
            jax.ShapeDtypeStruct((feeders, 8, width), f32),
            jax.ShapeDtypeStruct((matrix_rows, 2 * n), bf16),
        ),
        in_specs=[SMEM, VMEM, HBM] + [VMEM] * (nodes - 1),
        out_specs=(VMEM, VMEM),
        scratch_shapes=[
            pltpu.VMEM((width, rank), bf16),
            pltpu.VMEM((feeders, matrix_rows, 2 * n), bf16),
            pltpu.VMEM((feeders, n, width), f32),
            pltpu.VMEM((feeders, 2 * n, width), f32),
            pltpu.VMEM((feeders, EXTRA, width), f32),
            pltpu.SemaphoreType.DMA,
        ],
        compiler_params=limit(feeders * (matrix_rows * 4 * n + 3 * n * width * 4 + EXTRA * width * 4 + (n + EXTRA) * rank * 2)),
        name="heads",
    )(place, every, *in_hbm(pieces[0]), *pieces[1:])
    given = lax.all_to_all(heads, "feeder", 0, 0, tiled=True)
    given = given[::share]

    chunks = scen // width
    swing, drop = pl.pallas_call(
        functools.partial(first_kernel, nodes),
        out_shape=(
            jax.ShapeDtypeStruct((chunks, n, width), f32),
            jax.ShapeDtypeStruct((chunks, 2 * n, width), f32),
        ),
        in_specs=[SMEM, VMEM, HBM, HBM] + [VMEM] * (nodes - 1),
        out_specs=(VMEM, VMEM),
        scratch_shapes=[
            pltpu.VMEM((n, rank), bf16),
            pltpu.VMEM((rows, rank), bf16),
            pltpu.SemaphoreType.DMA((2,)),
        ],
        compiler_params=limit(3 * n * scen * 4 + scen * rank * 2),
        cost_estimate=pl.CostEstimate(flops=2 * scen * n * rank * 4, bytes_accessed=3 * n * scen * 4, transcendentals=scen * n),
        name="first",
    )(node.reshape(1), matrix, *in_hbm(loadings, pieces[0]), *pieces[1:])
    return pl.pallas_call(
        volts_kernel,
        out_shape=(
            jax.ShapeDtypeStruct((scen, n), f32),
            jax.ShapeDtypeStruct((scen, n), f32),
        ),
        in_specs=[VMEM] * 4,
        out_specs=(HBM, HBM),
        scratch_shapes=[pltpu.VMEM((2, scen, n), f32), pltpu.SemaphoreType.DMA((2, chunks))],
        compiler_params=limit(5 * n * scen * 4),
        name="volts",
    )(matrix, swing, drop, given)


def solution(mesh):
    feeders = mesh.shape["feeder"]
    nodes = mesh.shape["node"]
    return jax.shard_map(
        functools.partial(local, feeders, nodes),
        mesh=mesh,
        in_specs=(
            P("node", None),
            P(("feeder", "node"), None),
            P(("feeder", "node")),
            P(None, ("feeder", "node")),
            P(None, ("feeder", "node")),
            P(None, "feeder", "node"),
        ),
        out_specs=(P(None, ("feeder", "node")), P(None, ("feeder", "node"))),
        check_vma=False,
    )
```

```python
import functools

import jax
import jax.numpy as jnp
from jax import lax
from jax.experimental import pallas as pl
from jax.experimental.pallas import tpu as pltpu
from jax.sharding import PartitionSpec as P

SWEEPS = 3
EXTRA = 16
LANES = 128

VMEM = pl.BlockSpec(memory_space=pltpu.VMEM)
SMEM = pl.BlockSpec(memory_space=pltpu.SMEM)
HBM = pl.BlockSpec(memory_space=pltpu.HBM)
ANY = pl.BlockSpec(memory_space=pl.ANY)


def split(x):
    high = x.astype(jnp.bfloat16)
    low = (x - high.astype(jnp.float32)).astype(jnp.bfloat16)
    return high, low


def product(left, right):
    return jnp.dot(left, right, preferred_element_type=jnp.float32)


def product_nt(left, right):
    return lax.dot_general(left, right, (((1,), (1,)), ((), ())), preferred_element_type=jnp.float32)


def wide(row, width):
    n = row.shape[1]
    if width <= n:
        return row[:, :width]
    return jnp.concatenate([row] * (width // n), axis=1)


def pack_kernel(
    trunk_ref, loadings_ref, parents_ref, base_ref, z_ref, out_ref, trunk, loads, owners, rows_ref, meta_ref, sems
):
    n = loadings_ref.shape[0]
    copies = [
        pltpu.make_async_copy(loadings_ref, loads, sems.at[0]),
        pltpu.make_async_copy(parents_ref, owners, sems.at[1]),
        pltpu.make_async_copy(base_ref, rows_ref.at[0], sems.at[2]),
        pltpu.make_async_copy(z_ref, rows_ref.at[1], sems.at[3]),
        pltpu.make_async_copy(trunk_ref, trunk, sems.at[4]),
    ]
    for copy in copies:
        copy.start()
    for copy in copies[1:]:
        copy.wait()
    pair_ids = lax.broadcasted_iota(jnp.int32, (2, n), 0)
    trunk_rows = jnp.where(pair_ids == 0, trunk[0], trunk[1])
    for index, rows in enumerate((rows_ref[0], rows_ref[1], trunk_rows)):
        high = rows.astype(jnp.bfloat16).astype(jnp.float32)
        middle = (rows - high).astype(jnp.bfloat16).astype(jnp.float32)
        meta_ref[2 * index : 2 * index + 2, 0:n] = high
        meta_ref[2 * index : 2 * index + 2, n : 2 * n] = middle
        meta_ref[8 + 2 * index : 10 + 2 * index, 0:n] = rows - high - middle
    meta_ref[6:8, 0:n] = jnp.broadcast_to(owners[...].astype(jnp.float32), (2, n))
    meta_ref[6:8, n : 2 * n] = jnp.zeros((2, n), jnp.float32)
    meta_ref[14:16, 0:n] = jnp.zeros((2, n), jnp.float32)
    meta_ref[8:16, n : 2 * n] = jnp.zeros((8, n), jnp.float32)
    meta = meta_ref[...].astype(jnp.bfloat16)
    copies[0].wait()
    out_ref[0:n, :] = loads[...]
    out_ref[n : n + EXTRA, :] = meta


def constants(section_ref, n):
    meta = section_ref[n : n + EXTRA, :].astype(jnp.float32)
    high, middle = meta[0:8, 0:n], meta[0:8, n : 2 * n]
    return high, middle, high + middle + meta[8:16, 0:n]


def section_matrices(sections, n):
    row_ids = lax.broadcasted_iota(jnp.int32, (n, n), 0).astype(jnp.float32)
    lane_ids = lax.broadcasted_iota(jnp.int32, (n, n), 1).astype(jnp.float32)
    identity = (row_ids == lane_ids).astype(jnp.bfloat16)
    pad_ids = lax.broadcasted_iota(jnp.int32, (EXTRA, 2 * n), 0)
    highs, middles, rows = zip(*(constants(section, n) for section in sections))
    powers = [(jnp.broadcast_to(row.T[:, 6:7], (n, n)) == lane_ids).astype(jnp.bfloat16) for row in rows]
    paths = [identity + power for power in powers]
    powers = [product(power, power).astype(jnp.bfloat16) for power in powers]
    reach = 2
    while reach < n:
        if 2 * reach < n:
            both = [product(x, jnp.concatenate([x, p], axis=1)) for x, p in zip(powers, paths)]
            paths = [p + b[:, n:].astype(jnp.bfloat16) for p, b in zip(paths, both)]
            powers = [b[:, :n].astype(jnp.bfloat16) for b in both]
        else:
            paths = [p + product(x, p).astype(jnp.bfloat16) for x, p in zip(powers, paths)]
        reach *= 2
    shared = []
    for path, high, middle in zip(paths, highs, middles):
        wide_path = path.astype(jnp.float32)

        def scaled(index):
            return jnp.concatenate([wide_path * high[index : index + 1], wide_path * middle[index : index + 1]], axis=1)

        left = jnp.concatenate([scaled(2), scaled(3)], axis=0).astype(jnp.bfloat16)
        shared.append(product_nt(left, jnp.concatenate([path, path], axis=1)))
    out = []
    for both, row in zip(shared, rows):
        resist, react = both[:n], both[n:]
        base_active, base_reactive = row[0:1], row[1:2]
        real_high, real_low = split(resist * base_active + react * base_reactive)
        imag_high, imag_low = split(react * base_active - resist * base_reactive)
        row_real = jnp.concatenate([base_active, base_reactive], axis=1)
        row_imag = jnp.concatenate([-base_reactive, base_active], axis=1)
        sums_high, sums_low = split(jnp.where(pad_ids == 0, row_real, jnp.where(pad_ids == 1, row_imag, 0.0)))

        def whole(real_part, imag_part, sums_part):
            top = jnp.concatenate([real_part, -imag_part], axis=1)
            bottom = jnp.concatenate([imag_part, real_part], axis=1)
            return jnp.concatenate([top, bottom, sums_part], axis=0)

        out.append(
            jnp.concatenate(
                [whole(real_high, imag_high, sums_high), whole(real_low, imag_low, sums_low)], axis=0
            )
        )
    return out


def swing_of(loadings, factors):
    level = product_nt(loadings, factors).astype(jnp.bfloat16).astype(jnp.float32)
    return 1.0 + 0.5 * jnp.tanh(level)


def apply(matrix, high, low):
    half = matrix.shape[0] // 2
    first = product(matrix, high)
    return first[:half] + first[half:] + product(matrix[:half], low)


def apply_real(matrix, real):
    half, n = matrix.shape[0] // 2, matrix.shape[1] // 2
    high_part, low_part = matrix[:half, :n], matrix[half:, :n]
    left = jnp.concatenate(
        [
            jnp.concatenate([high_part, high_part], axis=1),
            jnp.concatenate([low_part, jnp.zeros_like(low_part)], axis=1),
        ],
        axis=0,
    )
    out = product(left, jnp.concatenate(split(real), axis=0))
    return out[:half] + out[half:]


def inverse_of(swing, real, imag):
    return swing / (real * real + imag * imag)


def scaled_volts(swing, real, imag):
    inverse = inverse_of(swing, real, imag)
    return jnp.concatenate([real * inverse, imag * inverse], axis=0)


def first_sweep(sections, factors, matrix_ref, swing_ref, drop_ref, inject_ref):
    n = swing_ref.shape[1]
    for start in range(0, len(sections), 8):
        group = sections[start : start + 8]
        for slot, matrix in enumerate(section_matrices(group, n), start):
            matrix_ref[slot] = matrix
        for slot, section in enumerate(group, start):
            swing = swing_of(section[0:n, :], factors)
            swing_ref[slot] = swing
            out = apply_real(matrix_ref[slot], swing)
            drop_ref[slot] = out[: 2 * n]
            inject_ref[slot] = out[2 * n :]


def early_kernel(pieces, place_ref, *refs):
    piece_refs, sections = refs[:pieces], refs[pieces:-9]
    factors_ref, own_ref, kept_ref, matrix_ref, swing_ref, drop_ref, inject_ref, sem, keep_sems = refs[-9:]
    width = factors_ref.shape[0]
    piece, offset = place_ref[0], place_ref[1]
    keeps = [
        pltpu.make_async_copy(piece_ref, kept_ref.at[index], keep_sems.at[index])
        for index, piece_ref in enumerate(piece_refs[1:])
    ]
    for copy in keeps:
        copy.start()
    for index, piece_ref in enumerate(piece_refs):
        @pl.when(piece == index)
        def _(piece_ref=piece_ref):
            rows = piece_ref.at[pl.ds(pl.multiple_of(offset, width), width), :]
            copy = pltpu.make_async_copy(rows, factors_ref, sem)
            copy.start()
            copy.wait()
    first_sweep(sections, factors_ref[...], matrix_ref, swing_ref, drop_ref, inject_ref)
    own_ref[...] = matrix_ref[0]
    for copy in keeps:
        copy.wait()


def heads_kernel(slots, early, place_ref, factors_ref, *refs):
    feeders = len(slots)
    sections = refs[:feeders]
    early_refs = refs[feeders : feeders + 4]
    head_ref, matrix_ref, swing_ref, drop_ref, inject_ref, again_ref, flow_ref, trunk_ref = refs[feeders + 4 :]
    width = factors_ref.shape[0]
    n = swing_ref.shape[1]
    first_sweep(sections[early:], factors_ref[...], matrix_ref, swing_ref, drop_ref, inject_ref)
    late_refs = (matrix_ref, swing_ref, drop_ref, inject_ref)
    place = [jnp.bitwise_xor(place_ref[2], slot) for slot in slots]

    def of(index, which):
        return early_refs[which].at[index] if index < early else late_refs[which].at[index - early]

    for index in range(feeders):
        row = constants(sections[index], n)[2]
        trunk_ref[place[index], 0:2, :] = wide(row[4:6], width)
        flow_ref[place[index]] = of(index, 3)[0:8, :]

    def heads(sweep):
        flows = [None] * feeders
        real = jnp.zeros((1, width), jnp.float32)
        imag = real
        for g in reversed(range(feeders)):
            real = real + flow_ref[g, 0:1, :]
            imag = imag + flow_ref[g, 1:2, :]
            flows[g] = (real, imag)
        head_real = jnp.ones((1, width), jnp.float32)
        head_imag = jnp.zeros((1, width), jnp.float32)
        for g in range(feeders):
            r, x = trunk_ref[g, 0:1, :], trunk_ref[g, 1:2, :]
            real, imag = flows[g]
            head_real = head_real - (r * real - x * imag)
            head_imag = head_imag - (r * imag + x * real)
            head_ref[g, 2 * sweep : 2 * sweep + 1, :] = head_real
            head_ref[g, 2 * sweep + 1 : 2 * sweep + 2, :] = head_imag

    heads(0)
    for sweep in range(1, SWEEPS):
        for index in range(feeders):
            drop = of(index, 2) if sweep == 1 else again_ref.at[index]
            real = head_ref[place[index], 2 * sweep - 2 : 2 * sweep - 1, :] - drop[0:n, :]
            imag = head_ref[place[index], 2 * sweep - 1 : 2 * sweep, :] - drop[n : 2 * n, :]
            swing = of(index, 1)[...]
            if sweep < SWEEPS - 1:
                out = apply(of(index, 0)[...], *split(scaled_volts(swing, real, imag)))
                again_ref[index] = out[: 2 * n]
                flow_ref[place[index]] = out[2 * n : 2 * n + 8]
            else:
                base = constants(sections[index], n)[2].T
                active, reactive = base[:, 0:1], base[:, 1:2]
                inverse = inverse_of(swing, real, imag)
                flow_ref[place[index], 0:1, :] = jnp.sum(inverse * (active * real + reactive * imag), axis=0, keepdims=True)
                flow_ref[place[index], 1:2, :] = jnp.sum(inverse * (active * imag - reactive * real), axis=0, keepdims=True)
        heads(sweep)
    for g in range(feeders):
        head_ref[g, 2 * SWEEPS :, :] = jnp.zeros((head_ref.shape[1] - 2 * SWEEPS, width), jnp.float32)


def drop_rows(matrix_ref, n):
    half = matrix_ref.shape[0] // 2
    return jnp.concatenate([matrix_ref[0 : 2 * n, :], matrix_ref[half : half + 2 * n, :]], axis=0)


def first_kernel(
    node_ref, matrix_ref, loadings_ref, rows_ref, kept_ref, swing_ref, drop_ref, loads, factors_ref, sems
):
    n = loadings_ref.shape[0]
    width = swing_ref.shape[2]
    pieces = 1 + kept_ref.shape[0]
    chunks = rows_ref.shape[0] // width
    copies = [pltpu.make_async_copy(loadings_ref, loads, sems.at[pieces])]
    for index in range(pieces):
        piece_ref = kept_ref.at[index - 1] if index else rows_ref
        copies.append(pltpu.make_async_copy(piece_ref, factors_ref.at[index], sems.at[index]))
    for copy in copies:
        copy.start()
    matrix = drop_rows(matrix_ref, n)
    copies[0].wait()
    loadings = loads[...]
    for index in range(pieces):
        copies[1 + index].wait()
        for part in range(chunks):
            chunk = jnp.bitwise_xor(node_ref[0], index) * chunks + part
            swing = swing_of(loadings, factors_ref[index, part * width : (part + 1) * width, :])
            swing_ref[chunk] = swing
            drop_ref[chunk] = apply_real(matrix, swing)


def volts_kernel(matrix_ref, swing_ref, drop_ref, head_ref, real_ref, imag_ref, out_ref, sems):
    n = swing_ref.shape[1]
    chunks, width = swing_ref.shape[0], swing_ref.shape[2]
    matrix = drop_rows(matrix_ref, n)
    drops = [None] * chunks
    copies = []
    for sweep in range(SWEEPS):
        for chunk in range(chunks):
            drop = drop_ref[chunk] if sweep == 0 else drops[chunk]
            real = head_ref[chunk, 2 * sweep : 2 * sweep + 1, :] - drop[:n]
            imag = head_ref[chunk, 2 * sweep + 1 : 2 * sweep + 2, :] - drop[n:]
            if sweep < SWEEPS - 1:
                high, low = split(scaled_volts(swing_ref[chunk], real, imag))
                drops[chunk] = apply(matrix, high, low)
            else:
                rows = slice(chunk * width, (chunk + 1) * width)
                for index, (part, to_ref) in enumerate(((real, real_ref), (imag, imag_ref))):
                    out_ref[index, rows, :] = part.T
                    copy = pltpu.make_async_copy(out_ref.at[index, rows, :], to_ref.at[rows, :], sems.at[index, chunk])
                    copy.start()
                    copies.append(copy)
    for copy in copies:
        copy.wait()


def in_hbm(*arrays):
    return [pltpu.with_memory_space_constraint(array, pltpu.HBM) for array in arrays]


def limit(nbytes):
    return pltpu.CompilerParams(vmem_limit_bytes=min(60 << 20, int(nbytes) + (16 << 20)))


def local(feeders, nodes, factors, loadings, parents, load_base, lateral_z, trunk_z):
    node = lax.axis_index("node").astype(jnp.int32)
    feeder = lax.axis_index("feeder").astype(jnp.int32)
    rows, rank = factors.shape
    scen = rows * nodes
    n = loadings.shape[0]
    width = max(scen // feeders, LANES)
    share = feeders * width // scen
    f32, bf16 = jnp.float32, jnp.bfloat16
    matrix_rows = 2 * (2 * n + EXTRA)

    held = {0: factors}
    step = nodes // 2
    while step >= 1:
        pairs = [(i, i ^ step) for i in range(nodes)]
        for offset in list(held):
            held[offset ^ step] = lax.ppermute(held[offset], "node", pairs)
        step //= 2
    pieces = [held[offset] for offset in range(nodes)]

    packed = pl.pallas_call(
        pack_kernel,
        out_shape=jax.ShapeDtypeStruct((n + EXTRA, rank), bf16),
        in_specs=[HBM] * 5,
        out_specs=VMEM,
        scratch_shapes=[
            pltpu.SMEM((2,), f32),
            pltpu.VMEM((n, rank), bf16),
            pltpu.VMEM((1, n), jnp.int32),
            pltpu.VMEM((2, 2, n), f32),
            pltpu.VMEM((EXTRA, rank), f32),
            pltpu.SemaphoreType.DMA((5,)),
        ],
        compiler_params=limit(2 * (n + EXTRA) * rank * 2),
        name="pack",
    )(*in_hbm(trunk_z.reshape(2), loadings, parents.reshape(1, n), load_base, lateral_z))

    def swap(block, offset):
        return lax.ppermute(block, "feeder", [(i, i ^ offset) for i in range(feeders)])

    every = {0: packed}
    for offset in sorted(range(2, feeders, 2), key=lambda o: -(o & -o)):
        every[offset] = swap(packed, offset)
    every[1] = swap(packed, 1)
    slots = list(every)
    early = len(slots)
    for offset in slots[1:-1]:
        every[offset + 1] = swap(every[offset], 1)
    slots = list(every)

    start = (feeder // share) * width
    place = jnp.stack([(start // rows) ^ node, start % rows, feeder])

    def states(count):
        return [
            ((count, matrix_rows, 2 * n), bf16),
            ((count, n, width), f32),
            ((count, 2 * n, width), f32),
            ((count, EXTRA, width), f32),
        ]

    state_bytes = matrix_rows * 4 * n + (3 * n + EXTRA) * width * 4 + (n + EXTRA) * rank * 2
    block, own, kept, *started = pl.pallas_call(
        functools.partial(early_kernel, nodes),
        out_shape=[
            jax.ShapeDtypeStruct((width, rank), bf16),
            jax.ShapeDtypeStruct((matrix_rows, 2 * n), bf16),
            pltpu.HBM((nodes - 1, rows, rank), bf16),
        ]
        + [jax.ShapeDtypeStruct(*state) for state in states(early)],
        in_specs=[SMEM, HBM] + [ANY] * (nodes - 1) + [VMEM] * early,
        out_specs=[VMEM, VMEM, HBM] + [VMEM] * 4,
        scratch_shapes=[pltpu.SemaphoreType.DMA, pltpu.SemaphoreType.DMA((nodes - 1,))],
        compiler_params=limit(early * state_bytes),
        cost_estimate=pl.CostEstimate(flops=early * (1 << 29), bytes_accessed=early * state_bytes, transcendentals=early * n * width),
        name="early",
    )(place, *in_hbm(pieces[0]), *pieces[1:], *(every[slot] for slot in slots[:early]))
    heads = pl.pallas_call(
        functools.partial(heads_kernel, slots, early),
        out_shape=jax.ShapeDtypeStruct((feeders, 8, width), f32),
        in_specs=[SMEM] + [VMEM] * (1 + feeders + 4),
        out_specs=VMEM,
        scratch_shapes=[pltpu.VMEM(*state) for state in states(max(feeders - early, 1))]
        + [
            pltpu.VMEM((feeders, 2 * n, width), f32),
            pltpu.VMEM((feeders, 8, width), f32),
            pltpu.VMEM((feeders, 8, width), f32),
        ],
        compiler_params=limit((feeders - early) * state_bytes + feeders * (2 * n + 16) * width * 4),
        name="heads",
    )(place, block, *(every[slot] for slot in slots), *started)
    given = lax.all_to_all(heads, "feeder", 0, 0, tiled=True)
    given = given[::share]

    chunks = scen // width
    swing, drop = pl.pallas_call(
        first_kernel,
        out_shape=(
            jax.ShapeDtypeStruct((chunks, n, width), f32),
            jax.ShapeDtypeStruct((chunks, 2 * n, width), f32),
        ),
        in_specs=[SMEM, VMEM, HBM, HBM, HBM],
        out_specs=(VMEM, VMEM),
        scratch_shapes=[
            pltpu.VMEM((n, rank), bf16),
            pltpu.VMEM((nodes, rows, rank), bf16),
            pltpu.SemaphoreType.DMA((nodes + 1,)),
        ],
        compiler_params=limit(3 * n * scen * 4 + scen * rank * 2),
        cost_estimate=pl.CostEstimate(flops=2 * scen * n * rank * 4, bytes_accessed=3 * n * scen * 4, transcendentals=scen * n),
        name="first",
    )(node.reshape(1), own, *in_hbm(loadings, factors, kept))
    return pl.pallas_call(
        volts_kernel,
        out_shape=(
            jax.ShapeDtypeStruct((scen, n), f32),
            jax.ShapeDtypeStruct((scen, n), f32),
        ),
        in_specs=[VMEM] * 4,
        out_specs=(HBM, HBM),
        scratch_shapes=[pltpu.VMEM((2, scen, n), f32), pltpu.SemaphoreType.DMA((2, chunks))],
        compiler_params=limit(5 * n * scen * 4),
        name="volts",
    )(own, swing, drop, given)


def solution(mesh):
    feeders = mesh.shape["feeder"]
    nodes = mesh.shape["node"]
    return jax.shard_map(
        functools.partial(local, feeders, nodes),
        mesh=mesh,
        in_specs=(
            P("node", None),
            P(("feeder", "node"), None),
            P(("feeder", "node")),
            P(None, ("feeder", "node")),
            P(None, ("feeder", "node")),
            P(None, "feeder", "node"),
        ),
        out_specs=(P(None, ("feeder", "node")), P(None, ("feeder", "node"))),
        check_vma=False,
    )
```

```python
import functools

import jax
import jax.numpy as jnp
from jax import lax
from jax.experimental import pallas as pl
from jax.experimental.pallas import tpu as pltpu
from jax.sharding import PartitionSpec as P

SWEEPS = 3
EXTRA = 16
LANES = 128

VMEM = pl.BlockSpec(memory_space=pltpu.VMEM)
SMEM = pl.BlockSpec(memory_space=pltpu.SMEM)
HBM = pl.BlockSpec(memory_space=pltpu.HBM)
ANY = pl.BlockSpec(memory_space=pl.ANY)


def split(x):
    high = x.astype(jnp.bfloat16)
    low = (x - high.astype(jnp.float32)).astype(jnp.bfloat16)
    return high, low


def product(left, right):
    return jnp.dot(left, right, preferred_element_type=jnp.float32)


def product_nt(left, right):
    return lax.dot_general(left, right, (((1,), (1,)), ((), ())), preferred_element_type=jnp.float32)


def wide(row, width):
    n = row.shape[1]
    if width <= n:
        return row[:, :width]
    return jnp.concatenate([row] * (width // n), axis=1)


def pack_kernel(
    trunk_ref, loadings_ref, parents_ref, base_ref, z_ref, out_ref, trunk, loads, owners, rows_ref, meta_ref, sems
):
    n = loadings_ref.shape[0]
    copies = [
        pltpu.make_async_copy(loadings_ref, loads, sems.at[0]),
        pltpu.make_async_copy(parents_ref, owners, sems.at[1]),
        pltpu.make_async_copy(base_ref, rows_ref.at[0], sems.at[2]),
        pltpu.make_async_copy(z_ref, rows_ref.at[1], sems.at[3]),
        pltpu.make_async_copy(trunk_ref, trunk, sems.at[4]),
    ]
    for copy in copies:
        copy.start()
    for copy in copies[1:]:
        copy.wait()
    pair_ids = lax.broadcasted_iota(jnp.int32, (2, n), 0)
    trunk_rows = jnp.where(pair_ids == 0, trunk[0], trunk[1])
    for index, rows in enumerate((rows_ref[0], rows_ref[1], trunk_rows)):
        high = rows.astype(jnp.bfloat16).astype(jnp.float32)
        middle = (rows - high).astype(jnp.bfloat16).astype(jnp.float32)
        meta_ref[2 * index : 2 * index + 2, 0:n] = high
        meta_ref[2 * index : 2 * index + 2, n : 2 * n] = middle
        meta_ref[8 + 2 * index : 10 + 2 * index, 0:n] = rows - high - middle
    meta_ref[6:8, 0:n] = jnp.broadcast_to(owners[...].astype(jnp.float32), (2, n))
    meta_ref[6:8, n : 2 * n] = jnp.zeros((2, n), jnp.float32)
    meta_ref[14:16, 0:n] = jnp.zeros((2, n), jnp.float32)
    meta_ref[8:16, n : 2 * n] = jnp.zeros((8, n), jnp.float32)
    meta = meta_ref[...].astype(jnp.bfloat16)
    copies[0].wait()
    out_ref[0:n, :] = loads[...]
    out_ref[n : n + EXTRA, :] = meta


def constants(section_ref, n):
    meta = section_ref[n : n + EXTRA, :].astype(jnp.float32)
    high, middle = meta[0:8, 0:n], meta[0:8, n : 2 * n]
    return high, middle, high + middle + meta[8:16, 0:n]


def section_matrices(sections, n):
    row_ids = lax.broadcasted_iota(jnp.int32, (n, n), 0).astype(jnp.float32)
    lane_ids = lax.broadcasted_iota(jnp.int32, (n, n), 1).astype(jnp.float32)
    identity = (row_ids == lane_ids).astype(jnp.bfloat16)
    pad_ids = lax.broadcasted_iota(jnp.int32, (EXTRA, 2 * n), 0)
    highs, middles, rows = zip(*(constants(section, n) for section in sections))
    powers = [(jnp.broadcast_to(row.T[:, 6:7], (n, n)) == lane_ids).astype(jnp.bfloat16) for row in rows]
    paths = [identity + power for power in powers]
    powers = [product(power, power).astype(jnp.bfloat16) for power in powers]
    reach = 2
    while reach < n:
        if 2 * reach < n:
            both = [product(x, jnp.concatenate([x, p], axis=1)) for x, p in zip(powers, paths)]
            paths = [p + b[:, n:].astype(jnp.bfloat16) for p, b in zip(paths, both)]
            powers = [b[:, :n].astype(jnp.bfloat16) for b in both]
        else:
            paths = [p + product(x, p).astype(jnp.bfloat16) for x, p in zip(powers, paths)]
        reach *= 2
    shared = []
    for path, high, middle in zip(paths, highs, middles):
        wide_path = path.astype(jnp.float32)

        def scaled(index):
            return jnp.concatenate([wide_path * high[index : index + 1], wide_path * middle[index : index + 1]], axis=1)

        left = jnp.concatenate([scaled(2), scaled(3)], axis=0).astype(jnp.bfloat16)
        shared.append(product_nt(left, jnp.concatenate([path, path], axis=1)))
    out = []
    for both, row in zip(shared, rows):
        resist, react = both[:n], both[n:]
        base_active, base_reactive = row[0:1], row[1:2]
        real_high, real_low = split(resist * base_active + react * base_reactive)
        imag_high, imag_low = split(react * base_active - resist * base_reactive)
        row_real = jnp.concatenate([base_active, base_reactive], axis=1)
        row_imag = jnp.concatenate([-base_reactive, base_active], axis=1)
        sums_high, sums_low = split(jnp.where(pad_ids == 0, row_real, jnp.where(pad_ids == 1, row_imag, 0.0)))

        def whole(real_part, imag_part, sums_part):
            top = jnp.concatenate([real_part, -imag_part], axis=1)
            bottom = jnp.concatenate([imag_part, real_part], axis=1)
            return jnp.concatenate([top, bottom, sums_part], axis=0)

        out.append(
            jnp.concatenate(
                [whole(real_high, imag_high, sums_high), whole(real_low, imag_low, sums_low)], axis=1
            )
        )
    return out


def swing_of(loadings, factors):
    level = product_nt(loadings, factors).astype(jnp.bfloat16).astype(jnp.float32)
    return 1.0 + 0.5 * jnp.tanh(level)


def apply(matrix, u):
    span = matrix.shape[1] // 2
    high, low = split(u)
    left = jnp.concatenate([matrix, matrix[:, :span]], axis=1)
    return product(left, jnp.concatenate([high, high, low], axis=0))


def apply_real(matrix, real):
    n = matrix.shape[1] // 4
    high, low = split(real)
    high_part, low_part = matrix[:, :n], matrix[:, 2 * n : 3 * n]
    left = jnp.concatenate([high_part, low_part, high_part], axis=1)
    return product(left, jnp.concatenate([high, high, low], axis=0))


def inverse_of(swing, real, imag):
    square = real * real + imag * imag
    guess = pl.reciprocal(square, approx=True)
    return swing * (guess * (2.0 - square * guess))


def scaled_volts(swing, real, imag):
    inverse = inverse_of(swing, real, imag)
    return jnp.concatenate([real * inverse, imag * inverse], axis=0)


def first_sweep(sections, factors_of, matrix_ref, swing_ref, drop_ref, inject_ref):
    n = swing_ref.shape[1]
    for start in range(0, len(sections), 8):
        group = sections[start : start + 8]
        for slot, matrix in enumerate(section_matrices(group, n), start):
            matrix_ref[slot] = matrix
        factors = factors_of(start)
        for slot, section in enumerate(group, start):
            swing = swing_of(section[0:n, :], factors)
            swing_ref[slot] = swing
            out = apply_real(matrix_ref[slot], swing)
            drop_ref[slot] = out[: 2 * n]
            inject_ref[slot] = out[2 * n :]


def early_kernel(pieces, place_ref, *refs):
    piece_refs, sections = refs[:pieces], refs[pieces:-9]
    factors_ref, own_ref, kept_ref, matrix_ref, swing_ref, drop_ref, inject_ref, sem, keep_sems = refs[-9:]
    width = factors_ref.shape[0]
    piece, offset = place_ref[0], place_ref[1]
    keeps = [
        pltpu.make_async_copy(piece_ref, kept_ref.at[index], keep_sems.at[index])
        for index, piece_ref in enumerate(piece_refs[1:])
    ]
    for copy in keeps:
        copy.start()
    for index, piece_ref in enumerate(piece_refs):
        @pl.when(piece == index)
        def _(piece_ref=piece_ref):
            rows = piece_ref.at[pl.ds(pl.multiple_of(offset, width), width), :]
            pltpu.make_async_copy(rows, factors_ref, sem).start()

    def factors_of(start):
        if start == 0:
            pltpu.make_async_copy(piece_refs[0].at[0:width, :], factors_ref, sem).wait()
        return factors_ref[...]

    first_sweep(sections, factors_of, matrix_ref, swing_ref, drop_ref, inject_ref)
    own_ref[...] = matrix_ref[0]
    for copy in keeps:
        copy.wait()


def heads_kernel(slots, early, place_ref, factors_ref, *refs):
    feeders = len(slots)
    sections = refs[:feeders]
    early_refs = refs[feeders : feeders + 4]
    head_ref, matrix_ref, swing_ref, drop_ref, inject_ref, again_ref, flow_ref, trunk_ref = refs[feeders + 4 :]
    width = factors_ref.shape[0]
    n = swing_ref.shape[1]
    first_sweep(sections[early:], lambda start: factors_ref[...], matrix_ref, swing_ref, drop_ref, inject_ref)
    late_refs = (matrix_ref, swing_ref, drop_ref, inject_ref)
    place = [jnp.bitwise_xor(place_ref[2], slot) for slot in slots]

    def of(index, which):
        return early_refs[which].at[index] if index < early else late_refs[which].at[index - early]

    for index in range(feeders):
        row = constants(sections[index], n)[2]
        trunk_ref[place[index], 0:2, :] = wide(row[4:6], width)
        flow_ref[place[index]] = of(index, 3)[0:8, :]

    def heads(sweep):
        flows = [None] * feeders
        real = jnp.zeros((1, width), jnp.float32)
        imag = real
        for g in reversed(range(feeders)):
            real = real + flow_ref[g, 0:1, :]
            imag = imag + flow_ref[g, 1:2, :]
            flows[g] = (real, imag)
        head_real = jnp.ones((1, width), jnp.float32)
        head_imag = jnp.zeros((1, width), jnp.float32)
        for g in range(feeders):
            r, x = trunk_ref[g, 0:1, :], trunk_ref[g, 1:2, :]
            real, imag = flows[g]
            head_real = head_real - (r * real - x * imag)
            head_imag = head_imag - (r * imag + x * real)
            head_ref[g, 2 * sweep : 2 * sweep + 1, :] = head_real
            head_ref[g, 2 * sweep + 1 : 2 * sweep + 2, :] = head_imag

    heads(0)
    for sweep in range(1, SWEEPS):
        for index in range(feeders):
            drop = of(index, 2) if sweep == 1 else again_ref.at[index]
            real = head_ref[place[index], 2 * sweep - 2 : 2 * sweep - 1, :] - drop[0:n, :]
            imag = head_ref[place[index], 2 * sweep - 1 : 2 * sweep, :] - drop[n : 2 * n, :]
            swing = of(index, 1)[...]
            if sweep < SWEEPS - 1:
                out = apply(of(index, 0)[...], scaled_volts(swing, real, imag))
                again_ref[index] = out[: 2 * n]
                flow_ref[place[index]] = out[2 * n : 2 * n + 8]
            else:
                base = constants(sections[index], n)[2].T
                active, reactive = base[:, 0:1], base[:, 1:2]
                inverse = inverse_of(swing, real, imag)
                flow_ref[place[index], 0:1, :] = jnp.sum(inverse * (active * real + reactive * imag), axis=0, keepdims=True)
                flow_ref[place[index], 1:2, :] = jnp.sum(inverse * (active * imag - reactive * real), axis=0, keepdims=True)
        heads(sweep)
    for g in range(feeders):
        head_ref[g, 2 * SWEEPS :, :] = jnp.zeros((head_ref.shape[1] - 2 * SWEEPS, width), jnp.float32)


def first_kernel(
    node_ref, matrix_ref, loadings_ref, rows_ref, kept_ref, swing_ref, drop_ref, loads, factors_ref, sems
):
    n = loadings_ref.shape[0]
    width = swing_ref.shape[2]
    pieces = 1 + kept_ref.shape[0]
    chunks = rows_ref.shape[0] // width
    copies = [pltpu.make_async_copy(loadings_ref, loads, sems.at[pieces])]
    for index in range(pieces):
        piece_ref = kept_ref.at[index - 1] if index else rows_ref
        copies.append(pltpu.make_async_copy(piece_ref, factors_ref.at[index], sems.at[index]))
    for copy in copies:
        copy.start()
    matrix = matrix_ref[0 : 2 * n, :]
    copies[0].wait()
    loadings = loads[...]
    for index in range(pieces):
        copies[1 + index].wait()
        for part in range(chunks):
            chunk = jnp.bitwise_xor(node_ref[0], index) * chunks + part
            swing = swing_of(loadings, factors_ref[index, part * width : (part + 1) * width, :])
            swing_ref[chunk] = swing
            drop_ref[chunk] = apply_real(matrix, swing)


def volts_kernel(matrix_ref, swing_ref, drop_ref, head_ref, real_ref, imag_ref, out_ref, sems):
    n = swing_ref.shape[1]
    chunks, width = swing_ref.shape[0], swing_ref.shape[2]
    matrix = matrix_ref[0 : 2 * n, :]
    drops = [None] * chunks
    copies = []
    for sweep in range(SWEEPS):
        for chunk in range(chunks):
            drop = drop_ref[chunk] if sweep == 0 else drops[chunk]
            real = head_ref[chunk, 2 * sweep : 2 * sweep + 1, :] - drop[:n]
            imag = head_ref[chunk, 2 * sweep + 1 : 2 * sweep + 2, :] - drop[n:]
            if sweep < SWEEPS - 1:
                drops[chunk] = apply(matrix, scaled_volts(swing_ref[chunk], real, imag))
            else:
                rows = slice(chunk * width, (chunk + 1) * width)
                for index, (part, to_ref) in enumerate(((real, real_ref), (imag, imag_ref))):
                    out_ref[index, rows, :] = part.T
                    copy = pltpu.make_async_copy(out_ref.at[index, rows, :], to_ref.at[rows, :], sems.at[index, chunk])
                    copy.start()
                    copies.append(copy)
    for copy in copies:
        copy.wait()


def after_kernel(*refs):
    del refs


def after(array, *others):
    return pl.pallas_call(
        after_kernel,
        out_shape=jax.ShapeDtypeStruct(array.shape, array.dtype),
        in_specs=[ANY] * (1 + len(others)),
        out_specs=ANY,
        input_output_aliases={0: 0},
        name="after",
    )(array, *others)


def in_hbm(*arrays):
    return [pltpu.with_memory_space_constraint(array, pltpu.HBM) for array in arrays]


def limit(nbytes):
    return pltpu.CompilerParams(vmem_limit_bytes=min(60 << 20, int(nbytes) + (16 << 20)))


def local(feeders, nodes, factors, loadings, parents, load_base, lateral_z, trunk_z):
    node = lax.axis_index("node").astype(jnp.int32)
    feeder = lax.axis_index("feeder").astype(jnp.int32)
    rows, rank = factors.shape
    scen = rows * nodes
    n = loadings.shape[0]
    width = max(scen // feeders, LANES)
    share = feeders * width // scen
    f32, bf16 = jnp.float32, jnp.bfloat16
    matrix_shape = (2 * n + EXTRA, 4 * n)

    def trade(block, offset):
        return lax.ppermute(block, "node", [(i, i ^ offset) for i in range(nodes)])

    held = {0: factors}
    far = nodes // 2
    if far:
        held[far] = trade(factors, far)

    packed = pl.pallas_call(
        pack_kernel,
        out_shape=jax.ShapeDtypeStruct((n + EXTRA, rank), bf16),
        in_specs=[HBM] * 5,
        out_specs=VMEM,
        scratch_shapes=[
            pltpu.SMEM((2,), f32),
            pltpu.VMEM((n, rank), bf16),
            pltpu.VMEM((1, n), jnp.int32),
            pltpu.VMEM((2, 2, n), f32),
            pltpu.VMEM((EXTRA, rank), f32),
            pltpu.SemaphoreType.DMA((5,)),
        ],
        compiler_params=limit(2 * (n + EXTRA) * rank * 2),
        name="pack",
    )(*in_hbm(trunk_z.reshape(2), loadings, parents.reshape(1, n), load_base, lateral_z))

    def swap(block, offset):
        return lax.ppermute(block, "feeder", [(i, i ^ offset) for i in range(feeders)])

    every = {0: packed}
    for offset in sorted(range(2, feeders, 2), key=lambda o: -(o & -o)):
        every[offset] = swap(packed, offset)
    every[1] = swap(packed, 1)
    slots = list(every)
    early = len(slots)
    for offset in slots[1:-1]:
        every[offset + 1] = swap(every[offset], 1)
    slots = list(every)

    if far:
        held[far] = after(held[far], *(every[slot] for slot in slots[:early]))
    step = far // 2
    while step >= 1:
        for offset in list(held):
            held[offset ^ step] = trade(held[offset], step)
        step //= 2
    pieces = [held[offset] for offset in range(nodes)]

    start = (feeder // share) * width
    place = jnp.stack([(start // rows) ^ node, start % rows, feeder])

    def states(count):
        return [
            ((count, *matrix_shape), bf16),
            ((count, n, width), f32),
            ((count, 2 * n, width), f32),
            ((count, EXTRA, width), f32),
        ]

    state_bytes = (2 * n + EXTRA) * 8 * n + (3 * n + EXTRA) * width * 4 + (n + EXTRA) * rank * 2
    block, own, kept, *started = pl.pallas_call(
        functools.partial(early_kernel, nodes),
        out_shape=[
            jax.ShapeDtypeStruct((width, rank), bf16),
            jax.ShapeDtypeStruct(matrix_shape, bf16),
            pltpu.HBM((nodes - 1, rows, rank), bf16),
        ]
        + [jax.ShapeDtypeStruct(*state) for state in states(early)],
        in_specs=[SMEM, HBM] + [ANY] * (nodes - 1) + [VMEM] * early,
        out_specs=[VMEM, VMEM, HBM] + [VMEM] * 4,
        scratch_shapes=[pltpu.SemaphoreType.DMA, pltpu.SemaphoreType.DMA((nodes - 1,))],
        compiler_params=limit(early * state_bytes),
        cost_estimate=pl.CostEstimate(flops=early * (1 << 29), bytes_accessed=early * state_bytes, transcendentals=early * n * width),
        name="early",
    )(place, *in_hbm(pieces[0]), *pieces[1:], *(every[slot] for slot in slots[:early]))
    heads = pl.pallas_call(
        functools.partial(heads_kernel, slots, early),
        out_shape=jax.ShapeDtypeStruct((feeders, 8, width), f32),
        in_specs=[SMEM] + [VMEM] * (1 + feeders + 4),
        out_specs=VMEM,
        scratch_shapes=[pltpu.VMEM(*state) for state in states(max(feeders - early, 1))]
        + [
            pltpu.VMEM((feeders, 2 * n, width), f32),
            pltpu.VMEM((feeders, 8, width), f32),
            pltpu.VMEM((feeders, 8, width), f32),
        ],
        compiler_params=limit((feeders - early) * state_bytes + feeders * (2 * n + 16) * width * 4),
        name="heads",
    )(place, block, *(every[slot] for slot in slots), *started)
    given = lax.all_to_all(heads, "feeder", 0, 0, tiled=True)
    given = given[::share]

    chunks = scen // width
    swing, drop = pl.pallas_call(
        first_kernel,
        out_shape=(
            jax.ShapeDtypeStruct((chunks, n, width), f32),
            jax.ShapeDtypeStruct((chunks, 2 * n, width), f32),
        ),
        in_specs=[SMEM, VMEM, HBM, HBM, HBM],
        out_specs=(VMEM, VMEM),
        scratch_shapes=[
            pltpu.VMEM((n, rank), bf16),
            pltpu.VMEM((nodes, rows, rank), bf16),
            pltpu.SemaphoreType.DMA((nodes + 1,)),
        ],
        compiler_params=limit(3 * n * scen * 4 + scen * rank * 2),
        cost_estimate=pl.CostEstimate(flops=2 * scen * n * rank * 4, bytes_accessed=3 * n * scen * 4, transcendentals=scen * n),
        name="first",
    )(node.reshape(1), own, *in_hbm(loadings, factors, kept))
    return pl.pallas_call(
        volts_kernel,
        out_shape=(
            jax.ShapeDtypeStruct((scen, n), f32),
            jax.ShapeDtypeStruct((scen, n), f32),
        ),
        in_specs=[VMEM] * 4,
        out_specs=(HBM, HBM),
        scratch_shapes=[pltpu.VMEM((2, scen, n), f32), pltpu.SemaphoreType.DMA((2, chunks))],
        compiler_params=limit(5 * n * scen * 4),
        name="volts",
    )(own, swing, drop, given)


def solution(mesh):
    feeders = mesh.shape["feeder"]
    nodes = mesh.shape["node"]
    return jax.shard_map(
        functools.partial(local, feeders, nodes),
        mesh=mesh,
        in_specs=(
            P("node", None),
            P(("feeder", "node"), None),
            P(("feeder", "node")),
            P(None, ("feeder", "node")),
            P(None, ("feeder", "node")),
            P(None, "feeder", "node"),
        ),
        out_specs=(P(None, ("feeder", "node")), P(None, ("feeder", "node"))),
        check_vma=False,
    )
```

```python
import functools

import jax
import jax.numpy as jnp
from jax import lax
from jax.experimental import pallas as pl
from jax.experimental.pallas import tpu as pltpu
from jax.sharding import PartitionSpec as P

SWEEPS = 3
EXTRA = 16
LANES = 128

VMEM = pl.BlockSpec(memory_space=pltpu.VMEM)
SMEM = pl.BlockSpec(memory_space=pltpu.SMEM)
HBM = pl.BlockSpec(memory_space=pltpu.HBM)
ANY = pl.BlockSpec(memory_space=pl.ANY)


def split(x):
    high = x.astype(jnp.bfloat16)
    low = (x - high.astype(jnp.float32)).astype(jnp.bfloat16)
    return high, low


def product(left, right):
    return jnp.dot(left, right, preferred_element_type=jnp.float32)


def product_nt(left, right):
    return lax.dot_general(left, right, (((1,), (1,)), ((), ())), preferred_element_type=jnp.float32)


def wide(row, width):
    n = row.shape[1]
    if width <= n:
        return row[:, :width]
    return jnp.concatenate([row] * (width // n), axis=1)


def pack_kernel(
    trunk_ref, loadings_ref, parents_ref, base_ref, z_ref, out_ref, trunk, loads, owners, rows_ref, meta_ref, sems
):
    n = loadings_ref.shape[0]
    copies = [
        pltpu.make_async_copy(loadings_ref, loads, sems.at[0]),
        pltpu.make_async_copy(parents_ref, owners, sems.at[1]),
        pltpu.make_async_copy(base_ref, rows_ref.at[0], sems.at[2]),
        pltpu.make_async_copy(z_ref, rows_ref.at[1], sems.at[3]),
        pltpu.make_async_copy(trunk_ref, trunk, sems.at[4]),
    ]
    for copy in copies:
        copy.start()
    for copy in copies[1:]:
        copy.wait()
    pair_ids = lax.broadcasted_iota(jnp.int32, (2, n), 0)
    trunk_rows = jnp.where(pair_ids == 0, trunk[0], trunk[1])
    for index, rows in enumerate((rows_ref[0], rows_ref[1], trunk_rows)):
        high = rows.astype(jnp.bfloat16).astype(jnp.float32)
        middle = (rows - high).astype(jnp.bfloat16).astype(jnp.float32)
        meta_ref[2 * index : 2 * index + 2, 0:n] = high
        meta_ref[2 * index : 2 * index + 2, n : 2 * n] = middle
        meta_ref[8 + 2 * index : 10 + 2 * index, 0:n] = rows - high - middle
    meta_ref[6:8, 0:n] = jnp.broadcast_to(owners[...].astype(jnp.float32), (2, n))
    meta_ref[6:8, n : 2 * n] = jnp.zeros((2, n), jnp.float32)
    meta_ref[14:16, 0:n] = jnp.zeros((2, n), jnp.float32)
    meta_ref[8:16, n : 2 * n] = jnp.zeros((8, n), jnp.float32)
    meta = meta_ref[...].astype(jnp.bfloat16)
    copies[0].wait()
    out_ref[0:n, :] = loads[...]
    out_ref[n : n + EXTRA, :] = meta


def constants(section_ref, n):
    meta = section_ref[n : n + EXTRA, :].astype(jnp.float32)
    high, middle = meta[0:8, 0:n], meta[0:8, n : 2 * n]
    return high, middle, high + middle + meta[8:16, 0:n]


def section_paths(parents, n):
    rows = max(8, len(parents))
    row_ids = lax.broadcasted_iota(jnp.int32, (n, n), 0)
    lane_ids = lax.broadcasted_iota(jnp.int32, (n, n), 1)
    section_ids = lax.broadcasted_iota(jnp.int32, (rows, n), 0)
    stacked = jnp.full((rows, n), -1, jnp.int32)
    for index, row in enumerate(parents):
        stacked = jnp.where(section_ids == index, row.astype(jnp.int32), stacked)
    known = {1: stacked}

    def ancestor(distance):
        if distance not in known:
            step = 1 << (distance.bit_length() - 1)
            if step == distance:
                step //= 2
            far, near = ancestor(step), ancestor(distance - step)
            known[distance] = jnp.where(near < 0, -1, jnp.take_along_axis(far, jnp.maximum(near, 0), axis=1))
        return known[distance]

    digits = []
    unit = 1
    while unit < n:
        digits.append([ancestor(unit * digit) for digit in range(1, 8) if unit * digit < n])
        unit *= 8
    last = [found.astype(jnp.float32).T.astype(jnp.int32) for found in digits.pop()]
    out = []
    for index in range(len(parents)):
        product_t = None
        for digit in digits:
            mask = row_ids == lane_ids
            for found in digit:
                mask = mask | (row_ids == found[index : index + 1, :])
            factor = mask.astype(jnp.bfloat16)
            product_t = factor if product_t is None else product(product_t, factor).astype(jnp.bfloat16)
        mask = row_ids == lane_ids
        for found in last:
            mask = mask | (lane_ids == found[:, index : index + 1])
        out.append((mask.astype(jnp.bfloat16), product_t))
    return [product_nt(left, right).astype(jnp.bfloat16) for left, right in out]


def section_matrices(sections, n):
    pad_ids = lax.broadcasted_iota(jnp.int32, (EXTRA, 2 * n), 0)
    highs, middles, rows = zip(*(constants(section, n) for section in sections))
    paths = section_paths([row[6:7] for row in rows], n)
    shared = []
    for path, high, middle in zip(paths, highs, middles):
        wide_path = path.astype(jnp.float32)

        def scaled(index):
            return jnp.concatenate([wide_path * high[index : index + 1], wide_path * middle[index : index + 1]], axis=1)

        left = jnp.concatenate([scaled(2), scaled(3)], axis=0).astype(jnp.bfloat16)
        shared.append(product_nt(left, jnp.concatenate([path, path], axis=1)))
    out = []
    for both, row in zip(shared, rows):
        resist, react = both[:n], both[n:]
        base_active, base_reactive = row[0:1], row[1:2]
        real_high, real_low = split(resist * base_active + react * base_reactive)
        imag_high, imag_low = split(react * base_active - resist * base_reactive)
        row_real = jnp.concatenate([base_active, base_reactive], axis=1)
        row_imag = jnp.concatenate([-base_reactive, base_active], axis=1)
        sums_high, sums_low = split(jnp.where(pad_ids == 0, row_real, jnp.where(pad_ids == 1, row_imag, 0.0)))

        def whole(real_part, imag_part, sums_part):
            top = jnp.concatenate([real_part, -imag_part], axis=1)
            bottom = jnp.concatenate([imag_part, real_part], axis=1)
            return jnp.concatenate([top, bottom, sums_part], axis=0)

        out.append(
            jnp.concatenate(
                [whole(real_high, imag_high, sums_high), whole(real_low, imag_low, sums_low)], axis=1
            )
        )
    return out


def swing_of(loadings, factors):
    level = product_nt(loadings, factors).astype(jnp.bfloat16).astype(jnp.float32)
    return 1.0 + 0.5 * jnp.tanh(level)


def apply(matrix, u):
    span = matrix.shape[1] // 2
    high, low = split(u)
    left = jnp.concatenate([matrix, matrix[:, :span]], axis=1)
    return product(left, jnp.concatenate([high, high, low], axis=0))


def apply_first(matrix, swing):
    n = matrix.shape[1] // 4
    high = swing.astype(jnp.bfloat16)
    return product(
        jnp.concatenate([matrix[:, :n], matrix[:, 2 * n : 3 * n]], axis=1), jnp.concatenate([high, high], axis=0)
    )


def apply_change(matrix, change):
    return product(matrix[:, : matrix.shape[1] // 2], change.astype(jnp.bfloat16))


def inverse_of(swing, real, imag):
    square = real * real + imag * imag
    guess = pl.reciprocal(square, approx=True)
    return swing * (guess * (2.0 - square * guess))


def scaled_volts(swing, real, imag, change=False):
    inverse = inverse_of(swing, real, imag)
    scaled = real * inverse
    if change:
        scaled = scaled - swing.astype(jnp.bfloat16).astype(jnp.float32)
    return jnp.concatenate([scaled, imag * inverse], axis=0)


def first_sweep(sections, factors_of, matrix_ref, swing_ref, drop_ref, inject_ref):
    n = swing_ref.shape[1]
    for start in range(0, len(sections), 8):
        group = sections[start : start + 8]
        for slot, matrix in enumerate(section_matrices(group, n), start):
            matrix_ref[slot] = matrix
        factors = factors_of(start)
        for slot, section in enumerate(group, start):
            swing = swing_of(section[0:n, :], factors)
            swing_ref[slot] = swing
            out = apply_first(matrix_ref[slot], swing)
            drop_ref[slot] = out[: 2 * n]
            inject_ref[slot] = out[2 * n :]


def early_kernel(pieces, place_ref, *refs):
    piece_refs, sections = refs[:pieces], refs[pieces:-9]
    factors_ref, own_ref, kept_ref, matrix_ref, swing_ref, drop_ref, inject_ref, sem, keep_sems = refs[-9:]
    width = factors_ref.shape[0]
    piece, offset = place_ref[0], place_ref[1]
    keeps = [
        pltpu.make_async_copy(piece_ref, kept_ref.at[index], keep_sems.at[index])
        for index, piece_ref in enumerate(piece_refs[1:])
    ]
    for copy in keeps:
        copy.start()
    for index, piece_ref in enumerate(piece_refs):
        @pl.when(piece == index)
        def _(piece_ref=piece_ref):
            rows = piece_ref.at[pl.ds(pl.multiple_of(offset, width), width), :]
            pltpu.make_async_copy(rows, factors_ref, sem).start()

    def factors_of(start):
        if start == 0:
            pltpu.make_async_copy(piece_refs[0].at[0:width, :], factors_ref, sem).wait()
        return factors_ref[...]

    first_sweep(sections, factors_of, matrix_ref, swing_ref, drop_ref, inject_ref)
    own_ref[...] = matrix_ref[0]
    for copy in keeps:
        copy.wait()


def heads_kernel(slots, early, place_ref, factors_ref, *refs):
    feeders = len(slots)
    sections = refs[:feeders]
    early_refs = refs[feeders : feeders + 4]
    head_ref, matrix_ref, swing_ref, drop_ref, inject_ref, again_ref, flow_ref, trunk_ref = refs[feeders + 4 :]
    width = factors_ref.shape[0]
    n = swing_ref.shape[1]
    first_sweep(sections[early:], lambda start: factors_ref[...], matrix_ref, swing_ref, drop_ref, inject_ref)
    late_refs = (matrix_ref, swing_ref, drop_ref, inject_ref)
    place = [jnp.bitwise_xor(place_ref[2], slot) for slot in slots]

    def of(index, which):
        return early_refs[which].at[index] if index < early else late_refs[which].at[index - early]

    for index in range(feeders):
        row = constants(sections[index], n)[2]
        trunk_ref[place[index], 0:2, :] = wide(row[4:6], width)
        flow_ref[place[index]] = of(index, 3)[0:8, :]

    def heads(sweep):
        flows = [None] * feeders
        real = jnp.zeros((1, width), jnp.float32)
        imag = real
        for g in reversed(range(feeders)):
            real = real + flow_ref[g, 0:1, :]
            imag = imag + flow_ref[g, 1:2, :]
            flows[g] = (real, imag)
        head_real = jnp.ones((1, width), jnp.float32)
        head_imag = jnp.zeros((1, width), jnp.float32)
        for g in range(feeders):
            r, x = trunk_ref[g, 0:1, :], trunk_ref[g, 1:2, :]
            real, imag = flows[g]
            head_real = head_real - (r * real - x * imag)
            head_imag = head_imag - (r * imag + x * real)
            head_ref[g, 2 * sweep : 2 * sweep + 1, :] = head_real
            head_ref[g, 2 * sweep + 1 : 2 * sweep + 2, :] = head_imag

    heads(0)
    for sweep in range(1, SWEEPS):
        for index in range(feeders):
            drop = of(index, 2) if sweep == 1 else again_ref.at[index]
            real = head_ref[place[index], 2 * sweep - 2 : 2 * sweep - 1, :] - drop[0:n, :]
            imag = head_ref[place[index], 2 * sweep - 1 : 2 * sweep, :] - drop[n : 2 * n, :]
            swing = of(index, 1)[...]
            if sweep < SWEEPS - 1:
                out = apply_change(of(index, 0)[...], scaled_volts(swing, real, imag, change=True))
                again_ref[index] = of(index, 2)[...] + out[: 2 * n]
                flow_ref[place[index]] = of(index, 3)[0:8, :] + out[2 * n : 2 * n + 8]
            else:
                base = constants(sections[index], n)[2].T
                active, reactive = base[:, 0:1], base[:, 1:2]
                inverse = inverse_of(swing, real, imag)
                flow_ref[place[index], 0:1, :] = jnp.sum(inverse * (active * real + reactive * imag), axis=0, keepdims=True)
                flow_ref[place[index], 1:2, :] = jnp.sum(inverse * (active * imag - reactive * real), axis=0, keepdims=True)
        heads(sweep)
    for g in range(feeders):
        head_ref[g, 2 * SWEEPS :, :] = jnp.zeros((head_ref.shape[1] - 2 * SWEEPS, width), jnp.float32)


def first_kernel(
    node_ref, matrix_ref, loadings_ref, rows_ref, kept_ref, swing_ref, drop_ref, loads, factors_ref, sems
):
    n = loadings_ref.shape[0]
    width = swing_ref.shape[2]
    pieces = 1 + kept_ref.shape[0]
    chunks = rows_ref.shape[0] // width
    copies = [pltpu.make_async_copy(loadings_ref, loads, sems.at[pieces])]
    for index in range(pieces):
        piece_ref = kept_ref.at[index - 1] if index else rows_ref
        copies.append(pltpu.make_async_copy(piece_ref, factors_ref.at[index], sems.at[index]))
    for copy in copies:
        copy.start()
    matrix = matrix_ref[0 : 2 * n, :]
    copies[0].wait()
    loadings = loads[...]
    for index in range(pieces):
        copies[1 + index].wait()
        for part in range(chunks):
            chunk = jnp.bitwise_xor(node_ref[0], index) * chunks + part
            swing = swing_of(loadings, factors_ref[index, part * width : (part + 1) * width, :])
            swing_ref[chunk] = swing
            drop_ref[chunk] = apply_first(matrix, swing)


def volts_kernel(matrix_ref, swing_ref, drop_ref, head_ref, real_ref, imag_ref, out_ref, sems):
    n = swing_ref.shape[1]
    chunks, width = swing_ref.shape[0], swing_ref.shape[2]
    matrix = matrix_ref[0 : 2 * n, :]
    drops = [None] * chunks
    copies = []
    for sweep in range(SWEEPS):
        for chunk in range(chunks):
            drop = drop_ref[chunk] if sweep == 0 else drops[chunk]
            real = head_ref[chunk, 2 * sweep : 2 * sweep + 1, :] - drop[:n]
            imag = head_ref[chunk, 2 * sweep + 1 : 2 * sweep + 2, :] - drop[n:]
            swing = swing_ref[chunk]
            if sweep < SWEEPS - 2:
                drops[chunk] = drop_ref[chunk] + apply_change(matrix, scaled_volts(swing, real, imag, change=True))
            elif sweep < SWEEPS - 1:
                drops[chunk] = apply(matrix, scaled_volts(swing, real, imag))
            else:
                rows = slice(chunk * width, (chunk + 1) * width)
                for index, (part, to_ref) in enumerate(((real, real_ref), (imag, imag_ref))):
                    out_ref[index, rows, :] = part.T
                    copy = pltpu.make_async_copy(out_ref.at[index, rows, :], to_ref.at[rows, :], sems.at[index, chunk])
                    copy.start()
                    copies.append(copy)
    for copy in copies:
        copy.wait()


def after_kernel(*refs):
    del refs


def after(array, *others):
    return pl.pallas_call(
        after_kernel,
        out_shape=jax.ShapeDtypeStruct(array.shape, array.dtype),
        in_specs=[ANY] * (1 + len(others)),
        out_specs=ANY,
        input_output_aliases={0: 0},
        compiler_params=limit(0),
        name="after",
    )(array, *others)


def in_hbm(*arrays):
    return [pltpu.with_memory_space_constraint(array, pltpu.HBM) for array in arrays]


def limit(nbytes):
    return pltpu.CompilerParams(vmem_limit_bytes=min(60 << 20, int(nbytes) + (16 << 20)))


def local(feeders, nodes, factors, loadings, parents, load_base, lateral_z, trunk_z):
    node = lax.axis_index("node").astype(jnp.int32)
    feeder = lax.axis_index("feeder").astype(jnp.int32)
    rows, rank = factors.shape
    scen = rows * nodes
    n = loadings.shape[0]
    width = max(scen // feeders, LANES)
    share = feeders * width // scen
    f32, bf16 = jnp.float32, jnp.bfloat16
    matrix_shape = (2 * n + EXTRA, 4 * n)

    def trade(block, offset):
        return lax.ppermute(block, "node", [(i, i ^ offset) for i in range(nodes)])

    held = {0: factors}
    far = nodes // 2
    if far:
        held[far] = trade(factors, far)

    packed = pl.pallas_call(
        pack_kernel,
        out_shape=jax.ShapeDtypeStruct((n + EXTRA, rank), bf16),
        in_specs=[HBM] * 5,
        out_specs=VMEM,
        scratch_shapes=[
            pltpu.SMEM((2,), f32),
            pltpu.VMEM((n, rank), bf16),
            pltpu.VMEM((1, n), jnp.int32),
            pltpu.VMEM((2, 2, n), f32),
            pltpu.VMEM((EXTRA, rank), f32),
            pltpu.SemaphoreType.DMA((5,)),
        ],
        compiler_params=limit(2 * (n + EXTRA) * rank * 2),
        name="pack",
    )(*in_hbm(trunk_z.reshape(2), loadings, parents.reshape(1, n), load_base, lateral_z))

    def swap(block, offset):
        return lax.ppermute(block, "feeder", [(i, i ^ offset) for i in range(feeders)])

    every = {0: packed}
    for offset in sorted(range(2, feeders, 2), key=lambda o: -(o & -o)):
        every[offset] = swap(packed, offset)
    every[1] = swap(packed, 1)
    slots = list(every)
    early = len(slots)
    for offset in slots[1:-1]:
        every[offset + 1] = swap(every[offset], 1)
    slots = list(every)

    if far:
        held[far] = after(held[far], *(every[slot] for slot in slots[:early]))
    step = far // 2
    while step >= 1:
        for offset in list(held):
            held[offset ^ step] = trade(held[offset], step)
        step //= 2
    pieces = [held[offset] for offset in range(nodes)]

    start = (feeder // share) * width
    place = jnp.stack([(start // rows) ^ node, start % rows, feeder])

    def states(count):
        return [
            ((count, *matrix_shape), bf16),
            ((count, n, width), f32),
            ((count, 2 * n, width), f32),
            ((count, EXTRA, width), f32),
        ]

    state_bytes = (2 * n + EXTRA) * 8 * n + (3 * n + EXTRA) * width * 4 + (n + EXTRA) * rank * 2
    block, own, kept, *started = pl.pallas_call(
        functools.partial(early_kernel, nodes),
        out_shape=[
            jax.ShapeDtypeStruct((width, rank), bf16),
            jax.ShapeDtypeStruct(matrix_shape, bf16),
            pltpu.HBM((nodes - 1, rows, rank), bf16),
        ]
        + [jax.ShapeDtypeStruct(*state) for state in states(early)],
        in_specs=[SMEM, HBM] + [ANY] * (nodes - 1) + [VMEM] * early,
        out_specs=[VMEM, VMEM, HBM] + [VMEM] * 4,
        scratch_shapes=[pltpu.SemaphoreType.DMA, pltpu.SemaphoreType.DMA((nodes - 1,))],
        compiler_params=limit(early * state_bytes),
        cost_estimate=pl.CostEstimate(flops=early * (1 << 29), bytes_accessed=early * state_bytes, transcendentals=early * n * width),
        name="early",
    )(place, *in_hbm(pieces[0]), *pieces[1:], *(every[slot] for slot in slots[:early]))
    heads = pl.pallas_call(
        functools.partial(heads_kernel, slots, early),
        out_shape=jax.ShapeDtypeStruct((feeders, 8, width), f32),
        in_specs=[SMEM] + [VMEM] * (1 + feeders + 4),
        out_specs=VMEM,
        scratch_shapes=[pltpu.VMEM(*state) for state in states(max(feeders - early, 1))]
        + [
            pltpu.VMEM((feeders, 2 * n, width), f32),
            pltpu.VMEM((feeders, 8, width), f32),
            pltpu.VMEM((feeders, 8, width), f32),
        ],
        compiler_params=limit((feeders - early) * state_bytes + feeders * (2 * n + 16) * width * 4),
        name="heads",
    )(place, block, *(every[slot] for slot in slots), *started)
    given = lax.all_to_all(heads, "feeder", 0, 0, tiled=True)
    given = given[::share]

    chunks = scen // width
    swing, drop = pl.pallas_call(
        first_kernel,
        out_shape=(
            jax.ShapeDtypeStruct((chunks, n, width), f32),
            jax.ShapeDtypeStruct((chunks, 2 * n, width), f32),
        ),
        in_specs=[SMEM, VMEM, HBM, HBM, HBM],
        out_specs=(VMEM, VMEM),
        scratch_shapes=[
            pltpu.VMEM((n, rank), bf16),
            pltpu.VMEM((nodes, rows, rank), bf16),
            pltpu.SemaphoreType.DMA((nodes + 1,)),
        ],
        compiler_params=limit(3 * n * scen * 4 + scen * rank * 2),
        cost_estimate=pl.CostEstimate(flops=2 * scen * n * rank * 4, bytes_accessed=3 * n * scen * 4, transcendentals=scen * n),
        name="first",
    )(node.reshape(1), own, *in_hbm(loadings, factors, kept))
    return pl.pallas_call(
        volts_kernel,
        out_shape=(
            jax.ShapeDtypeStruct((scen, n), f32),
            jax.ShapeDtypeStruct((scen, n), f32),
        ),
        in_specs=[VMEM] * 4,
        out_specs=(HBM, HBM),
        scratch_shapes=[pltpu.VMEM((2, scen, n), f32), pltpu.SemaphoreType.DMA((2, chunks))],
        compiler_params=limit(5 * n * scen * 4),
        name="volts",
    )(own, swing, drop, given)


def solution(mesh):
    feeders = mesh.shape["feeder"]
    nodes = mesh.shape["node"]
    return jax.shard_map(
        functools.partial(local, feeders, nodes),
        mesh=mesh,
        in_specs=(
            P("node", None),
            P(("feeder", "node"), None),
            P(("feeder", "node")),
            P(None, ("feeder", "node")),
            P(None, ("feeder", "node")),
            P(None, "feeder", "node"),
        ),
        out_specs=(P(None, ("feeder", "node")), P(None, ("feeder", "node"))),
        check_vma=False,
    )
```

```python
import functools

import jax
import jax.numpy as jnp
from jax import lax
from jax.experimental import pallas as pl
from jax.experimental.pallas import tpu as pltpu
from jax.sharding import PartitionSpec as P

SWEEPS = 3
EXTRA = 16
LANES = 128

VMEM = pl.BlockSpec(memory_space=pltpu.VMEM)
SMEM = pl.BlockSpec(memory_space=pltpu.SMEM)
HBM = pl.BlockSpec(memory_space=pltpu.HBM)
ANY = pl.BlockSpec(memory_space=pl.ANY)


def split(x):
    high = x.astype(jnp.bfloat16)
    low = (x - high.astype(jnp.float32)).astype(jnp.bfloat16)
    return high, low


def product(left, right):
    return jnp.dot(left, right, preferred_element_type=jnp.float32)


def product_nt(left, right):
    return lax.dot_general(left, right, (((1,), (1,)), ((), ())), preferred_element_type=jnp.float32)


def wide(row, width):
    n = row.shape[1]
    if width <= n:
        return row[:, :width]
    return jnp.concatenate([row] * (width // n), axis=1)


def pack_kernel(
    trunk_ref, loadings_ref, parents_ref, base_ref, z_ref, out_ref, trunk, loads, owners, rows_ref, meta_ref, sems
):
    n = loadings_ref.shape[0]
    copies = [
        pltpu.make_async_copy(loadings_ref, loads, sems.at[0]),
        pltpu.make_async_copy(parents_ref, owners, sems.at[1]),
        pltpu.make_async_copy(base_ref, rows_ref.at[0], sems.at[2]),
        pltpu.make_async_copy(z_ref, rows_ref.at[1], sems.at[3]),
        pltpu.make_async_copy(trunk_ref, trunk, sems.at[4]),
    ]
    for copy in copies:
        copy.start()
    for copy in copies[1:]:
        copy.wait()
    pair_ids = lax.broadcasted_iota(jnp.int32, (2, n), 0)
    trunk_rows = jnp.where(pair_ids == 0, trunk[0], trunk[1])
    for index, rows in enumerate((rows_ref[0], rows_ref[1], trunk_rows)):
        high = rows.astype(jnp.bfloat16).astype(jnp.float32)
        middle = (rows - high).astype(jnp.bfloat16).astype(jnp.float32)
        meta_ref[2 * index : 2 * index + 2, 0:n] = high
        meta_ref[2 * index : 2 * index + 2, n : 2 * n] = middle
        meta_ref[8 + 2 * index : 10 + 2 * index, 0:n] = rows - high - middle
    meta_ref[6:8, 0:n] = jnp.broadcast_to(owners[...].astype(jnp.float32), (2, n))
    meta_ref[6:8, n : 2 * n] = jnp.zeros((2, n), jnp.float32)
    meta_ref[14:16, 0:n] = jnp.zeros((2, n), jnp.float32)
    meta_ref[8:16, n : 2 * n] = jnp.zeros((8, n), jnp.float32)
    meta = meta_ref[...].astype(jnp.bfloat16)
    copies[0].wait()
    out_ref[0:n, :] = loads[...]
    out_ref[n : n + EXTRA, :] = meta


def constants(section_ref, n):
    meta = section_ref[n : n + EXTRA, :].astype(jnp.float32)
    high, middle = meta[0:8, 0:n], meta[0:8, n : 2 * n]
    return high, middle, high + middle + meta[8:16, 0:n]


def section_paths(parents, n):
    rows = max(8, len(parents))
    row_ids = lax.broadcasted_iota(jnp.int32, (n, n), 0)
    lane_ids = lax.broadcasted_iota(jnp.int32, (n, n), 1)
    section_ids = lax.broadcasted_iota(jnp.int32, (rows, n), 0)
    stacked = jnp.full((rows, n), -1, jnp.int32)
    for index, row in enumerate(parents):
        stacked = jnp.where(section_ids == index, row.astype(jnp.int32), stacked)
    known = {1: stacked}

    def ancestor(distance):
        if distance not in known:
            step = 1 << (distance.bit_length() - 1)
            if step == distance:
                step //= 2
            far, near = ancestor(step), ancestor(distance - step)
            known[distance] = jnp.where(near < 0, -1, jnp.take_along_axis(far, jnp.maximum(near, 0), axis=1))
        return known[distance]

    digits = []
    unit = 1
    while unit < n:
        digits.append([ancestor(unit * digit).astype(jnp.float32) for digit in range(1, 8) if unit * digit < n])
        unit *= 8
    last = [found.T for found in digits.pop()]
    rows_b, lanes_b = (ids.astype(jnp.float32).astype(jnp.bfloat16) for ids in (row_ids, lane_ids))
    one, zero = jnp.ones((n, n), jnp.bfloat16), jnp.zeros((n, n), jnp.bfloat16)
    identity = jnp.where(rows_b == lanes_b, one, zero)
    out = []
    for index in range(len(parents)):
        product_t = None
        for digit in digits:
            factor = identity
            for found in digit:
                row = jnp.broadcast_to(found[index : index + 1, :].astype(jnp.bfloat16), (n, n))
                factor = jnp.where(rows_b == row, one, factor)
            product_t = factor if product_t is None else product(product_t, factor).astype(jnp.bfloat16)
        factor = identity
        for found in last:
            column = jnp.broadcast_to(found[:, index : index + 1], (n, n)).astype(jnp.bfloat16)
            factor = jnp.where(lanes_b == column, one, factor)
        out.append((factor, product_t))
    return [product_nt(left, right).astype(jnp.bfloat16) for left, right in out]


def section_matrices(sections, n):
    pad_ids = lax.broadcasted_iota(jnp.int32, (EXTRA, 2 * n), 0)
    highs, middles, rows = zip(*(constants(section, n) for section in sections))
    paths = section_paths([row[6:7] for row in rows], n)
    shared = []
    for path, high, middle in zip(paths, highs, middles):
        wide_path = path.astype(jnp.float32)

        def scaled(index):
            return jnp.concatenate([wide_path * high[index : index + 1], wide_path * middle[index : index + 1]], axis=1)

        left = jnp.concatenate([scaled(2), scaled(3)], axis=0).astype(jnp.bfloat16)
        shared.append(product_nt(left, jnp.concatenate([path, path], axis=1)))
    out = []
    for both, row in zip(shared, rows):
        resist, react = both[:n], both[n:]
        base_active, base_reactive = row[0:1], row[1:2]
        real_high, real_low = split(resist * base_active + react * base_reactive)
        imag_high, imag_low = split(react * base_active - resist * base_reactive)
        row_real = jnp.concatenate([base_active, base_reactive], axis=1)
        row_imag = jnp.concatenate([-base_reactive, base_active], axis=1)
        sums_high, sums_low = split(jnp.where(pad_ids == 0, row_real, jnp.where(pad_ids == 1, row_imag, 0.0)))

        def whole(real_part, imag_part, sums_part):
            top = jnp.concatenate([real_part, -imag_part], axis=1)
            bottom = jnp.concatenate([imag_part, real_part], axis=1)
            return jnp.concatenate([top, bottom, sums_part], axis=0)

        out.append(
            jnp.concatenate(
                [whole(real_high, imag_high, sums_high), whole(real_low, imag_low, sums_low)], axis=1
            )
        )
    return out


def swing_of(loadings, factors):
    level = product_nt(loadings, factors).astype(jnp.bfloat16).astype(jnp.float32)
    return 1.0 + 0.5 * jnp.tanh(level)


def apply(matrix, u):
    span = matrix.shape[1] // 2
    high, low = split(u)
    left = jnp.concatenate([matrix, matrix[:, :span]], axis=1)
    return product(left, jnp.concatenate([high, high, low], axis=0))


def apply_first(matrix, swing):
    n = matrix.shape[1] // 4
    high, low = split(swing)
    high_part, low_part = matrix[:, :n], matrix[:, 2 * n : 3 * n]
    return product(
        jnp.concatenate([high_part, low_part, high_part], axis=1), jnp.concatenate([high, high, low], axis=0)
    )


def inverse_of(swing, real, imag):
    return swing * pltpu.reciprocal(real * real + imag * imag, approx=True)


def scaled_volts(swing, real, imag):
    inverse = inverse_of(swing, real, imag)
    return jnp.concatenate([real * inverse, imag * inverse], axis=0)


def first_sweep(sections, factors_of, matrix_ref, swing_ref, drop_ref, inject_ref):
    n = swing_ref.shape[1]
    for start in range(0, len(sections), 8):
        group = sections[start : start + 8]
        for slot, matrix in enumerate(section_matrices(group, n), start):
            matrix_ref[slot] = matrix
        factors = factors_of(start)
        for slot, section in enumerate(group, start):
            swing = swing_of(section[0:n, :], factors)
            swing_ref[slot] = swing
            out = apply_first(matrix_ref[slot], swing)
            drop_ref[slot] = out[: 2 * n]
            inject_ref[slot] = out[2 * n :]


def early_kernel(pieces, place_ref, *refs):
    piece_refs, sections = refs[:pieces], refs[pieces:-9]
    factors_ref, own_ref, kept_ref, matrix_ref, swing_ref, drop_ref, inject_ref, sem, keep_sems = refs[-9:]
    width = factors_ref.shape[0]
    piece, offset = place_ref[0], place_ref[1]
    keeps = [
        pltpu.make_async_copy(piece_ref, kept_ref.at[index], keep_sems.at[index])
        for index, piece_ref in enumerate(piece_refs[1:])
    ]
    for copy in keeps:
        copy.start()
    for index, piece_ref in enumerate(piece_refs):
        @pl.when(piece == index)
        def _(piece_ref=piece_ref):
            rows = piece_ref.at[pl.ds(pl.multiple_of(offset, width), width), :]
            pltpu.make_async_copy(rows, factors_ref, sem).start()

    def factors_of(start):
        if start == 0:
            pltpu.make_async_copy(piece_refs[0].at[0:width, :], factors_ref, sem).wait()
        return factors_ref[...]

    first_sweep(sections, factors_of, matrix_ref, swing_ref, drop_ref, inject_ref)
    own_ref[...] = matrix_ref[0]
    for copy in keeps:
        copy.wait()


def heads_kernel(slots, early, place_ref, factors_ref, *refs):
    feeders = len(slots)
    sections = refs[:feeders]
    early_refs = refs[feeders : feeders + 4]
    head_ref, matrix_ref, swing_ref, drop_ref, inject_ref, again_ref, flow_ref, trunk_ref = refs[feeders + 4 :]
    width = factors_ref.shape[0]
    n = swing_ref.shape[1]
    first_sweep(sections[early:], lambda start: factors_ref[...], matrix_ref, swing_ref, drop_ref, inject_ref)
    late_refs = (matrix_ref, swing_ref, drop_ref, inject_ref)
    place = [jnp.bitwise_xor(place_ref[2], slot) for slot in slots]

    def of(index, which):
        return early_refs[which].at[index] if index < early else late_refs[which].at[index - early]

    for index in range(feeders):
        row = constants(sections[index], n)[2]
        trunk_ref[place[index], 0:2, :] = wide(row[4:6], width)
        flow_ref[place[index]] = of(index, 3)[0:8, :]

    def heads(sweep):
        flows = [None] * feeders
        real = jnp.zeros((1, width), jnp.float32)
        imag = real
        for g in reversed(range(feeders)):
            real = real + flow_ref[g, 0:1, :]
            imag = imag + flow_ref[g, 1:2, :]
            flows[g] = (real, imag)
        head_real = jnp.ones((1, width), jnp.float32)
        head_imag = jnp.zeros((1, width), jnp.float32)
        for g in range(feeders):
            r, x = trunk_ref[g, 0:1, :], trunk_ref[g, 1:2, :]
            real, imag = flows[g]
            head_real = head_real - (r * real - x * imag)
            head_imag = head_imag - (r * imag + x * real)
            head_ref[g, 2 * sweep : 2 * sweep + 1, :] = head_real
            head_ref[g, 2 * sweep + 1 : 2 * sweep + 2, :] = head_imag

    heads(0)
    for sweep in range(1, SWEEPS):
        for index in range(feeders):
            drop = of(index, 2) if sweep == 1 else again_ref.at[index]
            real = head_ref[place[index], 2 * sweep - 2 : 2 * sweep - 1, :] - drop[0:n, :]
            imag = head_ref[place[index], 2 * sweep - 1 : 2 * sweep, :] - drop[n : 2 * n, :]
            swing = of(index, 1)[...]
            if sweep < SWEEPS - 1:
                out = apply(of(index, 0)[...], scaled_volts(swing, real, imag))
                again_ref[index] = out[: 2 * n]
                flow_ref[place[index]] = out[2 * n : 2 * n + 8]
            else:
                base = constants(sections[index], n)[2].T
                active, reactive = base[:, 0:1], base[:, 1:2]
                inverse = inverse_of(swing, real, imag)
                flow_ref[place[index], 0:1, :] = jnp.sum(inverse * (active * real + reactive * imag), axis=0, keepdims=True)
                flow_ref[place[index], 1:2, :] = jnp.sum(inverse * (active * imag - reactive * real), axis=0, keepdims=True)
        heads(sweep)
    for g in range(feeders):
        head_ref[g, 2 * SWEEPS :, :] = jnp.zeros((head_ref.shape[1] - 2 * SWEEPS, width), jnp.float32)


def first_kernel(
    node_ref, matrix_ref, loadings_ref, rows_ref, kept_ref, swing_ref, drop_ref, loads, factors_ref, sems
):
    n = loadings_ref.shape[0]
    width = swing_ref.shape[2]
    pieces = 1 + kept_ref.shape[0]
    chunks = rows_ref.shape[0] // width
    copies = [pltpu.make_async_copy(loadings_ref, loads, sems.at[pieces])]
    for index in range(pieces):
        piece_ref = kept_ref.at[index - 1] if index else rows_ref
        copies.append(pltpu.make_async_copy(piece_ref, factors_ref.at[index], sems.at[index]))
    for copy in copies:
        copy.start()
    matrix = matrix_ref[0 : 2 * n, :]
    for copy in copies:
        copy.wait()
    loadings = loads[...]
    together = 4 // chunks if chunks < 4 else 1

    @pl.loop(0, pieces // together)
    def _(outer):
        for inner in range(together):
            index = outer * together + inner
            for part in range(chunks):
                chunk = jnp.bitwise_xor(node_ref[0], index) * chunks + part
                swing = swing_of(loadings, factors_ref[index, part * width : (part + 1) * width, :])
                swing_ref[chunk] = swing
                drop_ref[chunk] = apply_first(matrix, swing)


def volts_kernel(matrix_ref, swing_ref, drop_ref, head_ref, real_ref, imag_ref, out_ref, sems):
    n = swing_ref.shape[1]
    chunks, width = swing_ref.shape[0], swing_ref.shape[2]
    matrix = matrix_ref[0 : 2 * n, :]
    together = 4
    rounds = chunks // together

    def copies(outer):
        rows = pl.ds(pl.multiple_of(outer * together * width, together * width), together * width)
        return [
            pltpu.make_async_copy(out_ref.at[index, rows, :], to_ref.at[rows, :], sems.at[index, outer])
            for index, to_ref in enumerate((real_ref, imag_ref))
        ]

    @pl.loop(0, rounds)
    def _(outer):
        drops = [None] * together
        for sweep in range(SWEEPS):
            for inner in range(together):
                chunk = outer * together + inner
                drop = drop_ref[chunk] if sweep == 0 else drops[inner]
                real = head_ref[chunk, 2 * sweep : 2 * sweep + 1, :] - drop[:n]
                imag = head_ref[chunk, 2 * sweep + 1 : 2 * sweep + 2, :] - drop[n:]
                if sweep < SWEEPS - 1:
                    drops[inner] = apply(matrix, scaled_volts(swing_ref[chunk], real, imag))
                else:
                    rows = pl.ds(pl.multiple_of(chunk * width, width), width)
                    out_ref[0, rows, :] = real.T
                    out_ref[1, rows, :] = imag.T
        for copy in copies(outer):
            copy.start()

    for outer in range(rounds):
        for copy in copies(outer):
            copy.wait()


def after_kernel(*refs):
    del refs


def after(array, *others):
    return pl.pallas_call(
        after_kernel,
        out_shape=jax.ShapeDtypeStruct(array.shape, array.dtype),
        in_specs=[ANY] * (1 + len(others)),
        out_specs=ANY,
        input_output_aliases={0: 0},
        compiler_params=limit(0),
        name="after",
    )(array, *others)


def in_hbm(*arrays):
    return [pltpu.with_memory_space_constraint(array, pltpu.HBM) for array in arrays]


def limit(nbytes):
    return pltpu.CompilerParams(vmem_limit_bytes=min(60 << 20, int(nbytes) + (16 << 20)))


def local(feeders, nodes, factors, loadings, parents, load_base, lateral_z, trunk_z):
    node = lax.axis_index("node").astype(jnp.int32)
    feeder = lax.axis_index("feeder").astype(jnp.int32)
    rows, rank = factors.shape
    scen = rows * nodes
    n = loadings.shape[0]
    width = max(scen // feeders, LANES)
    share = feeders * width // scen
    f32, bf16 = jnp.float32, jnp.bfloat16
    matrix_shape = (2 * n + EXTRA, 4 * n)

    def trade(block, offset):
        return lax.ppermute(block, "node", [(i, i ^ offset) for i in range(nodes)])

    held = {0: factors}
    far = nodes // 2
    if far:
        held[far] = trade(factors, far)

    packed = pl.pallas_call(
        pack_kernel,
        out_shape=jax.ShapeDtypeStruct((n + EXTRA, rank), bf16),
        in_specs=[HBM] * 5,
        out_specs=VMEM,
        scratch_shapes=[
            pltpu.SMEM((2,), f32),
            pltpu.VMEM((n, rank), bf16),
            pltpu.VMEM((1, n), jnp.int32),
            pltpu.VMEM((2, 2, n), f32),
            pltpu.VMEM((EXTRA, rank), f32),
            pltpu.SemaphoreType.DMA((5,)),
        ],
        compiler_params=limit(2 * (n + EXTRA) * rank * 2),
        name="pack",
    )(*in_hbm(trunk_z.reshape(2), loadings, parents.reshape(1, n), load_base, lateral_z))

    def swap(block, offset):
        return lax.ppermute(block, "feeder", [(i, i ^ offset) for i in range(feeders)])

    every = {0: packed}
    for offset in sorted(range(2, feeders, 2), key=lambda o: -(o & -o)):
        every[offset] = swap(packed, offset)
    every[1] = swap(packed, 1)
    slots = list(every)
    early = len(slots)
    for offset in slots[1:-1]:
        every[offset + 1] = swap(every[offset], 1)
    slots = list(every)

    if far:
        held[far] = after(held[far], *(every[slot] for slot in slots[:early]))
    step = far // 2
    while step >= 1:
        for offset in list(held):
            held[offset ^ step] = trade(held[offset], step)
        step //= 2
    pieces = [held[offset] for offset in range(nodes)]

    start = (feeder // share) * width
    place = jnp.stack([(start // rows) ^ node, start % rows, feeder])

    def states(count):
        return [
            ((count, *matrix_shape), bf16),
            ((count, n, width), f32),
            ((count, 2 * n, width), f32),
            ((count, EXTRA, width), f32),
        ]

    state_bytes = (2 * n + EXTRA) * 8 * n + (3 * n + EXTRA) * width * 4 + (n + EXTRA) * rank * 2
    block, own, kept, *started = pl.pallas_call(
        functools.partial(early_kernel, nodes),
        out_shape=[
            jax.ShapeDtypeStruct((width, rank), bf16),
            jax.ShapeDtypeStruct(matrix_shape, bf16),
            pltpu.HBM((nodes - 1, rows, rank), bf16),
        ]
        + [jax.ShapeDtypeStruct(*state) for state in states(early)],
        in_specs=[SMEM, HBM] + [ANY] * (nodes - 1) + [VMEM] * early,
        out_specs=[VMEM, VMEM, HBM] + [VMEM] * 4,
        scratch_shapes=[pltpu.SemaphoreType.DMA, pltpu.SemaphoreType.DMA((nodes - 1,))],
        compiler_params=limit(early * state_bytes),
        cost_estimate=pl.CostEstimate(flops=early * (1 << 29), bytes_accessed=early * state_bytes, transcendentals=early * n * width),
        name="early",
    )(place, *in_hbm(pieces[0]), *pieces[1:], *(every[slot] for slot in slots[:early]))
    heads = pl.pallas_call(
        functools.partial(heads_kernel, slots, early),
        out_shape=jax.ShapeDtypeStruct((feeders, 8, width), f32),
        in_specs=[SMEM] + [VMEM] * (1 + feeders + 4),
        out_specs=VMEM,
        scratch_shapes=[pltpu.VMEM(*state) for state in states(max(feeders - early, 1))]
        + [
            pltpu.VMEM((feeders, 2 * n, width), f32),
            pltpu.VMEM((feeders, 8, width), f32),
            pltpu.VMEM((feeders, 8, width), f32),
        ],
        compiler_params=limit((feeders - early) * state_bytes + feeders * (2 * n + 16) * width * 4),
        name="heads",
    )(place, block, *(every[slot] for slot in slots), *started)
    given = lax.all_to_all(heads, "feeder", 0, 0, tiled=True)
    given = given[::share]

    chunks = scen // width
    swing, drop = pl.pallas_call(
        first_kernel,
        out_shape=(
            jax.ShapeDtypeStruct((chunks, n, width), f32),
            jax.ShapeDtypeStruct((chunks, 2 * n, width), f32),
        ),
        in_specs=[SMEM, VMEM, HBM, HBM, HBM],
        out_specs=(VMEM, VMEM),
        scratch_shapes=[
            pltpu.VMEM((n, rank), bf16),
            pltpu.VMEM((nodes, rows, rank), bf16),
            pltpu.SemaphoreType.DMA((nodes + 1,)),
        ],
        compiler_params=limit(3 * n * scen * 4 + scen * rank * 2),
        cost_estimate=pl.CostEstimate(flops=2 * scen * n * rank * 4, bytes_accessed=3 * n * scen * 4, transcendentals=scen * n),
        name="first",
    )(node.reshape(1), own, *in_hbm(loadings, factors, kept))
    return pl.pallas_call(
        volts_kernel,
        out_shape=(
            jax.ShapeDtypeStruct((scen, n), f32),
            jax.ShapeDtypeStruct((scen, n), f32),
        ),
        in_specs=[VMEM] * 4,
        out_specs=(HBM, HBM),
        scratch_shapes=[pltpu.VMEM((2, scen, n), f32), pltpu.SemaphoreType.DMA((2, chunks))],
        compiler_params=limit(5 * n * scen * 4),
        name="volts",
    )(own, swing, drop, given)


def solution(mesh):
    feeders = mesh.shape["feeder"]
    nodes = mesh.shape["node"]
    return jax.shard_map(
        functools.partial(local, feeders, nodes),
        mesh=mesh,
        in_specs=(
            P("node", None),
            P(("feeder", "node"), None),
            P(("feeder", "node")),
            P(None, ("feeder", "node")),
            P(None, ("feeder", "node")),
            P(None, "feeder", "node"),
        ),
        out_specs=(P(None, ("feeder", "node")), P(None, ("feeder", "node"))),
        check_vma=False,
    )
```

```python
import functools

import jax
import jax.numpy as jnp
from jax import lax
from jax.experimental import pallas as pl
from jax.experimental.pallas import tpu as pltpu
from jax.sharding import PartitionSpec as P

SWEEPS = 3
EXTRA = 16
LANES = 128

VMEM = pl.BlockSpec(memory_space=pltpu.VMEM)
SMEM = pl.BlockSpec(memory_space=pltpu.SMEM)
HBM = pl.BlockSpec(memory_space=pltpu.HBM)
ANY = pl.BlockSpec(memory_space=pl.ANY)


def split(x):
    high = x.astype(jnp.bfloat16)
    low = (x - high.astype(jnp.float32)).astype(jnp.bfloat16)
    return high, low


def product(left, right):
    return jnp.dot(left, right, preferred_element_type=jnp.float32)


def product_nt(left, right):
    return lax.dot_general(left, right, (((1,), (1,)), ((), ())), preferred_element_type=jnp.float32)


def wide(row, width):
    n = row.shape[1]
    if width <= n:
        return row[:, :width]
    return jnp.concatenate([row] * (width // n), axis=1)


def pack_kernel(
    trunk_ref, loadings_ref, parents_ref, base_ref, z_ref, out_ref, trunk, loads, owners, rows_ref, meta_ref, sems
):
    n = loadings_ref.shape[0]
    copies = [
        pltpu.make_async_copy(loadings_ref, loads, sems.at[0]),
        pltpu.make_async_copy(parents_ref, owners, sems.at[1]),
        pltpu.make_async_copy(base_ref, rows_ref.at[0], sems.at[2]),
        pltpu.make_async_copy(z_ref, rows_ref.at[1], sems.at[3]),
        pltpu.make_async_copy(trunk_ref, trunk, sems.at[4]),
    ]
    for copy in copies:
        copy.start()
    for copy in copies[1:]:
        copy.wait()
    pair_ids = lax.broadcasted_iota(jnp.int32, (2, n), 0)
    trunk_rows = jnp.where(pair_ids == 0, trunk[0], trunk[1])
    for index, rows in enumerate((rows_ref[0], rows_ref[1], trunk_rows)):
        high = rows.astype(jnp.bfloat16).astype(jnp.float32)
        middle = (rows - high).astype(jnp.bfloat16).astype(jnp.float32)
        meta_ref[2 * index : 2 * index + 2, 0:n] = high
        meta_ref[2 * index : 2 * index + 2, n : 2 * n] = middle
        meta_ref[8 + 2 * index : 10 + 2 * index, 0:n] = rows - high - middle
    meta_ref[6:8, 0:n] = jnp.broadcast_to(owners[...].astype(jnp.float32), (2, n))
    meta_ref[6:8, n : 2 * n] = jnp.zeros((2, n), jnp.float32)
    meta_ref[14:16, 0:n] = jnp.zeros((2, n), jnp.float32)
    meta_ref[8:16, n : 2 * n] = jnp.zeros((8, n), jnp.float32)
    meta = meta_ref[...].astype(jnp.bfloat16)
    copies[0].wait()
    out_ref[0:n, :] = loads[...]
    out_ref[n : n + EXTRA, :] = meta


def constants(section_ref, n):
    meta = section_ref[n : n + EXTRA, :].astype(jnp.float32)
    high, middle = meta[0:8, 0:n], meta[0:8, n : 2 * n]
    return high, middle, high + middle + meta[8:16, 0:n]


def matrix_steps(sections, n):
    highs, middles, rows = zip(*(constants(section, n) for section in sections))
    row_ids = lax.broadcasted_iota(jnp.int32, (n, n), 0)
    lane_ids = lax.broadcasted_iota(jnp.int32, (n, n), 1)
    section_ids = lax.broadcasted_iota(jnp.int32, (max(8, len(sections)), n), 0)
    stacked = jnp.full(section_ids.shape, -1, jnp.int32)
    for index, row in enumerate(rows):
        stacked = jnp.where(section_ids == index, row[6:7].astype(jnp.int32), stacked)
    known = {1: stacked}

    def ancestor(distance):
        if distance not in known:
            step = 1 << (distance.bit_length() - 1)
            if step == distance:
                step //= 2
            far, near = ancestor(step), ancestor(distance - step)
            known[distance] = jnp.where(near < 0, -1, jnp.take_along_axis(far, jnp.maximum(near, 0), axis=1))
        return known[distance]

    digits = []
    unit = 1
    while unit < n:
        digits.append([ancestor(unit * digit).astype(jnp.float32) for digit in range(1, 8) if unit * digit < n])
        unit *= 8
    last = [found.T for found in digits.pop()]
    yield None

    rows_b, lanes_b = (ids.astype(jnp.float32).astype(jnp.bfloat16) for ids in (row_ids, lane_ids))
    one, zero = jnp.ones((n, n), jnp.bfloat16), jnp.zeros((n, n), jnp.bfloat16)
    identity = jnp.where(rows_b == lanes_b, one, zero)
    products = [None] * len(sections)
    for index in range(len(sections)):
        for digit in digits:
            factor = identity
            for found in digit:
                row = jnp.broadcast_to(found[index : index + 1, :].astype(jnp.bfloat16), (n, n))
                factor = jnp.where(rows_b == row, one, factor)
            done = products[index]
            products[index] = factor if done is None else product(done, factor).astype(jnp.bfloat16)
    yield None

    paths = []
    for index in range(len(sections)):
        factor = identity
        for found in last:
            column = jnp.broadcast_to(found[:, index : index + 1], (n, n)).astype(jnp.bfloat16)
            factor = jnp.where(lanes_b == column, one, factor)
        paths.append(product_nt(factor, products[index]).astype(jnp.bfloat16))
    yield None

    shared = []
    for path, high, middle in zip(paths, highs, middles):
        wide_path = path.astype(jnp.float32)

        def scaled(index):
            return jnp.concatenate([wide_path * high[index : index + 1], wide_path * middle[index : index + 1]], axis=1)

        left = jnp.concatenate([scaled(2), scaled(3)], axis=0).astype(jnp.bfloat16)
        shared.append(product_nt(left, jnp.concatenate([path, path], axis=1)))
    yield None

    pad_ids = lax.broadcasted_iota(jnp.int32, (EXTRA, 2 * n), 0)
    out = []
    for both, row in zip(shared, rows):
        resist, react = both[:n], both[n:]
        base_active, base_reactive = row[0:1], row[1:2]
        real_high, real_low = split(resist * base_active + react * base_reactive)
        imag_high, imag_low = split(react * base_active - resist * base_reactive)
        row_real = jnp.concatenate([base_active, base_reactive], axis=1)
        row_imag = jnp.concatenate([-base_reactive, base_active], axis=1)
        sums_high, sums_low = split(jnp.where(pad_ids == 0, row_real, jnp.where(pad_ids == 1, row_imag, 0.0)))

        def whole(real_part, imag_part, sums_part):
            top = jnp.concatenate([real_part, -imag_part], axis=1)
            bottom = jnp.concatenate([imag_part, real_part], axis=1)
            return jnp.concatenate([top, bottom, sums_part], axis=0)

        out.append(
            jnp.concatenate(
                [whole(real_high, imag_high, sums_high), whole(real_low, imag_low, sums_low)], axis=1
            )
        )
    yield out


def swing_of(loadings, factors):
    level = product_nt(loadings, factors).astype(jnp.bfloat16).astype(jnp.float32)
    return 1.0 + 0.5 * jnp.tanh(level)


def apply(matrix, u):
    span = matrix.shape[1] // 2
    high, low = split(u)
    left = jnp.concatenate([matrix, matrix[:, :span]], axis=1)
    return product(left, jnp.concatenate([high, high, low], axis=0))


def apply_first(matrix, swing):
    n = matrix.shape[1] // 4
    high, low = split(swing)
    high_part, low_part = matrix[:, :n], matrix[:, 2 * n : 3 * n]
    return product(
        jnp.concatenate([high_part, low_part, high_part], axis=1), jnp.concatenate([high, high, low], axis=0)
    )


def inverse_of(swing, real, imag):
    return swing * pltpu.reciprocal(real * real + imag * imag, approx=True)


def scaled_volts(swing, real, imag):
    inverse = inverse_of(swing, real, imag)
    return jnp.concatenate([real * inverse, imag * inverse], axis=0)


def early_kernel(pieces, place_ref, *refs):
    piece_refs, sections = refs[:pieces], refs[pieces:-9]
    factors_ref, own_ref, kept_ref, matrix_ref, swing_ref, drop_ref, inject_ref, sem, keep_sems = refs[-9:]
    width = factors_ref.shape[0]
    piece, offset = place_ref[0], place_ref[1]
    keeps = [
        pltpu.make_async_copy(piece_ref, kept_ref.at[index], keep_sems.at[index])
        for index, piece_ref in enumerate(piece_refs[1:])
    ]
    for copy in keeps:
        copy.start()
    for index, piece_ref in enumerate(piece_refs):
        @pl.when(piece == index)
        def _(piece_ref=piece_ref):
            rows = piece_ref.at[pl.ds(pl.multiple_of(offset, width), width), :]
            pltpu.make_async_copy(rows, factors_ref, sem).start()

    n = swing_ref.shape[1]
    for start in range(0, len(sections), 8):
        group = list(enumerate(sections))[start : start + 8]
        steps = matrix_steps([section for _, section in group], n)
        next(steps)
        if start == 0:
            pltpu.make_async_copy(piece_refs[0].at[0:width, :], factors_ref, sem).wait()
        for slot, section in group:
            swing_ref[slot] = swing_of(section[0:n, :], factors_ref[...])
        *_, matrices = steps
        for (slot, _), matrix in zip(group, matrices):
            matrix_ref[slot] = matrix
            out = apply_first(matrix_ref[slot], swing_ref[slot])
            drop_ref[slot] = out[: 2 * n]
            inject_ref[slot] = out[2 * n :]
    own_ref[...] = matrix_ref[0]
    for copy in keeps:
        copy.wait()


def heads_kernel(slots, early, place_ref, factors_ref, *refs):
    feeders = len(slots)
    sections = refs[:feeders]
    early_refs = refs[feeders : feeders + 4]
    head_ref, matrix_ref, swing_ref, drop_ref, again_ref, flow_ref, trunk_ref = refs[feeders + 4 :]
    width = factors_ref.shape[0]
    n = swing_ref.shape[1]
    place = [jnp.bitwise_xor(place_ref[2], slot) for slot in slots]
    late_refs = (matrix_ref, swing_ref, drop_ref)

    def of(index, which):
        return early_refs[which].at[index] if index < early else late_refs[which].at[index - early]

    def flow_of(index, real, imag):
        base = constants(sections[index], n)[2].T
        active, reactive = base[:, 0:1], base[:, 1:2]
        if imag is None:
            parts = (active * real, -reactive * real)
        else:
            parts = (active * real + reactive * imag, active * imag - reactive * real)
        return [jnp.sum(part, axis=0, keepdims=True) for part in parts]

    groups = [list(range(start, min(start + 8, feeders))) for start in range(early, feeders, 8)]
    steps = [matrix_steps([sections[index] for index in group], n) for group in groups]
    if steps:
        next(steps[0])
    for index in range(feeders):
        row = constants(sections[index], n)[2]
        trunk_ref[place[index], 0:2, :] = wide(row[4:6], width)
        if index < early:
            flow_ref[place[index]] = of(index, 3)[0:8, :]
        else:
            swing = swing_of(sections[index][0:n, :], factors_ref[...])
            of(index, 1)[...] = swing
            for part, total in enumerate(flow_of(index, swing, None)):
                flow_ref[place[index], part : part + 1, :] = total

    def heads(sweep):
        flows = [None] * feeders
        real = jnp.zeros((1, width), jnp.float32)
        imag = real
        for g in reversed(range(feeders)):
            real = real + flow_ref[g, 0:1, :]
            imag = imag + flow_ref[g, 1:2, :]
            flows[g] = (real, imag)
        head_real = jnp.ones((1, width), jnp.float32)
        head_imag = jnp.zeros((1, width), jnp.float32)
        for g in range(feeders):
            r, x = trunk_ref[g, 0:1, :], trunk_ref[g, 1:2, :]
            real, imag = flows[g]
            head_real = head_real - (r * real - x * imag)
            head_imag = head_imag - (r * imag + x * real)
            head_ref[g, 2 * sweep : 2 * sweep + 1, :] = head_real
            head_ref[g, 2 * sweep + 1 : 2 * sweep + 2, :] = head_imag

    def volts(index, sweep):
        drop = of(index, 2) if sweep == 1 else again_ref.at[index]
        real = head_ref[place[index], 2 * sweep - 2 : 2 * sweep - 1, :] - drop[0:n, :]
        imag = head_ref[place[index], 2 * sweep - 1 : 2 * sweep, :] - drop[n : 2 * n, :]
        return real, imag

    def middle(index, sweep):
        out = apply(of(index, 0)[...], scaled_volts(of(index, 1)[...], *volts(index, sweep)))
        again_ref[index] = out[: 2 * n]
        flow_ref[place[index]] = out[2 * n : 2 * n + 8]

    heads(0)
    ready = list(range(early))
    for group, step in zip(groups, steps):
        for matrices in step:
            if ready:
                middle(ready.pop(0), 1)
        for index, matrix in zip(group, matrices):
            of(index, 0)[...] = matrix
            of(index, 2)[...] = apply_first(matrix, of(index, 1)[...])[: 2 * n]
    for index in ready + list(range(early, feeders)):
        middle(index, 1)
    heads(1)
    for sweep in range(2, SWEEPS):
        for index in range(feeders):
            if sweep < SWEEPS - 1:
                middle(index, sweep)
            else:
                real, imag = volts(index, sweep)
                inverse = inverse_of(of(index, 1)[...], real, imag)
                for part, total in enumerate(flow_of(index, real * inverse, imag * inverse)):
                    flow_ref[place[index], part : part + 1, :] = total
        heads(sweep)
    for g in range(feeders):
        head_ref[g, 2 * SWEEPS :, :] = jnp.zeros((head_ref.shape[1] - 2 * SWEEPS, width), jnp.float32)


def first_kernel(
    node_ref, matrix_ref, loadings_ref, rows_ref, kept_ref, swing_ref, drop_ref, loads, factors_ref, sems
):
    n = loadings_ref.shape[0]
    width = swing_ref.shape[2]
    pieces = 1 + kept_ref.shape[0]
    chunks = rows_ref.shape[0] // width
    copies = [pltpu.make_async_copy(loadings_ref, loads, sems.at[pieces])]
    for index in range(pieces):
        piece_ref = kept_ref.at[index - 1] if index else rows_ref
        copies.append(pltpu.make_async_copy(piece_ref, factors_ref.at[index], sems.at[index]))
    for copy in copies:
        copy.start()
    matrix = matrix_ref[0 : 2 * n, :]
    for copy in copies:
        copy.wait()
    loadings = loads[...]
    together = 4 // chunks if chunks < 4 else 1

    @pl.loop(0, pieces // together)
    def _(outer):
        for inner in range(together):
            index = outer * together + inner
            for part in range(chunks):
                chunk = jnp.bitwise_xor(node_ref[0], index) * chunks + part
                swing = swing_of(loadings, factors_ref[index, part * width : (part + 1) * width, :])
                swing_ref[chunk] = swing
                drop_ref[chunk] = apply_first(matrix, swing)


def volts_kernel(matrix_ref, swing_ref, drop_ref, head_ref, real_ref, imag_ref, out_ref, sems):
    n = swing_ref.shape[1]
    chunks, width = swing_ref.shape[0], swing_ref.shape[2]
    matrix = matrix_ref[0 : 2 * n, :]
    drops = [None] * chunks
    copies = []

    def advance(chunk, sweep):
        drop = drop_ref[chunk] if sweep == 0 else drops[chunk]
        real = head_ref[chunk, 2 * sweep : 2 * sweep + 1, :] - drop[:n]
        imag = head_ref[chunk, 2 * sweep + 1 : 2 * sweep + 2, :] - drop[n:]
        if sweep < SWEEPS - 1:
            drops[chunk] = apply(matrix, scaled_volts(swing_ref[chunk], real, imag))
            return
        rows = slice(chunk * width, (chunk + 1) * width)
        for index, (part, to_ref) in enumerate(((real, real_ref), (imag, imag_ref))):
            out_ref[index, rows, :] = part.T
            copies.append(pltpu.make_async_copy(out_ref.at[index, rows, :], to_ref.at[rows, :], sems.at[index, chunk]))
            copies[-1].start()

    for turn in range(chunks + SWEEPS - 1):
        for sweep in reversed(range(SWEEPS)):
            if 0 <= turn - sweep < chunks:
                advance(turn - sweep, sweep)
    for copy in copies:
        copy.wait()


def after_kernel(*refs):
    del refs


def after(array, *others):
    return pl.pallas_call(
        after_kernel,
        out_shape=jax.ShapeDtypeStruct(array.shape, array.dtype),
        in_specs=[ANY] * (1 + len(others)),
        out_specs=ANY,
        input_output_aliases={0: 0},
        compiler_params=limit(0),
        name="after",
    )(array, *others)


def in_hbm(*arrays):
    return [pltpu.with_memory_space_constraint(array, pltpu.HBM) for array in arrays]


def limit(nbytes):
    return pltpu.CompilerParams(vmem_limit_bytes=min(60 << 20, int(nbytes) + (16 << 20)))


def local(feeders, nodes, factors, loadings, parents, load_base, lateral_z, trunk_z):
    node = lax.axis_index("node").astype(jnp.int32)
    feeder = lax.axis_index("feeder").astype(jnp.int32)
    rows, rank = factors.shape
    scen = rows * nodes
    n = loadings.shape[0]
    width = max(scen // feeders, LANES)
    share = feeders * width // scen
    f32, bf16 = jnp.float32, jnp.bfloat16
    matrix_shape = (2 * n + EXTRA, 4 * n)

    def trade(block, offset):
        return lax.ppermute(block, "node", [(i, i ^ offset) for i in range(nodes)])

    held = {0: factors}
    far = nodes // 2
    if far:
        held[far] = trade(factors, far)

    packed = pl.pallas_call(
        pack_kernel,
        out_shape=jax.ShapeDtypeStruct((n + EXTRA, rank), bf16),
        in_specs=[HBM] * 5,
        out_specs=VMEM,
        scratch_shapes=[
            pltpu.SMEM((2,), f32),
            pltpu.VMEM((n, rank), bf16),
            pltpu.VMEM((1, n), jnp.int32),
            pltpu.VMEM((2, 2, n), f32),
            pltpu.VMEM((EXTRA, rank), f32),
            pltpu.SemaphoreType.DMA((5,)),
        ],
        compiler_params=limit(2 * (n + EXTRA) * rank * 2),
        name="pack",
    )(*in_hbm(trunk_z.reshape(2), loadings, parents.reshape(1, n), load_base, lateral_z))

    def swap(block, offset):
        return lax.ppermute(block, "feeder", [(i, i ^ offset) for i in range(feeders)])

    every = {0: packed}
    for offset in sorted(range(2, feeders, 2), key=lambda o: -(o & -o)):
        every[offset] = swap(packed, offset)
    every[1] = swap(packed, 1)
    slots = list(every)
    early = len(slots)
    for offset in slots[1:-1]:
        every[offset + 1] = swap(every[offset], 1)
    slots = list(every)

    if far:
        held[far] = after(held[far], *(every[slot] for slot in slots[:early]))
    step = far // 2
    while step >= 1:
        for offset in list(held):
            held[offset ^ step] = trade(held[offset], step)
        step //= 2
    pieces = [held[offset] for offset in range(nodes)]

    start = (feeder // share) * width
    place = jnp.stack([(start // rows) ^ node, start % rows, feeder])

    def states(count):
        return [
            ((count, *matrix_shape), bf16),
            ((count, n, width), f32),
            ((count, 2 * n, width), f32),
            ((count, EXTRA, width), f32),
        ]

    state_bytes = (2 * n + EXTRA) * 8 * n + (3 * n + EXTRA) * width * 4 + (n + EXTRA) * rank * 2
    block, own, kept, *started = pl.pallas_call(
        functools.partial(early_kernel, nodes),
        out_shape=[
            jax.ShapeDtypeStruct((width, rank), bf16),
            jax.ShapeDtypeStruct(matrix_shape, bf16),
            pltpu.HBM((nodes - 1, rows, rank), bf16),
        ]
        + [jax.ShapeDtypeStruct(*state) for state in states(early)],
        in_specs=[SMEM, HBM] + [ANY] * (nodes - 1) + [VMEM] * early,
        out_specs=[VMEM, VMEM, HBM] + [VMEM] * 4,
        scratch_shapes=[pltpu.SemaphoreType.DMA, pltpu.SemaphoreType.DMA((nodes - 1,))],
        compiler_params=limit(early * state_bytes),
        cost_estimate=pl.CostEstimate(flops=early * (1 << 29), bytes_accessed=early * state_bytes, transcendentals=early * n * width),
        name="early",
    )(place, *in_hbm(pieces[0]), *pieces[1:], *(every[slot] for slot in slots[:early]))
    heads = pl.pallas_call(
        functools.partial(heads_kernel, slots, early),
        out_shape=jax.ShapeDtypeStruct((feeders, 8, width), f32),
        in_specs=[SMEM] + [VMEM] * (1 + feeders + 4),
        out_specs=VMEM,
        scratch_shapes=[pltpu.VMEM(*state) for state in states(max(feeders - early, 1))[:3]]
        + [
            pltpu.VMEM((feeders, 2 * n, width), f32),
            pltpu.VMEM((feeders, 8, width), f32),
            pltpu.VMEM((feeders, 8, width), f32),
        ],
        compiler_params=limit((feeders - early) * state_bytes + feeders * (2 * n + 16) * width * 4),
        name="heads",
    )(place, block, *(every[slot] for slot in slots), *started)
    given = lax.all_to_all(heads, "feeder", 0, 0, tiled=True)
    given = given[::share]

    chunks = scen // width
    swing, drop = pl.pallas_call(
        first_kernel,
        out_shape=(
            jax.ShapeDtypeStruct((chunks, n, width), f32),
            jax.ShapeDtypeStruct((chunks, 2 * n, width), f32),
        ),
        in_specs=[SMEM, VMEM, HBM, HBM, HBM],
        out_specs=(VMEM, VMEM),
        scratch_shapes=[
            pltpu.VMEM((n, rank), bf16),
            pltpu.VMEM((nodes, rows, rank), bf16),
            pltpu.SemaphoreType.DMA((nodes + 1,)),
        ],
        compiler_params=limit(3 * n * scen * 4 + scen * rank * 2),
        cost_estimate=pl.CostEstimate(flops=2 * scen * n * rank * 4, bytes_accessed=3 * n * scen * 4, transcendentals=scen * n),
        name="first",
    )(node.reshape(1), own, *in_hbm(loadings, factors, kept))
    return pl.pallas_call(
        volts_kernel,
        out_shape=(
            jax.ShapeDtypeStruct((scen, n), f32),
            jax.ShapeDtypeStruct((scen, n), f32),
        ),
        in_specs=[VMEM] * 4,
        out_specs=(HBM, HBM),
        scratch_shapes=[pltpu.VMEM((2, scen, n), f32), pltpu.SemaphoreType.DMA((2, chunks))],
        compiler_params=limit(5 * n * scen * 4),
        name="volts",
    )(own, swing, drop, given)


def solution(mesh):
    feeders = mesh.shape["feeder"]
    nodes = mesh.shape["node"]
    return jax.shard_map(
        functools.partial(local, feeders, nodes),
        mesh=mesh,
        in_specs=(
            P("node", None),
            P(("feeder", "node"), None),
            P(("feeder", "node")),
            P(None, ("feeder", "node")),
            P(None, ("feeder", "node")),
            P(None, "feeder", "node"),
        ),
        out_specs=(P(None, ("feeder", "node")), P(None, ("feeder", "node"))),
        check_vma=False,
    )
```

```python
import functools

import jax
import jax.numpy as jnp
from jax import lax
from jax.experimental import pallas as pl
from jax.experimental.pallas import tpu as pltpu
from jax.sharding import PartitionSpec as P

SWEEPS = 3
EXTRA = 16
LANES = 128

VMEM = pl.BlockSpec(memory_space=pltpu.VMEM)
SMEM = pl.BlockSpec(memory_space=pltpu.SMEM)
HBM = pl.BlockSpec(memory_space=pltpu.HBM)
ANY = pl.BlockSpec(memory_space=pl.ANY)


def split(x):
    high = x.astype(jnp.bfloat16)
    low = (x - high.astype(jnp.float32)).astype(jnp.bfloat16)
    return high, low


def product(left, right):
    return jnp.dot(left, right, preferred_element_type=jnp.float32)


def product_nt(left, right):
    return lax.dot_general(left, right, (((1,), (1,)), ((), ())), preferred_element_type=jnp.float32)


def wide(row, width):
    n = row.shape[1]
    if width <= n:
        return row[:, :width]
    return jnp.concatenate([row] * (width // n), axis=1)


def pack_kernel(
    trunk_ref, loadings_ref, parents_ref, base_ref, z_ref, out_ref, trunk, loads, owners, rows_ref, meta_ref, sems
):
    n = loadings_ref.shape[0]
    copies = [
        pltpu.make_async_copy(loadings_ref, loads, sems.at[0]),
        pltpu.make_async_copy(parents_ref, owners, sems.at[1]),
        pltpu.make_async_copy(base_ref, rows_ref.at[0], sems.at[2]),
        pltpu.make_async_copy(z_ref, rows_ref.at[1], sems.at[3]),
        pltpu.make_async_copy(trunk_ref, trunk, sems.at[4]),
    ]
    for copy in copies:
        copy.start()
    for copy in copies[1:]:
        copy.wait()
    pair_ids = lax.broadcasted_iota(jnp.int32, (2, n), 0)
    trunk_rows = jnp.where(pair_ids == 0, trunk[0], trunk[1])
    for index, rows in enumerate((rows_ref[0], rows_ref[1], trunk_rows)):
        high = rows.astype(jnp.bfloat16).astype(jnp.float32)
        middle = (rows - high).astype(jnp.bfloat16).astype(jnp.float32)
        meta_ref[2 * index : 2 * index + 2, 0:n] = high
        meta_ref[2 * index : 2 * index + 2, n : 2 * n] = middle
        meta_ref[8 + 2 * index : 10 + 2 * index, 0:n] = rows - high - middle
    meta_ref[6:8, 0:n] = jnp.broadcast_to(owners[...].astype(jnp.float32), (2, n))
    meta_ref[6:8, n : 2 * n] = jnp.zeros((2, n), jnp.float32)
    meta_ref[14:16, 0:n] = jnp.zeros((2, n), jnp.float32)
    meta_ref[8:16, n : 2 * n] = jnp.zeros((8, n), jnp.float32)
    meta = meta_ref[...].astype(jnp.bfloat16)
    copies[0].wait()
    out_ref[0:n, :] = loads[...]
    out_ref[n : n + EXTRA, :] = meta


def constants(section_ref, n):
    meta = section_ref[n : n + EXTRA, :].astype(jnp.float32)
    high, middle = meta[0:8, 0:n], meta[0:8, n : 2 * n]
    return high, middle, high + middle + meta[8:16, 0:n]


def matrix_steps(sections, n):
    highs, middles, rows = zip(*(constants(section, n) for section in sections))
    row_ids = lax.broadcasted_iota(jnp.int32, (n, n), 0)
    lane_ids = lax.broadcasted_iota(jnp.int32, (n, n), 1)
    section_ids = lax.broadcasted_iota(jnp.int32, (max(8, len(sections)), n), 0)
    stacked = jnp.full(section_ids.shape, -1, jnp.int32)
    for index, row in enumerate(rows):
        stacked = jnp.where(section_ids == index, row[6:7].astype(jnp.int32), stacked)
    known = {1: stacked}

    def ancestor(distance):
        if distance not in known:
            step = 1 << (distance.bit_length() - 1)
            if step == distance:
                step //= 2
            far, near = ancestor(step), ancestor(distance - step)
            known[distance] = jnp.where(near < 0, -1, jnp.take_along_axis(far, jnp.maximum(near, 0), axis=1))
        return known[distance]

    digits = []
    unit = 1
    while unit < n:
        digits.append([ancestor(unit * digit).astype(jnp.float32) for digit in range(1, 8) if unit * digit < n])
        unit *= 8
    last = [found.T for found in digits.pop()]
    rows_b, lanes_b = (ids.astype(jnp.float32).astype(jnp.bfloat16) for ids in (row_ids, lane_ids))
    one, zero = jnp.ones((n, n), jnp.bfloat16), jnp.zeros((n, n), jnp.bfloat16)
    identity = jnp.where(rows_b == lanes_b, one, zero)
    pad_ids = lax.broadcasted_iota(jnp.int32, (EXTRA, 2 * n), 0)
    state = [None] * len(sections)

    def near_step(index):
        done = None
        for digit in digits:
            factor = identity
            for found in digit:
                row = jnp.broadcast_to(found[index : index + 1, :].astype(jnp.bfloat16), (n, n))
                factor = jnp.where(rows_b == row, one, factor)
            done = factor if done is None else product(done, factor).astype(jnp.bfloat16)
        state[index] = done

    def paths_step(index):
        factor = identity
        for found in last:
            column = jnp.broadcast_to(found[:, index : index + 1], (n, n)).astype(jnp.bfloat16)
            factor = jnp.where(lanes_b == column, one, factor)
        state[index] = product_nt(factor, state[index]).astype(jnp.bfloat16)

    def shared_step(index):
        path = state[index]
        wide_path = path.astype(jnp.float32)
        left = [
            jnp.concatenate([wide_path * part[row : row + 1] for part in (highs[index], middles[index])], axis=1)
            for row in (2, 3)
        ]
        left = jnp.concatenate(left, axis=0).astype(jnp.bfloat16)
        state[index] = product_nt(left, jnp.concatenate([path, path], axis=1))

    def matrix_step(index):
        resist, react = state[index][:n], state[index][n:]
        base_active, base_reactive = rows[index][0:1], rows[index][1:2]
        real_high, real_low = split(resist * base_active + react * base_reactive)
        imag_high, imag_low = split(react * base_active - resist * base_reactive)
        row_real = jnp.concatenate([base_active, base_reactive], axis=1)
        row_imag = jnp.concatenate([-base_reactive, base_active], axis=1)
        sums_high, sums_low = split(jnp.where(pad_ids == 0, row_real, jnp.where(pad_ids == 1, row_imag, 0.0)))

        def whole(real_part, imag_part, sums_part):
            top = jnp.concatenate([real_part, -imag_part], axis=1)
            bottom = jnp.concatenate([imag_part, real_part], axis=1)
            return jnp.concatenate([top, bottom, sums_part], axis=0)

        high, low = whole(real_high, imag_high, sums_high), whole(real_low, imag_low, sums_low)
        state[index] = jnp.concatenate([high, low], axis=1)
        return state[index]

    return [near_step, paths_step, shared_step, matrix_step]


def stagger(count, steps, between=None):
    for turn in range(count + len(steps) - 1):
        for depth in reversed(range(len(steps))):
            if 0 <= turn - depth < count:
                steps[depth](turn - depth)
        if between is not None:
            between()


def swing_of(loadings, factors):
    level = product_nt(loadings, factors).astype(jnp.bfloat16).astype(jnp.float32)
    return 1.0 + 0.5 * jnp.tanh(level)


def apply(matrix, u):
    span = matrix.shape[1] // 2
    high, low = split(u)
    left = jnp.concatenate([matrix, matrix[:, :span]], axis=1)
    return product(left, jnp.concatenate([high, high, low], axis=0))


def apply_first(matrix, swing):
    n = matrix.shape[1] // 4
    high, low = split(swing)
    high_part, low_part = matrix[:, :n], matrix[:, 2 * n : 3 * n]
    return product(
        jnp.concatenate([high_part, low_part, high_part], axis=1), jnp.concatenate([high, high, low], axis=0)
    )


def inverse_of(swing, real, imag):
    return swing * pltpu.reciprocal(real * real + imag * imag, approx=True)


def scaled_volts(swing, real, imag):
    inverse = inverse_of(swing, real, imag)
    return jnp.concatenate([real * inverse, imag * inverse], axis=0)


def early_kernel(pieces, place_ref, *refs):
    piece_refs, sections = refs[:pieces], refs[pieces:-9]
    factors_ref, own_ref, kept_ref, matrix_ref, swing_ref, drop_ref, inject_ref, sem, keep_sems = refs[-9:]
    width = factors_ref.shape[0]
    piece, offset = place_ref[0], place_ref[1]
    keeps = [
        pltpu.make_async_copy(piece_ref, kept_ref.at[index], keep_sems.at[index])
        for index, piece_ref in enumerate(piece_refs[1:])
    ]
    for copy in keeps:
        copy.start()
    for index, piece_ref in enumerate(piece_refs):
        @pl.when(piece == index)
        def _(piece_ref=piece_ref):
            rows = piece_ref.at[pl.ds(pl.multiple_of(offset, width), width), :]
            pltpu.make_async_copy(rows, factors_ref, sem).start()

    n = swing_ref.shape[1]
    for start in range(0, len(sections), 8):
        group = sections[start : start + 8]
        near_step, *more, matrix_step = matrix_steps(group, n)
        if start == 0:
            pltpu.make_async_copy(piece_refs[0].at[0:width, :], factors_ref, sem).wait()

        def start_step(index):
            near_step(index)
            swing_ref[start + index] = swing_of(group[index][0:n, :], factors_ref[...])

        def keep_step(index):
            matrix_ref[start + index] = matrix_step(index)

        def sweep_step(index):
            out = apply_first(matrix_ref[start + index], swing_ref[start + index])
            drop_ref[start + index] = out[: 2 * n]
            inject_ref[start + index] = out[2 * n :]

        stagger(len(group), [start_step, *more, keep_step, sweep_step])
    own_ref[...] = matrix_ref[0]
    for copy in keeps:
        copy.wait()


def heads_kernel(slots, early, place_ref, factors_ref, *refs):
    feeders = len(slots)
    sections = refs[:feeders]
    early_refs = refs[feeders : feeders + 4]
    head_ref, matrix_ref, swing_ref, drop_ref, again_ref, flow_ref, trunk_ref = refs[feeders + 4 :]
    width = factors_ref.shape[0]
    n = swing_ref.shape[1]
    place = [jnp.bitwise_xor(place_ref[2], slot) for slot in slots]
    late_refs = (matrix_ref, swing_ref, drop_ref)

    def of(index, which):
        return early_refs[which].at[index] if index < early else late_refs[which].at[index - early]

    def flow_of(index, real, imag):
        base = constants(sections[index], n)[2].T
        active, reactive = base[:, 0:1], base[:, 1:2]
        if imag is None:
            parts = (active * real, -reactive * real)
        else:
            parts = (active * real + reactive * imag, active * imag - reactive * real)
        return [jnp.sum(part, axis=0, keepdims=True) for part in parts]

    groups = [list(range(start, min(start + 8, feeders))) for start in range(early, feeders, 8)]
    steps = [matrix_steps([sections[index] for index in group], n) for group in groups]
    for index in range(feeders):
        row = constants(sections[index], n)[2]
        trunk_ref[place[index], 0:2, :] = wide(row[4:6], width)
        if index < early:
            flow_ref[place[index]] = of(index, 3)[0:8, :]
        else:
            swing = swing_of(sections[index][0:n, :], factors_ref[...])
            of(index, 1)[...] = swing
            for part, total in enumerate(flow_of(index, swing, None)):
                flow_ref[place[index], part : part + 1, :] = total

    def heads(sweep):
        flows = [None] * feeders
        real = jnp.zeros((1, width), jnp.float32)
        imag = real
        for g in reversed(range(feeders)):
            real = real + flow_ref[g, 0:1, :]
            imag = imag + flow_ref[g, 1:2, :]
            flows[g] = (real, imag)
        head_real = jnp.ones((1, width), jnp.float32)
        head_imag = jnp.zeros((1, width), jnp.float32)
        for g in range(feeders):
            r, x = trunk_ref[g, 0:1, :], trunk_ref[g, 1:2, :]
            real, imag = flows[g]
            head_real = head_real - (r * real - x * imag)
            head_imag = head_imag - (r * imag + x * real)
            head_ref[g, 2 * sweep : 2 * sweep + 1, :] = head_real
            head_ref[g, 2 * sweep + 1 : 2 * sweep + 2, :] = head_imag

    def volts(index, sweep):
        drop = of(index, 2) if sweep == 1 else again_ref.at[index]
        real = head_ref[place[index], 2 * sweep - 2 : 2 * sweep - 1, :] - drop[0:n, :]
        imag = head_ref[place[index], 2 * sweep - 1 : 2 * sweep, :] - drop[n : 2 * n, :]
        return real, imag

    def middle(index, sweep):
        out = apply(of(index, 0)[...], scaled_volts(of(index, 1)[...], *volts(index, sweep)))
        again_ref[index] = out[: 2 * n]
        flow_ref[place[index]] = out[2 * n : 2 * n + 8]

    heads(0)
    ready = list(range(early))

    def between():
        if ready:
            middle(ready.pop(0), 1)

    for group, (*more, matrix_step) in zip(groups, steps):
        def keep_step(index):
            of(group[index], 0)[...] = matrix_step(index)

        def sweep_step(index):
            out = apply_first(of(group[index], 0)[...], of(group[index], 1)[...])
            of(group[index], 2)[...] = out[: 2 * n]

        stagger(len(group), [*more, keep_step, sweep_step], between)
    for index in ready + list(range(early, feeders)):
        middle(index, 1)
    heads(1)
    for sweep in range(2, SWEEPS):
        for index in range(feeders):
            if sweep < SWEEPS - 1:
                middle(index, sweep)
            else:
                real, imag = volts(index, sweep)
                inverse = inverse_of(of(index, 1)[...], real, imag)
                for part, total in enumerate(flow_of(index, real * inverse, imag * inverse)):
                    flow_ref[place[index], part : part + 1, :] = total
        heads(sweep)
    for g in range(feeders):
        head_ref[g, 2 * SWEEPS :, :] = jnp.zeros((head_ref.shape[1] - 2 * SWEEPS, width), jnp.float32)


def first_kernel(
    node_ref, matrix_ref, loadings_ref, rows_ref, kept_ref, swing_ref, drop_ref, loads, factors_ref, sems
):
    n = loadings_ref.shape[0]
    width = swing_ref.shape[2]
    pieces = 1 + kept_ref.shape[0]
    chunks = rows_ref.shape[0] // width
    copies = [pltpu.make_async_copy(loadings_ref, loads, sems.at[pieces])]
    for index in range(pieces):
        piece_ref = kept_ref.at[index - 1] if index else rows_ref
        copies.append(pltpu.make_async_copy(piece_ref, factors_ref.at[index], sems.at[index]))
    for copy in copies:
        copy.start()
    matrix = matrix_ref[0 : 2 * n, :]
    for copy in copies:
        copy.wait()
    loadings = loads[...]
    together = 4 // chunks if chunks < 4 else 1

    @pl.loop(0, pieces // together)
    def _(outer):
        for inner in range(together):
            index = outer * together + inner
            for part in range(chunks):
                chunk = jnp.bitwise_xor(node_ref[0], index) * chunks + part
                swing = swing_of(loadings, factors_ref[index, part * width : (part + 1) * width, :])
                swing_ref[chunk] = swing
                drop_ref[chunk] = apply_first(matrix, swing)


def volts_kernel(matrix_ref, swing_ref, drop_ref, head_ref, real_ref, imag_ref, out_ref, sems):
    n = swing_ref.shape[1]
    chunks, width = swing_ref.shape[0], swing_ref.shape[2]
    matrix = matrix_ref[0 : 2 * n, :]
    drops = [None] * chunks
    copies = []

    def advance(chunk, sweep):
        drop = drop_ref[chunk] if sweep == 0 else drops[chunk]
        real = head_ref[chunk, 2 * sweep : 2 * sweep + 1, :] - drop[:n]
        imag = head_ref[chunk, 2 * sweep + 1 : 2 * sweep + 2, :] - drop[n:]
        if sweep < SWEEPS - 1:
            drops[chunk] = apply(matrix, scaled_volts(swing_ref[chunk], real, imag))
            return
        rows = slice(chunk * width, (chunk + 1) * width)
        for index, (part, to_ref) in enumerate(((real, real_ref), (imag, imag_ref))):
            out_ref[index, rows, :] = part.T
            copies.append(pltpu.make_async_copy(out_ref.at[index, rows, :], to_ref.at[rows, :], sems.at[index, chunk]))
            copies[-1].start()

    stagger(chunks, [functools.partial(advance, sweep=sweep) for sweep in range(SWEEPS)])
    for copy in copies:
        copy.wait()


def after_kernel(*refs):
    del refs


def after(array, *others):
    return pl.pallas_call(
        after_kernel,
        out_shape=jax.ShapeDtypeStruct(array.shape, array.dtype),
        in_specs=[ANY] * (1 + len(others)),
        out_specs=ANY,
        input_output_aliases={0: 0},
        compiler_params=limit(0),
        name="after",
    )(array, *others)


def in_hbm(*arrays):
    return [pltpu.with_memory_space_constraint(array, pltpu.HBM) for array in arrays]


def limit(nbytes):
    return pltpu.CompilerParams(vmem_limit_bytes=min(60 << 20, int(nbytes) + (16 << 20)))


def local(feeders, nodes, factors, loadings, parents, load_base, lateral_z, trunk_z):
    node = lax.axis_index("node").astype(jnp.int32)
    feeder = lax.axis_index("feeder").astype(jnp.int32)
    rows, rank = factors.shape
    scen = rows * nodes
    n = loadings.shape[0]
    width = max(scen // feeders, LANES)
    share = feeders * width // scen
    f32, bf16 = jnp.float32, jnp.bfloat16
    matrix_shape = (2 * n + EXTRA, 4 * n)

    def trade(block, offset):
        return lax.ppermute(block, "node", [(i, i ^ offset) for i in range(nodes)])

    held = {0: factors}
    far = nodes // 2
    if far:
        held[far] = trade(factors, far)

    packed = pl.pallas_call(
        pack_kernel,
        out_shape=jax.ShapeDtypeStruct((n + EXTRA, rank), bf16),
        in_specs=[HBM] * 5,
        out_specs=VMEM,
        scratch_shapes=[
            pltpu.SMEM((2,), f32),
            pltpu.VMEM((n, rank), bf16),
            pltpu.VMEM((1, n), jnp.int32),
            pltpu.VMEM((2, 2, n), f32),
            pltpu.VMEM((EXTRA, rank), f32),
            pltpu.SemaphoreType.DMA((5,)),
        ],
        compiler_params=limit(2 * (n + EXTRA) * rank * 2),
        name="pack",
    )(*in_hbm(trunk_z.reshape(2), loadings, parents.reshape(1, n), load_base, lateral_z))

    def swap(block, offset):
        return lax.ppermute(block, "feeder", [(i, i ^ offset) for i in range(feeders)])

    every = {0: packed}
    for offset in sorted(range(2, feeders, 2), key=lambda o: -(o & -o)):
        every[offset] = swap(packed, offset)
    every[1] = swap(packed, 1)
    slots = list(every)
    early = len(slots)
    for offset in slots[1:-1]:
        every[offset + 1] = swap(every[offset], 1)
    slots = list(every)

    if far:
        held[far] = after(held[far], *(every[slot] for slot in slots[:early]))
    step = far // 2
    while step >= 1:
        for offset in list(held):
            held[offset ^ step] = trade(held[offset], step)
        step //= 2
    pieces = [held[offset] for offset in range(nodes)]

    start = (feeder // share) * width
    place = jnp.stack([(start // rows) ^ node, start % rows, feeder])

    def states(count):
        return [
            ((count, *matrix_shape), bf16),
            ((count, n, width), f32),
            ((count, 2 * n, width), f32),
            ((count, EXTRA, width), f32),
        ]

    state_bytes = (2 * n + EXTRA) * 8 * n + (3 * n + EXTRA) * width * 4 + (n + EXTRA) * rank * 2
    block, own, kept, *started = pl.pallas_call(
        functools.partial(early_kernel, nodes),
        out_shape=[
            jax.ShapeDtypeStruct((width, rank), bf16),
            jax.ShapeDtypeStruct(matrix_shape, bf16),
            pltpu.HBM((nodes - 1, rows, rank), bf16),
        ]
        + [jax.ShapeDtypeStruct(*state) for state in states(early)],
        in_specs=[SMEM, HBM] + [ANY] * (nodes - 1) + [VMEM] * early,
        out_specs=[VMEM, VMEM, HBM] + [VMEM] * 4,
        scratch_shapes=[pltpu.SemaphoreType.DMA, pltpu.SemaphoreType.DMA((nodes - 1,))],
        compiler_params=limit(early * state_bytes),
        cost_estimate=pl.CostEstimate(flops=early * (1 << 29), bytes_accessed=early * state_bytes, transcendentals=early * n * width),
        name="early",
    )(place, *in_hbm(pieces[0]), *pieces[1:], *(every[slot] for slot in slots[:early]))
    heads = pl.pallas_call(
        functools.partial(heads_kernel, slots, early),
        out_shape=jax.ShapeDtypeStruct((feeders, 8, width), f32),
        in_specs=[SMEM] + [VMEM] * (1 + feeders + 4),
        out_specs=VMEM,
        scratch_shapes=[pltpu.VMEM(*state) for state in states(max(feeders - early, 1))[:3]]
        + [
            pltpu.VMEM((feeders, 2 * n, width), f32),
            pltpu.VMEM((feeders, 8, width), f32),
            pltpu.VMEM((feeders, 8, width), f32),
        ],
        compiler_params=limit((feeders - early) * state_bytes + feeders * (2 * n + 16) * width * 4),
        name="heads",
    )(place, block, *(every[slot] for slot in slots), *started)
    given = lax.all_to_all(heads, "feeder", 0, 0, tiled=True)
    given = given[::share]

    chunks = scen // width
    swing, drop = pl.pallas_call(
        first_kernel,
        out_shape=(
            jax.ShapeDtypeStruct((chunks, n, width), f32),
            jax.ShapeDtypeStruct((chunks, 2 * n, width), f32),
        ),
        in_specs=[SMEM, VMEM, HBM, HBM, HBM],
        out_specs=(VMEM, VMEM),
        scratch_shapes=[
            pltpu.VMEM((n, rank), bf16),
            pltpu.VMEM((nodes, rows, rank), bf16),
            pltpu.SemaphoreType.DMA((nodes + 1,)),
        ],
        compiler_params=limit(3 * n * scen * 4 + scen * rank * 2),
        cost_estimate=pl.CostEstimate(flops=2 * scen * n * rank * 4, bytes_accessed=3 * n * scen * 4, transcendentals=scen * n),
        name="first",
    )(node.reshape(1), own, *in_hbm(loadings, factors, kept))
    return pl.pallas_call(
        volts_kernel,
        out_shape=(
            jax.ShapeDtypeStruct((scen, n), f32),
            jax.ShapeDtypeStruct((scen, n), f32),
        ),
        in_specs=[VMEM] * 4,
        out_specs=(HBM, HBM),
        scratch_shapes=[pltpu.VMEM((2, scen, n), f32), pltpu.SemaphoreType.DMA((2, chunks))],
        compiler_params=limit(5 * n * scen * 4),
        name="volts",
    )(own, swing, drop, given)


def solution(mesh):
    feeders = mesh.shape["feeder"]
    nodes = mesh.shape["node"]
    return jax.shard_map(
        functools.partial(local, feeders, nodes),
        mesh=mesh,
        in_specs=(
            P("node", None),
            P(("feeder", "node"), None),
            P(("feeder", "node")),
            P(None, ("feeder", "node")),
            P(None, ("feeder", "node")),
            P(None, "feeder", "node"),
        ),
        out_specs=(P(None, ("feeder", "node")), P(None, ("feeder", "node"))),
        check_vma=False,
    )
```

```python
import functools

import jax
import jax.numpy as jnp
from jax import lax
from jax.experimental import pallas as pl
from jax.experimental.pallas import tpu as pltpu
from jax.sharding import PartitionSpec as P

SWEEPS = 3
EXTRA = 16
LANES = 128

VMEM = pl.BlockSpec(memory_space=pltpu.VMEM)
SMEM = pl.BlockSpec(memory_space=pltpu.SMEM)
HBM = pl.BlockSpec(memory_space=pltpu.HBM)
ANY = pl.BlockSpec(memory_space=pl.ANY)


def split(x):
    high = x.astype(jnp.bfloat16)
    low = (x - high.astype(jnp.float32)).astype(jnp.bfloat16)
    return high, low


def product(left, right):
    return jnp.dot(left, right, preferred_element_type=jnp.float32)


def product_nt(left, right):
    return lax.dot_general(left, right, (((1,), (1,)), ((), ())), preferred_element_type=jnp.float32)


def wide(row, width):
    n = row.shape[1]
    if width <= n:
        return row[:, :width]
    return jnp.concatenate([row] * (width // n), axis=1)


def pack_kernel(
    trunk_ref, loadings_ref, parents_ref, base_ref, z_ref, out_ref, trunk, loads, owners, rows_ref, meta_ref, sems
):
    n = loadings_ref.shape[0]
    copies = [
        pltpu.make_async_copy(loadings_ref, loads, sems.at[0]),
        pltpu.make_async_copy(parents_ref, owners, sems.at[1]),
        pltpu.make_async_copy(base_ref, rows_ref.at[0], sems.at[2]),
        pltpu.make_async_copy(z_ref, rows_ref.at[1], sems.at[3]),
        pltpu.make_async_copy(trunk_ref, trunk, sems.at[4]),
    ]
    for copy in copies:
        copy.start()
    for copy in copies[1:]:
        copy.wait()
    pair_ids = lax.broadcasted_iota(jnp.int32, (2, n), 0)
    trunk_rows = jnp.where(pair_ids == 0, trunk[0], trunk[1])
    for index, rows in enumerate((rows_ref[0], rows_ref[1], trunk_rows)):
        high = rows.astype(jnp.bfloat16).astype(jnp.float32)
        middle = (rows - high).astype(jnp.bfloat16).astype(jnp.float32)
        meta_ref[2 * index : 2 * index + 2, 0:n] = high
        meta_ref[2 * index : 2 * index + 2, n : 2 * n] = middle
        meta_ref[8 + 2 * index : 10 + 2 * index, 0:n] = rows - high - middle
    meta_ref[6:8, 0:n] = jnp.broadcast_to(owners[...].astype(jnp.float32), (2, n))
    meta_ref[6:8, n : 2 * n] = jnp.zeros((2, n), jnp.float32)
    meta_ref[14:16, 0:n] = jnp.zeros((2, n), jnp.float32)
    meta_ref[8:16, n : 2 * n] = jnp.zeros((8, n), jnp.float32)
    meta = meta_ref[...].astype(jnp.bfloat16)
    copies[0].wait()
    out_ref[0:n, :] = loads[...]
    out_ref[n : n + EXTRA, :] = meta


def constants(section_ref, n):
    meta = section_ref[n : n + EXTRA, :].astype(jnp.float32)
    high, middle = meta[0:8, 0:n], meta[0:8, n : 2 * n]
    return high, middle, high + middle + meta[8:16, 0:n]


def matrix_steps(sections, n):
    highs, middles, rows = zip(*(constants(section, n) for section in sections))
    row_ids = lax.broadcasted_iota(jnp.int32, (n, n), 0)
    lane_ids = lax.broadcasted_iota(jnp.int32, (n, n), 1)
    section_ids = lax.broadcasted_iota(jnp.int32, (max(8, len(sections)), n), 0)
    stacked = jnp.full(section_ids.shape, -1, jnp.int32)
    for index, row in enumerate(rows):
        stacked = jnp.where(section_ids == index, row[6:7].astype(jnp.int32), stacked)
    known = {1: stacked}

    def ancestor(distance):
        if distance not in known:
            step = 1 << (distance.bit_length() - 1)
            if step == distance:
                step //= 2
            far, near = ancestor(step), ancestor(distance - step)
            known[distance] = jnp.where(near < 0, -1, jnp.take_along_axis(far, jnp.maximum(near, 0), axis=1))
        return known[distance]

    digits = []
    unit = 1
    while unit < n:
        digits.append([ancestor(unit * digit).astype(jnp.float32) for digit in range(1, 8) if unit * digit < n])
        unit *= 8
    last = [found.T for found in digits.pop()]
    yield None

    rows_b, lanes_b = (ids.astype(jnp.float32).astype(jnp.bfloat16) for ids in (row_ids, lane_ids))
    one, zero = jnp.ones((n, n), jnp.bfloat16), jnp.zeros((n, n), jnp.bfloat16)
    identity = jnp.where(rows_b == lanes_b, one, zero)
    products = [None] * len(sections)
    for index in range(len(sections)):
        for digit in digits:
            factor = identity
            for found in digit:
                row = jnp.broadcast_to(found[index : index + 1, :].astype(jnp.bfloat16), (n, n))
                factor = jnp.where(rows_b == row, one, factor)
            done = products[index]
            products[index] = factor if done is None else product(done, factor).astype(jnp.bfloat16)
    yield None

    paths = []
    for index in range(len(sections)):
        factor = identity
        for found in last:
            column = jnp.broadcast_to(found[:, index : index + 1], (n, n)).astype(jnp.bfloat16)
            factor = jnp.where(lanes_b == column, one, factor)
        paths.append(product_nt(factor, products[index]).astype(jnp.bfloat16))
    yield None

    shared = []
    for path, high, middle in zip(paths, highs, middles):
        wide_path = path.astype(jnp.float32)

        def scaled(index):
            return jnp.concatenate([wide_path * high[index : index + 1], wide_path * middle[index : index + 1]], axis=1)

        left = jnp.concatenate([scaled(2), scaled(3)], axis=0).astype(jnp.bfloat16)
        shared.append(product_nt(left, jnp.concatenate([path, path], axis=1)))
    yield None

    pad_ids = lax.broadcasted_iota(jnp.int32, (EXTRA, 2 * n), 0)
    out = []
    for both, row in zip(shared, rows):
        resist, react = both[:n], both[n:]
        base_active, base_reactive = row[0:1], row[1:2]
        real_high, real_low = split(resist * base_active + react * base_reactive)
        imag_high, imag_low = split(react * base_active - resist * base_reactive)
        row_real = jnp.concatenate([base_active, base_reactive], axis=1)
        row_imag = jnp.concatenate([-base_reactive, base_active], axis=1)
        sums_high, sums_low = split(jnp.where(pad_ids == 0, row_real, jnp.where(pad_ids == 1, row_imag, 0.0)))

        def whole(real_part, imag_part, sums_part):
            top = jnp.concatenate([real_part, -imag_part], axis=1)
            bottom = jnp.concatenate([imag_part, real_part], axis=1)
            return jnp.concatenate([top, bottom, sums_part], axis=0)

        out.append(
            jnp.concatenate(
                [whole(real_high, imag_high, sums_high), whole(real_low, imag_low, sums_low)], axis=1
            )
        )
    yield out


def swing_of(loadings, factors):
    level = product_nt(loadings, factors).astype(jnp.bfloat16).astype(jnp.float32)
    return 1.0 + 0.5 * jnp.tanh(level)


def apply(matrix, u):
    span = matrix.shape[1] // 2
    high, low = split(u)
    left = jnp.concatenate([matrix, matrix[:, :span]], axis=1)
    return product(left, jnp.concatenate([high, high, low], axis=0))


def apply_first(matrix, swing):
    n = matrix.shape[1] // 4
    high, low = split(swing)
    high_part, low_part = matrix[:, :n], matrix[:, 2 * n : 3 * n]
    return product(
        jnp.concatenate([high_part, low_part, high_part], axis=1), jnp.concatenate([high, high, low], axis=0)
    )


def inverse_of(swing, real, imag):
    return swing * pltpu.reciprocal(real * real + imag * imag, approx=True)


def scaled_volts(swing, real, imag):
    inverse = inverse_of(swing, real, imag)
    return jnp.concatenate([real * inverse, imag * inverse], axis=0)


def early_kernel(pieces, place_ref, *refs):
    piece_refs, sections = refs[:pieces], refs[pieces:-9]
    factors_ref, own_ref, kept_ref, matrix_ref, swing_ref, drop_ref, inject_ref, sem, keep_sems = refs[-9:]
    width = factors_ref.shape[0]
    piece, offset = place_ref[0], place_ref[1]
    keeps = [
        pltpu.make_async_copy(piece_ref, kept_ref.at[index], keep_sems.at[index])
        for index, piece_ref in enumerate(piece_refs[1:])
    ]
    for copy in keeps:
        copy.start()
    for index, piece_ref in enumerate(piece_refs):
        @pl.when(piece == index)
        def _(piece_ref=piece_ref):
            rows = piece_ref.at[pl.ds(pl.multiple_of(offset, width), width), :]
            pltpu.make_async_copy(rows, factors_ref, sem).start()

    n = swing_ref.shape[1]
    for start in range(0, len(sections), 8):
        group = list(enumerate(sections))[start : start + 8]
        steps = matrix_steps([section for _, section in group], n)
        next(steps)
        if start == 0:
            pltpu.make_async_copy(piece_refs[0].at[0:width, :], factors_ref, sem).wait()
        for slot, section in group:
            swing_ref[slot] = swing_of(section[0:n, :], factors_ref[...])
        *_, matrices = steps
        for (slot, _), matrix in zip(group, matrices):
            matrix_ref[slot] = matrix
            out = apply_first(matrix_ref[slot], swing_ref[slot])
            drop_ref[slot] = out[: 2 * n]
            inject_ref[slot] = out[2 * n :]
    own_ref[...] = matrix_ref[0]
    for copy in keeps:
        copy.wait()


def heads_kernel(slots, early, place_ref, factors_ref, *refs):
    feeders = len(slots)
    sections = refs[:feeders]
    early_refs = refs[feeders : feeders + 4]
    head_ref, matrix_ref, swing_ref, drop_ref, again_ref, flow_ref, trunk_ref = refs[feeders + 4 :]
    width = factors_ref.shape[0]
    n = swing_ref.shape[1]
    place = [jnp.bitwise_xor(place_ref[2], slot) for slot in slots]
    late_refs = (matrix_ref, swing_ref, drop_ref)

    def of(index, which):
        return early_refs[which].at[index] if index < early else late_refs[which].at[index - early]

    def flow_of(index, real, imag):
        base = constants(sections[index], n)[2].T
        active, reactive = base[:, 0:1], base[:, 1:2]
        if imag is None:
            parts = (active * real, -reactive * real)
        else:
            parts = (active * real + reactive * imag, active * imag - reactive * real)
        return [jnp.sum(part, axis=0, keepdims=True) for part in parts]

    groups = [list(range(start, min(start + 8, feeders))) for start in range(early, feeders, 8)]
    steps = [matrix_steps([sections[index] for index in group], n) for group in groups]
    if steps:
        next(steps[0])
    for index in range(feeders):
        row = constants(sections[index], n)[2]
        trunk_ref[place[index], 0:2, :] = wide(row[4:6], width)
        if index < early:
            flow_ref[place[index]] = of(index, 3)[0:8, :]
        else:
            swing = swing_of(sections[index][0:n, :], factors_ref[...])
            of(index, 1)[...] = swing
            for part, total in enumerate(flow_of(index, swing, None)):
                flow_ref[place[index], part : part + 1, :] = total

    def heads(sweep):
        flows = [None] * feeders
        real = jnp.zeros((1, width), jnp.float32)
        imag = real
        for g in reversed(range(feeders)):
            real = real + flow_ref[g, 0:1, :]
            imag = imag + flow_ref[g, 1:2, :]
            flows[g] = (real, imag)
        head_real = jnp.ones((1, width), jnp.float32)
        head_imag = jnp.zeros((1, width), jnp.float32)
        for g in range(feeders):
            r, x = trunk_ref[g, 0:1, :], trunk_ref[g, 1:2, :]
            real, imag = flows[g]
            head_real = head_real - (r * real - x * imag)
            head_imag = head_imag - (r * imag + x * real)
            head_ref[g, 2 * sweep : 2 * sweep + 1, :] = head_real
            head_ref[g, 2 * sweep + 1 : 2 * sweep + 2, :] = head_imag

    def volts(index, sweep):
        drop = of(index, 2) if sweep == 1 else again_ref.at[index]
        real = head_ref[place[index], 2 * sweep - 2 : 2 * sweep - 1, :] - drop[0:n, :]
        imag = head_ref[place[index], 2 * sweep - 1 : 2 * sweep, :] - drop[n : 2 * n, :]
        return real, imag

    def middle(index, sweep):
        out = apply(of(index, 0)[...], scaled_volts(of(index, 1)[...], *volts(index, sweep)))
        again_ref[index] = out[: 2 * n]
        flow_ref[place[index]] = out[2 * n : 2 * n + 8]

    heads(0)
    ready = list(range(early))
    for group, step in zip(groups, steps):
        for matrices in step:
            if ready:
                middle(ready.pop(0), 1)
        for index, matrix in zip(group, matrices):
            of(index, 0)[...] = matrix
            of(index, 2)[...] = apply_first(matrix, of(index, 1)[...])[: 2 * n]
    for index in ready + list(range(early, feeders)):
        middle(index, 1)
    heads(1)
    for sweep in range(2, SWEEPS):
        for index in range(feeders):
            if sweep < SWEEPS - 1:
                middle(index, sweep)
            else:
                real, imag = volts(index, sweep)
                inverse = inverse_of(of(index, 1)[...], real, imag)
                for part, total in enumerate(flow_of(index, real * inverse, imag * inverse)):
                    flow_ref[place[index], part : part + 1, :] = total
        heads(sweep)
    for g in range(feeders):
        head_ref[g, 2 * SWEEPS :, :] = jnp.zeros((head_ref.shape[1] - 2 * SWEEPS, width), jnp.float32)


def first_kernel(
    node_ref, matrix_ref, loadings_ref, rows_ref, kept_ref, swing_ref, drop_ref, loads, factors_ref, sems
):
    n = loadings_ref.shape[0]
    width = swing_ref.shape[2]
    pieces = 1 + kept_ref.shape[0]
    chunks = rows_ref.shape[0] // width
    copies = [pltpu.make_async_copy(loadings_ref, loads, sems.at[pieces])]
    for index in range(pieces):
        piece_ref = kept_ref.at[index - 1] if index else rows_ref
        copies.append(pltpu.make_async_copy(piece_ref, factors_ref.at[index], sems.at[index]))
    for copy in copies:
        copy.start()
    matrix = matrix_ref[0 : 2 * n, :]
    for copy in copies:
        copy.wait()
    loadings = loads[...]
    together = 4 // chunks if chunks < 4 else 1

    @pl.loop(0, pieces // together)
    def _(outer):
        for inner in range(together):
            index = outer * together + inner
            for part in range(chunks):
                chunk = jnp.bitwise_xor(node_ref[0], index) * chunks + part
                swing = swing_of(loadings, factors_ref[index, part * width : (part + 1) * width, :])
                swing_ref[chunk] = swing
                drop_ref[chunk] = apply_first(matrix, swing)


def volts_kernel(matrix_ref, swing_ref, drop_ref, head_ref, real_ref, imag_ref, out_ref, sems):
    n = swing_ref.shape[1]
    chunks, width = swing_ref.shape[0], swing_ref.shape[2]
    matrix = matrix_ref[0 : 2 * n, :]
    drops = [None] * chunks
    copies = []

    def advance(chunk, sweep):
        drop = drop_ref[chunk] if sweep == 0 else drops[chunk]
        real = head_ref[chunk, 2 * sweep : 2 * sweep + 1, :] - drop[:n]
        imag = head_ref[chunk, 2 * sweep + 1 : 2 * sweep + 2, :] - drop[n:]
        if sweep < SWEEPS - 1:
            drops[chunk] = apply(matrix, scaled_volts(swing_ref[chunk], real, imag))
            return
        rows = slice(chunk * width, (chunk + 1) * width)
        for index, (part, to_ref) in enumerate(((real, real_ref), (imag, imag_ref))):
            out_ref[index, rows, :] = part.T
            copies.append(pltpu.make_async_copy(out_ref.at[index, rows, :], to_ref.at[rows, :], sems.at[index, chunk]))
            copies[-1].start()

    for turn in range(chunks + SWEEPS - 1):
        for sweep in reversed(range(SWEEPS)):
            if 0 <= turn - sweep < chunks:
                advance(turn - sweep, sweep)
    for copy in copies:
        copy.wait()


def after_kernel(*refs):
    del refs


def after(array, *others):
    return pl.pallas_call(
        after_kernel,
        out_shape=jax.ShapeDtypeStruct(array.shape, array.dtype),
        in_specs=[ANY] * (1 + len(others)),
        out_specs=ANY,
        input_output_aliases={0: 0},
        compiler_params=limit(0),
        name="after",
    )(array, *others)


def in_hbm(*arrays):
    return [pltpu.with_memory_space_constraint(array, pltpu.HBM) for array in arrays]


def limit(nbytes):
    return pltpu.CompilerParams(vmem_limit_bytes=min(60 << 20, int(nbytes) + (16 << 20)))


def local(feeders, nodes, factors, loadings, parents, load_base, lateral_z, trunk_z):
    node = lax.axis_index("node").astype(jnp.int32)
    feeder = lax.axis_index("feeder").astype(jnp.int32)
    rows, rank = factors.shape
    scen = rows * nodes
    n = loadings.shape[0]
    width = max(scen // feeders, LANES)
    share = feeders * width // scen
    f32, bf16 = jnp.float32, jnp.bfloat16
    matrix_shape = (2 * n + EXTRA, 4 * n)

    def trade(block, offset):
        return lax.ppermute(block, "node", [(i, i ^ offset) for i in range(nodes)])

    held = {0: factors}
    far = nodes // 2
    if far:
        held[far] = trade(factors, far)

    packed = pl.pallas_call(
        pack_kernel,
        out_shape=jax.ShapeDtypeStruct((n + EXTRA, rank), bf16),
        in_specs=[HBM] * 5,
        out_specs=VMEM,
        scratch_shapes=[
            pltpu.SMEM((2,), f32),
            pltpu.VMEM((n, rank), bf16),
            pltpu.VMEM((1, n), jnp.int32),
            pltpu.VMEM((2, 2, n), f32),
            pltpu.VMEM((EXTRA, rank), f32),
            pltpu.SemaphoreType.DMA((5,)),
        ],
        compiler_params=limit(2 * (n + EXTRA) * rank * 2),
        name="pack",
    )(*in_hbm(trunk_z.reshape(2), loadings, parents.reshape(1, n), load_base, lateral_z))

    def swap(block, offset):
        return lax.ppermute(block, "feeder", [(i, i ^ offset) for i in range(feeders)])

    every = {0: packed}
    for offset in sorted(range(2, feeders, 2), key=lambda o: -(o & -o)):
        every[offset] = swap(packed, offset)
    every[1] = swap(packed, 1)
    slots = list(every)
    early = len(slots)
    first_on, *others_on, last_on = slots[1:-1]
    every[first_on + 1] = swap(every[first_on], 1)
    for offset in others_on:
        every[offset + 1] = swap(every[offset], 1)
    every[last_on] = after(every[last_on], every[first_on + 1], *(every[offset + 1] for offset in others_on))
    every[last_on + 1] = swap(every[last_on], 1)
    slots = list(every)

    if far:
        held[far] = after(held[far], *(every[slot] for slot in slots[:early]))
    step = far // 2
    while step >= 1:
        for offset in list(held):
            held[offset ^ step] = trade(held[offset], step)
        step //= 2
    pieces = [held[offset] for offset in range(nodes)]

    start = (feeder // share) * width
    place = jnp.stack([(start // rows) ^ node, start % rows, feeder])

    def states(count):
        return [
            ((count, *matrix_shape), bf16),
            ((count, n, width), f32),
            ((count, 2 * n, width), f32),
            ((count, EXTRA, width), f32),
        ]

    state_bytes = (2 * n + EXTRA) * 8 * n + (3 * n + EXTRA) * width * 4 + (n + EXTRA) * rank * 2
    block, own, kept, *started = pl.pallas_call(
        functools.partial(early_kernel, nodes),
        out_shape=[
            jax.ShapeDtypeStruct((width, rank), bf16),
            jax.ShapeDtypeStruct(matrix_shape, bf16),
            pltpu.HBM((nodes - 1, rows, rank), bf16),
        ]
        + [jax.ShapeDtypeStruct(*state) for state in states(early)],
        in_specs=[SMEM, HBM] + [ANY] * (nodes - 1) + [VMEM] * early,
        out_specs=[VMEM, VMEM, HBM] + [VMEM] * 4,
        scratch_shapes=[pltpu.SemaphoreType.DMA, pltpu.SemaphoreType.DMA((nodes - 1,))],
        compiler_params=limit(early * state_bytes),
        cost_estimate=pl.CostEstimate(flops=early * (1 << 29), bytes_accessed=early * state_bytes, transcendentals=early * n * width),
        name="early",
    )(place, *in_hbm(pieces[0]), *pieces[1:], *(every[slot] for slot in slots[:early]))
    heads = pl.pallas_call(
        functools.partial(heads_kernel, slots, early),
        out_shape=jax.ShapeDtypeStruct((feeders, 8, width), f32),
        in_specs=[SMEM] + [VMEM] * (1 + feeders + 4),
        out_specs=VMEM,
        scratch_shapes=[pltpu.VMEM(*state) for state in states(max(feeders - early, 1))[:3]]
        + [
            pltpu.VMEM((feeders, 2 * n, width), f32),
            pltpu.VMEM((feeders, 8, width), f32),
            pltpu.VMEM((feeders, 8, width), f32),
        ],
        compiler_params=limit((feeders - early) * state_bytes + feeders * (2 * n + 16) * width * 4),
        name="heads",
    )(place, block, *(every[slot] for slot in slots), *started)
    given = lax.all_to_all(heads, "feeder", 0, 0, tiled=True)
    given = given[::share]

    chunks = scen // width
    swing, drop = pl.pallas_call(
        first_kernel,
        out_shape=(
            jax.ShapeDtypeStruct((chunks, n, width), f32),
            jax.ShapeDtypeStruct((chunks, 2 * n, width), f32),
        ),
        in_specs=[SMEM, VMEM, HBM, HBM, HBM],
        out_specs=(VMEM, VMEM),
        scratch_shapes=[
            pltpu.VMEM((n, rank), bf16),
            pltpu.VMEM((nodes, rows, rank), bf16),
            pltpu.SemaphoreType.DMA((nodes + 1,)),
        ],
        compiler_params=limit(3 * n * scen * 4 + scen * rank * 2),
        cost_estimate=pl.CostEstimate(flops=2 * scen * n * rank * 4, bytes_accessed=3 * n * scen * 4, transcendentals=scen * n),
        name="first",
    )(node.reshape(1), own, *in_hbm(loadings, factors, kept))
    return pl.pallas_call(
        volts_kernel,
        out_shape=(
            jax.ShapeDtypeStruct((scen, n), f32),
            jax.ShapeDtypeStruct((scen, n), f32),
        ),
        in_specs=[VMEM] * 4,
        out_specs=(HBM, HBM),
        scratch_shapes=[pltpu.VMEM((2, scen, n), f32), pltpu.SemaphoreType.DMA((2, chunks))],
        compiler_params=limit(5 * n * scen * 4),
        name="volts",
    )(own, swing, drop, given)


def solution(mesh):
    feeders = mesh.shape["feeder"]
    nodes = mesh.shape["node"]
    return jax.shard_map(
        functools.partial(local, feeders, nodes),
        mesh=mesh,
        in_specs=(
            P("node", None),
            P(("feeder", "node"), None),
            P(("feeder", "node")),
            P(None, ("feeder", "node")),
            P(None, ("feeder", "node")),
            P(None, "feeder", "node"),
        ),
        out_specs=(P(None, ("feeder", "node")), P(None, ("feeder", "node"))),
        check_vma=False,
    )
```

```python
import functools

import jax
import jax.numpy as jnp
from jax import lax
from jax.experimental import pallas as pl
from jax.experimental.pallas import tpu as pltpu
from jax.sharding import PartitionSpec as P

SWEEPS = 3
EXTRA = 16
LANES = 128

VMEM = pl.BlockSpec(memory_space=pltpu.VMEM)
SMEM = pl.BlockSpec(memory_space=pltpu.SMEM)
HBM = pl.BlockSpec(memory_space=pltpu.HBM)
ANY = pl.BlockSpec(memory_space=pl.ANY)


def split(x):
    high = x.astype(jnp.bfloat16)
    low = (x - high.astype(jnp.float32)).astype(jnp.bfloat16)
    return high, low


def product(left, right):
    return jnp.dot(left, right, preferred_element_type=jnp.float32)


def product_nt(left, right):
    return lax.dot_general(left, right, (((1,), (1,)), ((), ())), preferred_element_type=jnp.float32)


def wide(row, width):
    n = row.shape[1]
    if width <= n:
        return row[:, :width]
    return jnp.concatenate([row] * (width // n), axis=1)


def pack_kernel(
    trunk_ref, loadings_ref, parents_ref, base_ref, z_ref, out_ref, trunk, loads, owners, rows_ref, meta_ref, sems
):
    n = loadings_ref.shape[0]
    copies = [
        pltpu.make_async_copy(loadings_ref, loads, sems.at[0]),
        pltpu.make_async_copy(parents_ref, owners, sems.at[1]),
        pltpu.make_async_copy(base_ref, rows_ref.at[0], sems.at[2]),
        pltpu.make_async_copy(z_ref, rows_ref.at[1], sems.at[3]),
        pltpu.make_async_copy(trunk_ref, trunk, sems.at[4]),
    ]
    for copy in copies:
        copy.start()
    for copy in copies[1:]:
        copy.wait()
    pair_ids = lax.broadcasted_iota(jnp.int32, (2, n), 0)
    trunk_rows = jnp.where(pair_ids == 0, trunk[0], trunk[1])
    for index, rows in enumerate((rows_ref[0], rows_ref[1], trunk_rows)):
        high = rows.astype(jnp.bfloat16).astype(jnp.float32)
        middle = (rows - high).astype(jnp.bfloat16).astype(jnp.float32)
        meta_ref[2 * index : 2 * index + 2, 0:n] = high
        meta_ref[2 * index : 2 * index + 2, n : 2 * n] = middle
        meta_ref[8 + 2 * index : 10 + 2 * index, 0:n] = rows - high - middle
    meta_ref[6:8, 0:n] = jnp.broadcast_to(owners[...].astype(jnp.float32), (2, n))
    meta_ref[6:8, n : 2 * n] = jnp.zeros((2, n), jnp.float32)
    meta_ref[14:16, 0:n] = jnp.zeros((2, n), jnp.float32)
    meta_ref[8:16, n : 2 * n] = jnp.zeros((8, n), jnp.float32)
    meta = meta_ref[...].astype(jnp.bfloat16)
    copies[0].wait()
    out_ref[0:n, :] = loads[...]
    out_ref[n : n + EXTRA, :] = meta


def constants(section_ref, n):
    meta = section_ref[n : n + EXTRA, :].astype(jnp.float32)
    high, middle = meta[0:8, 0:n], meta[0:8, n : 2 * n]
    return high, middle, high + middle + meta[8:16, 0:n]


def matrix_steps(sections, n):
    highs, middles, rows = zip(*(constants(section, n) for section in sections))
    row_ids = lax.broadcasted_iota(jnp.int32, (n, n), 0)
    lane_ids = lax.broadcasted_iota(jnp.int32, (n, n), 1)
    section_ids = lax.broadcasted_iota(jnp.int32, (max(8, len(sections)), n), 0)
    stacked = jnp.full(section_ids.shape, -1, jnp.int32)
    for index, row in enumerate(rows):
        stacked = jnp.where(section_ids == index, row[6:7].astype(jnp.int32), stacked)
    known = {1: stacked}

    def ancestor(distance):
        if distance not in known:
            step = 1 << (distance.bit_length() - 1)
            if step == distance:
                step //= 2
            far, near = ancestor(step), ancestor(distance - step)
            known[distance] = jnp.where(near < 0, -1, jnp.take_along_axis(far, jnp.maximum(near, 0), axis=1))
        return known[distance]

    digits = []
    unit = 1
    while unit < n:
        digits.append([ancestor(unit * digit).astype(jnp.float32) for digit in range(1, 8) if unit * digit < n])
        unit *= 8
    last = [found.T for found in digits.pop()]
    yield None

    rows_b, lanes_b = (ids.astype(jnp.float32).astype(jnp.bfloat16) for ids in (row_ids, lane_ids))
    one, zero = jnp.ones((n, n), jnp.bfloat16), jnp.zeros((n, n), jnp.bfloat16)
    identity = jnp.where(rows_b == lanes_b, one, zero)
    products = [None] * len(sections)
    for index in range(len(sections)):
        for digit in digits:
            factor = identity
            for found in digit:
                row = jnp.broadcast_to(found[index : index + 1, :].astype(jnp.bfloat16), (n, n))
                factor = jnp.where(rows_b == row, one, factor)
            done = products[index]
            products[index] = factor if done is None else product(done, factor).astype(jnp.bfloat16)
    yield None

    paths = []
    for index in range(len(sections)):
        factor = identity
        for found in last:
            column = jnp.broadcast_to(found[:, index : index + 1], (n, n)).astype(jnp.bfloat16)
            factor = jnp.where(lanes_b == column, one, factor)
        paths.append(product_nt(factor, products[index]).astype(jnp.bfloat16))
    yield None

    shared = []
    for path, high, middle in zip(paths, highs, middles):
        wide_path = path.astype(jnp.float32)

        def scaled(index):
            return jnp.concatenate([wide_path * high[index : index + 1], wide_path * middle[index : index + 1]], axis=1)

        left = jnp.concatenate([scaled(2), scaled(3)], axis=0).astype(jnp.bfloat16)
        shared.append(product_nt(left, jnp.concatenate([path, path], axis=1)))
    yield None

    pad_ids = lax.broadcasted_iota(jnp.int32, (EXTRA, 2 * n), 0)
    out = []
    for both, row in zip(shared, rows):
        resist, react = both[:n], both[n:]
        base_active, base_reactive = row[0:1], row[1:2]
        real_high, real_low = split(resist * base_active + react * base_reactive)
        imag_high, imag_low = split(react * base_active - resist * base_reactive)
        row_real = jnp.concatenate([base_active, base_reactive], axis=1)
        row_imag = jnp.concatenate([-base_reactive, base_active], axis=1)
        sums_high, sums_low = split(jnp.where(pad_ids == 0, row_real, jnp.where(pad_ids == 1, row_imag, 0.0)))

        def whole(real_part, imag_part, sums_part):
            top = jnp.concatenate([real_part, -imag_part], axis=1)
            bottom = jnp.concatenate([imag_part, real_part], axis=1)
            return jnp.concatenate([top, bottom, sums_part], axis=0)

        out.append(
            jnp.concatenate(
                [whole(real_high, imag_high, sums_high), whole(real_low, imag_low, sums_low)], axis=1
            )
        )
    yield out


def swing_of(loadings, factors):
    level = product_nt(loadings, factors).astype(jnp.bfloat16).astype(jnp.float32)
    return 1.0 + 0.5 * jnp.tanh(level)


def apply(matrix, u):
    span = matrix.shape[1] // 2
    high, low = split(u)
    left = jnp.concatenate([matrix, matrix[:, :span]], axis=1)
    return product(left, jnp.concatenate([high, high, low], axis=0))


def apply_first(matrix, swing):
    n = matrix.shape[1] // 4
    high, low = split(swing)
    high_part, low_part = matrix[:, :n], matrix[:, 2 * n : 3 * n]
    return product(
        jnp.concatenate([high_part, low_part, high_part], axis=1), jnp.concatenate([high, high, low], axis=0)
    )


def inverse_of(swing, real, imag):
    return swing * pltpu.reciprocal(real * real + imag * imag, approx=True)


def scaled_volts(swing, real, imag):
    inverse = inverse_of(swing, real, imag)
    return jnp.concatenate([real * inverse, imag * inverse], axis=0)


def first_sweep(sections, factors_ref, matrix_ref, swing_ref, drop_ref, inject_ref, arrived=None):
    n = swing_ref.shape[1]
    for start in range(0, len(sections), 8):
        group = list(enumerate(sections))[start : start + 8]
        steps = matrix_steps([section for _, section in group], n)
        next(steps)
        if start == 0 and arrived is not None:
            arrived()
        for slot, section in group:
            swing_ref[slot] = swing_of(section[0:n, :], factors_ref[...])
        *_, matrices = steps
        for (slot, _), matrix in zip(group, matrices):
            matrix_ref[slot] = matrix
            out = apply_first(matrix_ref[slot], swing_ref[slot])
            drop_ref[slot] = out[: 2 * n]
            inject_ref[slot] = out[2 * n :]


def between_kernel(factors_ref, *refs):
    first_sweep(refs[:-4], factors_ref, *refs[-4:])


def early_kernel(pieces, place_ref, *refs):
    piece_refs, sections = refs[:pieces], refs[pieces:-9]
    factors_ref, own_ref, kept_ref, matrix_ref, swing_ref, drop_ref, inject_ref, sem, keep_sems = refs[-9:]
    width = factors_ref.shape[0]
    piece, offset = place_ref[0], place_ref[1]
    keeps = [
        pltpu.make_async_copy(piece_ref, kept_ref.at[index], keep_sems.at[index])
        for index, piece_ref in enumerate(piece_refs[1:])
    ]
    for copy in keeps:
        copy.start()
    for index, piece_ref in enumerate(piece_refs):
        @pl.when(piece == index)
        def _(piece_ref=piece_ref):
            rows = piece_ref.at[pl.ds(pl.multiple_of(offset, width), width), :]
            pltpu.make_async_copy(rows, factors_ref, sem).start()

    def arrived():
        pltpu.make_async_copy(piece_refs[0].at[0:width, :], factors_ref, sem).wait()

    first_sweep(sections, factors_ref, matrix_ref, swing_ref, drop_ref, inject_ref, arrived)
    own_ref[...] = matrix_ref[0]
    for copy in keeps:
        copy.wait()


def heads_kernel(slots, counts, place_ref, factors_ref, *refs):
    feeders, early = len(slots), sum(counts)
    sections, refs = refs[:feeders], refs[feeders:]
    done = []
    for count in counts:
        done += [[ref.at[index] for ref in refs[:4]] for index in range(count)]
        refs = refs[4:]
    head_ref, matrix_ref, swing_ref, drop_ref, again_ref, flow_ref, trunk_ref = refs
    width = factors_ref.shape[0]
    n = swing_ref.shape[1]
    place = [jnp.bitwise_xor(place_ref[2], slot) for slot in slots]
    late_refs = (matrix_ref, swing_ref, drop_ref)

    def of(index, which):
        return done[index][which] if index < early else late_refs[which].at[index - early]

    def flow_of(index, real, imag):
        base = constants(sections[index], n)[2].T
        active, reactive = base[:, 0:1], base[:, 1:2]
        if imag is None:
            parts = (active * real, -reactive * real)
        else:
            parts = (active * real + reactive * imag, active * imag - reactive * real)
        return [jnp.sum(part, axis=0, keepdims=True) for part in parts]

    groups = [list(range(start, min(start + 8, feeders))) for start in range(early, feeders, 8)]
    steps = [matrix_steps([sections[index] for index in group], n) for group in groups]
    if steps:
        next(steps[0])
    for index in range(feeders):
        row = constants(sections[index], n)[2]
        trunk_ref[place[index], 0:2, :] = wide(row[4:6], width)
        if index < early:
            flow_ref[place[index]] = of(index, 3)[0:8, :]
        else:
            swing = swing_of(sections[index][0:n, :], factors_ref[...])
            of(index, 1)[...] = swing
            for part, total in enumerate(flow_of(index, swing, None)):
                flow_ref[place[index], part : part + 1, :] = total

    def heads(sweep):
        flows = [None] * feeders
        real = jnp.zeros((1, width), jnp.float32)
        imag = real
        for g in reversed(range(feeders)):
            real = real + flow_ref[g, 0:1, :]
            imag = imag + flow_ref[g, 1:2, :]
            flows[g] = (real, imag)
        head_real = jnp.ones((1, width), jnp.float32)
        head_imag = jnp.zeros((1, width), jnp.float32)
        for g in range(feeders):
            r, x = trunk_ref[g, 0:1, :], trunk_ref[g, 1:2, :]
            real, imag = flows[g]
            head_real = head_real - (r * real - x * imag)
            head_imag = head_imag - (r * imag + x * real)
            head_ref[g, 2 * sweep : 2 * sweep + 1, :] = head_real
            head_ref[g, 2 * sweep + 1 : 2 * sweep + 2, :] = head_imag

    def volts(index, sweep):
        drop = of(index, 2) if sweep == 1 else again_ref.at[index]
        real = head_ref[place[index], 2 * sweep - 2 : 2 * sweep - 1, :] - drop[0:n, :]
        imag = head_ref[place[index], 2 * sweep - 1 : 2 * sweep, :] - drop[n : 2 * n, :]
        return real, imag

    def middle(index, sweep):
        out = apply(of(index, 0)[...], scaled_volts(of(index, 1)[...], *volts(index, sweep)))
        again_ref[index] = out[: 2 * n]
        flow_ref[place[index]] = out[2 * n : 2 * n + 8]

    heads(0)
    ready = list(range(early))
    for group, step in zip(groups, steps):
        for matrices in step:
            if ready:
                middle(ready.pop(0), 1)
        for index, matrix in zip(group, matrices):
            of(index, 0)[...] = matrix
            of(index, 2)[...] = apply_first(matrix, of(index, 1)[...])[: 2 * n]
    for index in ready + list(range(early, feeders)):
        middle(index, 1)
    heads(1)
    for sweep in range(2, SWEEPS):
        for index in range(feeders):
            if sweep < SWEEPS - 1:
                middle(index, sweep)
            else:
                real, imag = volts(index, sweep)
                inverse = inverse_of(of(index, 1)[...], real, imag)
                for part, total in enumerate(flow_of(index, real * inverse, imag * inverse)):
                    flow_ref[place[index], part : part + 1, :] = total
        heads(sweep)
    for g in range(feeders):
        head_ref[g, 2 * SWEEPS :, :] = jnp.zeros((head_ref.shape[1] - 2 * SWEEPS, width), jnp.float32)


def first_kernel(
    node_ref, matrix_ref, loadings_ref, rows_ref, kept_ref, swing_ref, drop_ref, loads, factors_ref, sems
):
    n = loadings_ref.shape[0]
    width = swing_ref.shape[2]
    pieces = 1 + kept_ref.shape[0]
    chunks = rows_ref.shape[0] // width
    copies = [pltpu.make_async_copy(loadings_ref, loads, sems.at[pieces])]
    for index in range(pieces):
        piece_ref = kept_ref.at[index - 1] if index else rows_ref
        copies.append(pltpu.make_async_copy(piece_ref, factors_ref.at[index], sems.at[index]))
    for copy in copies:
        copy.start()
    matrix = matrix_ref[0 : 2 * n, :]
    for copy in copies:
        copy.wait()
    loadings = loads[...]
    together = 4 // chunks if chunks < 4 else 1

    @pl.loop(0, pieces // together)
    def _(outer):
        for inner in range(together):
            index = outer * together + inner
            for part in range(chunks):
                chunk = jnp.bitwise_xor(node_ref[0], index) * chunks + part
                swing = swing_of(loadings, factors_ref[index, part * width : (part + 1) * width, :])
                swing_ref[chunk] = swing
                drop_ref[chunk] = apply_first(matrix, swing)


def volts_kernel(matrix_ref, swing_ref, drop_ref, head_ref, real_ref, imag_ref, out_ref, sems):
    n = swing_ref.shape[1]
    chunks, width = swing_ref.shape[0], swing_ref.shape[2]
    matrix = matrix_ref[0 : 2 * n, :]
    drops = [None] * chunks
    copies = []

    def advance(chunk, sweep):
        drop = drop_ref[chunk] if sweep == 0 else drops[chunk]
        real = head_ref[chunk, 2 * sweep : 2 * sweep + 1, :] - drop[:n]
        imag = head_ref[chunk, 2 * sweep + 1 : 2 * sweep + 2, :] - drop[n:]
        if sweep < SWEEPS - 1:
            drops[chunk] = apply(matrix, scaled_volts(swing_ref[chunk], real, imag))
            return
        rows = slice(chunk * width, (chunk + 1) * width)
        for index, (part, to_ref) in enumerate(((real, real_ref), (imag, imag_ref))):
            out_ref[index, rows, :] = part.T
            copies.append(pltpu.make_async_copy(out_ref.at[index, rows, :], to_ref.at[rows, :], sems.at[index, chunk]))
            copies[-1].start()

    for turn in range(chunks + SWEEPS - 1):
        for sweep in reversed(range(SWEEPS)):
            if 0 <= turn - sweep < chunks:
                advance(turn - sweep, sweep)
    for copy in copies:
        copy.wait()


def after_kernel(*refs):
    del refs


def after(array, *others):
    return pl.pallas_call(
        after_kernel,
        out_shape=jax.ShapeDtypeStruct(array.shape, array.dtype),
        in_specs=[ANY] * (1 + len(others)),
        out_specs=ANY,
        input_output_aliases={0: 0},
        compiler_params=limit(0),
        name="after",
    )(array, *others)


def in_hbm(*arrays):
    return [pltpu.with_memory_space_constraint(array, pltpu.HBM) for array in arrays]


def limit(nbytes):
    return pltpu.CompilerParams(vmem_limit_bytes=min(60 << 20, int(nbytes) + (16 << 20)))


def local(feeders, nodes, factors, loadings, parents, load_base, lateral_z, trunk_z):
    node = lax.axis_index("node").astype(jnp.int32)
    feeder = lax.axis_index("feeder").astype(jnp.int32)
    rows, rank = factors.shape
    scen = rows * nodes
    n = loadings.shape[0]
    width = max(scen // feeders, LANES)
    share = feeders * width // scen
    f32, bf16 = jnp.float32, jnp.bfloat16
    matrix_shape = (2 * n + EXTRA, 4 * n)

    def trade(block, offset):
        return lax.ppermute(block, "node", [(i, i ^ offset) for i in range(nodes)])

    held = {0: factors}
    far = nodes // 2
    if far:
        held[far] = trade(factors, far)

    packed = pl.pallas_call(
        pack_kernel,
        out_shape=jax.ShapeDtypeStruct((n + EXTRA, rank), bf16),
        in_specs=[HBM] * 5,
        out_specs=VMEM,
        scratch_shapes=[
            pltpu.SMEM((2,), f32),
            pltpu.VMEM((n, rank), bf16),
            pltpu.VMEM((1, n), jnp.int32),
            pltpu.VMEM((2, 2, n), f32),
            pltpu.VMEM((EXTRA, rank), f32),
            pltpu.SemaphoreType.DMA((5,)),
        ],
        compiler_params=limit(2 * (n + EXTRA) * rank * 2),
        name="pack",
    )(*in_hbm(trunk_z.reshape(2), loadings, parents.reshape(1, n), load_base, lateral_z))

    def swap(block, offset):
        return lax.ppermute(block, "feeder", [(i, i ^ offset) for i in range(feeders)])

    every = {0: packed}
    for offset in sorted(range(2, feeders, 2), key=lambda o: -(o & -o)):
        every[offset] = swap(packed, offset)
    every[1] = swap(packed, 1)
    slots = list(every)
    early = len(slots)
    middle = [3] if 2 in every else []
    for offset in middle:
        every[offset] = swap(every[1], offset ^ 1)
    for offset in slots[1:-1]:
        if offset + 1 not in every:
            every[offset + 1] = swap(every[offset], 1)
    slots = list(every)

    if far:
        held[far] = after(held[far], *(every[slot] for slot in slots[:early]))
    step = far // 2
    while step >= 1:
        for offset in list(held):
            held[offset ^ step] = trade(held[offset], step)
        step //= 2
    pieces = [held[offset] for offset in range(nodes)]

    start = (feeder // share) * width
    place = jnp.stack([(start // rows) ^ node, start % rows, feeder])

    def states(count):
        return [
            ((count, *matrix_shape), bf16),
            ((count, n, width), f32),
            ((count, 2 * n, width), f32),
            ((count, EXTRA, width), f32),
        ]

    state_bytes = (2 * n + EXTRA) * 8 * n + (3 * n + EXTRA) * width * 4 + (n + EXTRA) * rank * 2
    block, own, kept, *started = pl.pallas_call(
        functools.partial(early_kernel, nodes),
        out_shape=[
            jax.ShapeDtypeStruct((width, rank), bf16),
            jax.ShapeDtypeStruct(matrix_shape, bf16),
            pltpu.HBM((nodes - 1, rows, rank), bf16),
        ]
        + [jax.ShapeDtypeStruct(*state) for state in states(early)],
        in_specs=[SMEM, HBM] + [ANY] * (nodes - 1) + [VMEM] * early,
        out_specs=[VMEM, VMEM, HBM] + [VMEM] * 4,
        scratch_shapes=[pltpu.SemaphoreType.DMA, pltpu.SemaphoreType.DMA((nodes - 1,))],
        compiler_params=limit(early * state_bytes),
        cost_estimate=pl.CostEstimate(flops=early * (1 << 29), bytes_accessed=early * state_bytes, transcendentals=early * n * width),
        name="early",
    )(place, *in_hbm(pieces[0]), *pieces[1:], *(every[slot] for slot in slots[:early]))
    counts = [early]
    if middle:
        counts.append(len(middle))
        started += pl.pallas_call(
            between_kernel,
            out_shape=[jax.ShapeDtypeStruct(*state) for state in states(len(middle))],
            in_specs=[VMEM] * (1 + len(middle)),
            out_specs=[VMEM] * 4,
            compiler_params=limit(len(middle) * state_bytes),
            cost_estimate=pl.CostEstimate(flops=1 << 20, bytes_accessed=1 << 10, transcendentals=0),
            name="between",
        )(block, *(every[slot] for slot in middle))
    late = feeders - sum(counts)
    heads = pl.pallas_call(
        functools.partial(heads_kernel, slots, counts),
        out_shape=jax.ShapeDtypeStruct((feeders, 8, width), f32),
        in_specs=[SMEM] + [VMEM] * (1 + feeders + len(started)),
        out_specs=VMEM,
        scratch_shapes=[pltpu.VMEM(*state) for state in states(max(late, 1))[:3]]
        + [
            pltpu.VMEM((feeders, 2 * n, width), f32),
            pltpu.VMEM((feeders, 8, width), f32),
            pltpu.VMEM((feeders, 8, width), f32),
        ],
        compiler_params=limit(feeders * state_bytes + feeders * (2 * n + 16) * width * 4),
        name="heads",
    )(place, block, *(every[slot] for slot in slots), *started)
    given = lax.all_to_all(heads, "feeder", 0, 0, tiled=True)
    given = given[::share]

    chunks = scen // width
    swing, drop = pl.pallas_call(
        first_kernel,
        out_shape=(
            jax.ShapeDtypeStruct((chunks, n, width), f32),
            jax.ShapeDtypeStruct((chunks, 2 * n, width), f32),
        ),
        in_specs=[SMEM, VMEM, HBM, HBM, HBM],
        out_specs=(VMEM, VMEM),
        scratch_shapes=[
            pltpu.VMEM((n, rank), bf16),
            pltpu.VMEM((nodes, rows, rank), bf16),
            pltpu.SemaphoreType.DMA((nodes + 1,)),
        ],
        compiler_params=limit(3 * n * scen * 4 + scen * rank * 2),
        cost_estimate=pl.CostEstimate(flops=2 * scen * n * rank * 4, bytes_accessed=3 * n * scen * 4, transcendentals=scen * n),
        name="first",
    )(node.reshape(1), own, *in_hbm(loadings, factors, kept))
    return pl.pallas_call(
        volts_kernel,
        out_shape=(
            jax.ShapeDtypeStruct((scen, n), f32),
            jax.ShapeDtypeStruct((scen, n), f32),
        ),
        in_specs=[VMEM] * 4,
        out_specs=(HBM, HBM),
        scratch_shapes=[pltpu.VMEM((2, scen, n), f32), pltpu.SemaphoreType.DMA((2, chunks))],
        compiler_params=limit(5 * n * scen * 4),
        name="volts",
    )(own, swing, drop, given)


def solution(mesh):
    feeders = mesh.shape["feeder"]
    nodes = mesh.shape["node"]
    return jax.shard_map(
        functools.partial(local, feeders, nodes),
        mesh=mesh,
        in_specs=(
            P("node", None),
            P(("feeder", "node"), None),
            P(("feeder", "node")),
            P(None, ("feeder", "node")),
            P(None, ("feeder", "node")),
            P(None, "feeder", "node"),
        ),
        out_specs=(P(None, ("feeder", "node")), P(None, ("feeder", "node"))),
        check_vma=False,
    )
```

```python
import functools

import jax
import jax.numpy as jnp
from jax import lax
from jax.experimental import pallas as pl
from jax.experimental.pallas import tpu as pltpu
from jax.sharding import PartitionSpec as P

SWEEPS = 3
EXTRA = 16
LANES = 128

VMEM = pl.BlockSpec(memory_space=pltpu.VMEM)
SMEM = pl.BlockSpec(memory_space=pltpu.SMEM)
HBM = pl.BlockSpec(memory_space=pltpu.HBM)
ANY = pl.BlockSpec(memory_space=pl.ANY)


def split(x):
    high = x.astype(jnp.bfloat16)
    low = (x - high.astype(jnp.float32)).astype(jnp.bfloat16)
    return high, low


def product(left, right):
    return jnp.dot(left, right, preferred_element_type=jnp.float32)


def product_nt(left, right):
    return lax.dot_general(left, right, (((1,), (1,)), ((), ())), preferred_element_type=jnp.float32)


def wide(row, width):
    n = row.shape[1]
    if width <= n:
        return row[:, :width]
    return jnp.concatenate([row] * (width // n), axis=1)


def pack_kernel(
    trunk_ref, loadings_ref, parents_ref, base_ref, z_ref, out_ref, trunk, loads, owners, rows_ref, meta_ref, sems
):
    n = loadings_ref.shape[0]
    copies = [
        pltpu.make_async_copy(loadings_ref, loads, sems.at[0]),
        pltpu.make_async_copy(parents_ref, owners, sems.at[1]),
        pltpu.make_async_copy(base_ref, rows_ref.at[0], sems.at[2]),
        pltpu.make_async_copy(z_ref, rows_ref.at[1], sems.at[3]),
        pltpu.make_async_copy(trunk_ref, trunk, sems.at[4]),
    ]
    for copy in copies:
        copy.start()
    for copy in copies[1:]:
        copy.wait()
    pair_ids = lax.broadcasted_iota(jnp.int32, (2, n), 0)
    trunk_rows = jnp.where(pair_ids == 0, trunk[0], trunk[1])
    for index, rows in enumerate((rows_ref[0], rows_ref[1], trunk_rows)):
        high = rows.astype(jnp.bfloat16).astype(jnp.float32)
        middle = (rows - high).astype(jnp.bfloat16).astype(jnp.float32)
        meta_ref[2 * index : 2 * index + 2, 0:n] = high
        meta_ref[2 * index : 2 * index + 2, n : 2 * n] = middle
        meta_ref[8 + 2 * index : 10 + 2 * index, 0:n] = rows - high - middle
    meta_ref[6:8, 0:n] = jnp.broadcast_to(owners[...].astype(jnp.float32), (2, n))
    meta_ref[6:8, n : 2 * n] = jnp.zeros((2, n), jnp.float32)
    meta_ref[14:16, 0:n] = jnp.zeros((2, n), jnp.float32)
    meta_ref[8:16, n : 2 * n] = jnp.zeros((8, n), jnp.float32)
    meta = meta_ref[...].astype(jnp.bfloat16)
    copies[0].wait()
    out_ref[0:n, :] = loads[...]
    out_ref[n : n + EXTRA, :] = meta


def constants(section_ref, n):
    meta = section_ref[n : n + EXTRA, :].astype(jnp.float32)
    high, middle = meta[0:8, 0:n], meta[0:8, n : 2 * n]
    return high, middle, high + middle + meta[8:16, 0:n]


def matrix_steps(sections, n):
    highs, middles, rows = zip(*(constants(section, n) for section in sections))
    row_ids = lax.broadcasted_iota(jnp.int32, (n, n), 0)
    lane_ids = lax.broadcasted_iota(jnp.int32, (n, n), 1)
    section_ids = lax.broadcasted_iota(jnp.int32, (max(8, len(sections)), n), 0)
    stacked = jnp.full(section_ids.shape, -1, jnp.int32)
    for index, row in enumerate(rows):
        stacked = jnp.where(section_ids == index, row[6:7].astype(jnp.int32), stacked)
    known = {1: stacked}

    def ancestor(distance):
        if distance not in known:
            step = 1 << (distance.bit_length() - 1)
            if step == distance:
                step //= 2
            far, near = ancestor(step), ancestor(distance - step)
            known[distance] = jnp.where(near < 0, -1, jnp.take_along_axis(far, jnp.maximum(near, 0), axis=1))
        return known[distance]

    digits = []
    unit = 1
    while unit < n:
        digits.append([ancestor(unit * digit).astype(jnp.float32) for digit in range(1, 8) if unit * digit < n])
        unit *= 8
    last = [found.T for found in digits.pop()]
    yield None

    rows_b, lanes_b = (ids.astype(jnp.float32).astype(jnp.bfloat16) for ids in (row_ids, lane_ids))
    one, zero = jnp.ones((n, n), jnp.bfloat16), jnp.zeros((n, n), jnp.bfloat16)
    identity = jnp.where(rows_b == lanes_b, one, zero)
    products = [None] * len(sections)
    for index in range(len(sections)):
        for digit in digits:
            factor = identity
            for found in digit:
                row = jnp.broadcast_to(found[index : index + 1, :].astype(jnp.bfloat16), (n, n))
                factor = jnp.where(rows_b == row, one, factor)
            done = products[index]
            products[index] = factor if done is None else product(done, factor).astype(jnp.bfloat16)
    yield None

    paths = []
    for index in range(len(sections)):
        factor = identity
        for found in last:
            column = jnp.broadcast_to(found[:, index : index + 1], (n, n)).astype(jnp.bfloat16)
            factor = jnp.where(lanes_b == column, one, factor)
        paths.append(product_nt(factor, products[index]).astype(jnp.bfloat16))
    yield None

    shared = []
    for path, high, middle in zip(paths, highs, middles):
        wide_path = path.astype(jnp.float32)

        def scaled(index):
            return jnp.concatenate([wide_path * high[index : index + 1], wide_path * middle[index : index + 1]], axis=1)

        left = jnp.concatenate([scaled(2), scaled(3)], axis=0).astype(jnp.bfloat16)
        shared.append(product_nt(left, jnp.concatenate([path, path], axis=1)))
    yield None

    pad_ids = lax.broadcasted_iota(jnp.int32, (EXTRA, 2 * n), 0)
    out = []
    for both, row in zip(shared, rows):
        resist, react = both[:n], both[n:]
        base_active, base_reactive = row[0:1], row[1:2]
        real_high, real_low = split(resist * base_active + react * base_reactive)
        imag_high, imag_low = split(react * base_active - resist * base_reactive)
        row_real = jnp.concatenate([base_active, base_reactive], axis=1)
        row_imag = jnp.concatenate([-base_reactive, base_active], axis=1)
        sums_high, sums_low = split(jnp.where(pad_ids == 0, row_real, jnp.where(pad_ids == 1, row_imag, 0.0)))

        def whole(real_part, imag_part, sums_part):
            top = jnp.concatenate([real_part, -imag_part], axis=1)
            bottom = jnp.concatenate([imag_part, real_part], axis=1)
            return jnp.concatenate([top, bottom, sums_part], axis=0)

        out.append(
            jnp.concatenate(
                [whole(real_high, imag_high, sums_high), whole(real_low, imag_low, sums_low)], axis=1
            )
        )
    yield out


def swing_of(loadings, factors):
    level = product_nt(loadings, factors).astype(jnp.bfloat16).astype(jnp.float32)
    return 1.0 + 0.5 * jnp.tanh(level)


def apply(matrix, u):
    span = matrix.shape[1] // 2
    high, low = split(u)
    left = jnp.concatenate([matrix, matrix[:, :span]], axis=1)
    return product(left, jnp.concatenate([high, high, low], axis=0))


def apply_first(matrix, swing):
    n = matrix.shape[1] // 4
    high, low = split(swing)
    high_part, low_part = matrix[:, :n], matrix[:, 2 * n : 3 * n]
    return product(
        jnp.concatenate([high_part, low_part, high_part], axis=1), jnp.concatenate([high, high, low], axis=0)
    )


def inverse_of(swing, real, imag):
    return swing * pltpu.reciprocal(real * real + imag * imag, approx=True)


def scaled_volts(swing, real, imag):
    inverse = inverse_of(swing, real, imag)
    return jnp.concatenate([real * inverse, imag * inverse], axis=0)


def first_sweep(sections, factors_ref, matrix_ref, swing_ref, drop_ref, inject_ref, arrived=None):
    n = swing_ref.shape[1]
    for start in range(0, len(sections), 8):
        group = list(enumerate(sections))[start : start + 8]
        steps = matrix_steps([section for _, section in group], n)
        next(steps)
        if start == 0 and arrived is not None:
            arrived()
        for slot, section in group:
            swing_ref[slot] = swing_of(section[0:n, :], factors_ref[...])
        *_, matrices = steps
        for (slot, _), matrix in zip(group, matrices):
            matrix_ref[slot] = matrix
            out = apply_first(matrix_ref[slot], swing_ref[slot])
            drop_ref[slot] = out[: 2 * n]
            inject_ref[slot] = out[2 * n :]


def between_kernel(factors_ref, *refs):
    first_sweep(refs[:-4], factors_ref, *refs[-4:])


def early_kernel(pieces, place_ref, *refs):
    piece_refs, sections = refs[:pieces], refs[pieces:-9]
    factors_ref, own_ref, kept_ref, matrix_ref, swing_ref, drop_ref, inject_ref, sem, keep_sems = refs[-9:]
    width = factors_ref.shape[0]
    piece, offset = place_ref[0], place_ref[1]
    keeps = [
        pltpu.make_async_copy(piece_ref, kept_ref.at[index], keep_sems.at[index])
        for index, piece_ref in enumerate(piece_refs[1:])
    ]
    for copy in keeps:
        copy.start()
    for index, piece_ref in enumerate(piece_refs):
        @pl.when(piece == index)
        def _(piece_ref=piece_ref):
            rows = piece_ref.at[pl.ds(pl.multiple_of(offset, width), width), :]
            pltpu.make_async_copy(rows, factors_ref, sem).start()

    def arrived():
        pltpu.make_async_copy(piece_refs[0].at[0:width, :], factors_ref, sem).wait()

    first_sweep(sections, factors_ref, matrix_ref, swing_ref, drop_ref, inject_ref, arrived)
    own_ref[...] = matrix_ref[0]
    for copy in keeps:
        copy.wait()


def heads_kernel(slots, counts, place_ref, factors_ref, *refs):
    feeders, early = len(slots), sum(counts)
    sections, refs = refs[:feeders], refs[feeders:]
    done = []
    for count in counts:
        done += [[ref.at[index] for ref in refs[:4]] for index in range(count)]
        refs = refs[4:]
    head_ref, matrix_ref, swing_ref, drop_ref, again_ref, flow_ref, trunk_ref = refs
    width = factors_ref.shape[0]
    n = swing_ref.shape[1]
    place = [jnp.bitwise_xor(place_ref[2], slot) for slot in slots]
    late_refs = (matrix_ref, swing_ref, drop_ref)

    def of(index, which):
        return done[index][which] if index < early else late_refs[which].at[index - early]

    def flow_of(index, real, imag):
        base = constants(sections[index], n)[2].T
        active, reactive = base[:, 0:1], base[:, 1:2]
        if imag is None:
            parts = (active * real, -reactive * real)
        else:
            parts = (active * real + reactive * imag, active * imag - reactive * real)
        return [jnp.sum(part, axis=0, keepdims=True) for part in parts]

    groups = [list(range(start, min(start + 8, feeders))) for start in range(early, feeders, 8)]
    steps = [matrix_steps([sections[index] for index in group], n) for group in groups]
    if steps:
        next(steps[0])
    for index in range(feeders):
        row = constants(sections[index], n)[2]
        trunk_ref[place[index], 0:2, :] = wide(row[4:6], width)
        if index < early:
            flow_ref[place[index]] = of(index, 3)[0:8, :]
        else:
            swing = swing_of(sections[index][0:n, :], factors_ref[...])
            of(index, 1)[...] = swing
            for part, total in enumerate(flow_of(index, swing, None)):
                flow_ref[place[index], part : part + 1, :] = total

    def heads(sweep):
        flows = [None] * feeders
        real = jnp.zeros((1, width), jnp.float32)
        imag = real
        for g in reversed(range(feeders)):
            real = real + flow_ref[g, 0:1, :]
            imag = imag + flow_ref[g, 1:2, :]
            flows[g] = (real, imag)
        head_real = jnp.ones((1, width), jnp.float32)
        head_imag = jnp.zeros((1, width), jnp.float32)
        for g in range(feeders):
            r, x = trunk_ref[g, 0:1, :], trunk_ref[g, 1:2, :]
            real, imag = flows[g]
            head_real = head_real - (r * real - x * imag)
            head_imag = head_imag - (r * imag + x * real)
            head_ref[g, 2 * sweep : 2 * sweep + 1, :] = head_real
            head_ref[g, 2 * sweep + 1 : 2 * sweep + 2, :] = head_imag

    def volts(index, sweep):
        drop = of(index, 2) if sweep == 1 else again_ref.at[index]
        real = head_ref[place[index], 2 * sweep - 2 : 2 * sweep - 1, :] - drop[0:n, :]
        imag = head_ref[place[index], 2 * sweep - 1 : 2 * sweep, :] - drop[n : 2 * n, :]
        return real, imag

    def middle(index, sweep):
        out = apply(of(index, 0)[...], scaled_volts(of(index, 1)[...], *volts(index, sweep)))
        again_ref[index] = out[: 2 * n]
        flow_ref[place[index]] = out[2 * n : 2 * n + 8]

    heads(0)
    ready = list(range(early))
    for group, step in zip(groups, steps):
        for matrices in step:
            if ready:
                middle(ready.pop(0), 1)
        for index, matrix in zip(group, matrices):
            of(index, 0)[...] = matrix
            of(index, 2)[...] = apply_first(matrix, of(index, 1)[...])[: 2 * n]
    for index in ready + list(range(early, feeders)):
        middle(index, 1)
    heads(1)
    for sweep in range(2, SWEEPS):
        for index in range(feeders):
            if sweep < SWEEPS - 1:
                middle(index, sweep)
            else:
                real, imag = volts(index, sweep)
                inverse = inverse_of(of(index, 1)[...], real, imag)
                for part, total in enumerate(flow_of(index, real * inverse, imag * inverse)):
                    flow_ref[place[index], part : part + 1, :] = total
        heads(sweep)
    for g in range(feeders):
        head_ref[g, 2 * SWEEPS :, :] = jnp.zeros((head_ref.shape[1] - 2 * SWEEPS, width), jnp.float32)


def first_kernel(
    node_ref, matrix_ref, loadings_ref, rows_ref, kept_ref, swing_ref, drop_ref, loads, factors_ref, sems
):
    n = loadings_ref.shape[0]
    width = swing_ref.shape[2]
    pieces = 1 + kept_ref.shape[0]
    chunks = rows_ref.shape[0] // width
    copies = [pltpu.make_async_copy(loadings_ref, loads, sems.at[pieces])]
    for index in range(pieces):
        piece_ref = kept_ref.at[index - 1] if index else rows_ref
        copies.append(pltpu.make_async_copy(piece_ref, factors_ref.at[index], sems.at[index]))
    for copy in copies:
        copy.start()
    matrix = matrix_ref[0 : 2 * n, :]
    for copy in copies:
        copy.wait()
    loadings = loads[...]
    together = 4 // chunks if chunks < 4 else 1

    @pl.loop(0, pieces // together)
    def _(outer):
        for inner in range(together):
            index = outer * together + inner
            for part in range(chunks):
                chunk = jnp.bitwise_xor(node_ref[0], index) * chunks + part
                swing = swing_of(loadings, factors_ref[index, part * width : (part + 1) * width, :])
                swing_ref[chunk] = swing
                drop_ref[chunk] = apply_first(matrix, swing)


def volts_kernel(matrix_ref, swing_ref, drop_ref, head_ref, real_ref, imag_ref, out_ref, sems):
    n = swing_ref.shape[1]
    chunks, width = swing_ref.shape[0], swing_ref.shape[2]
    matrix = matrix_ref[0 : 2 * n, :]
    drops = [None] * chunks
    copies = []

    def advance(chunk, sweep):
        drop = drop_ref[chunk] if sweep == 0 else drops[chunk]
        real = head_ref[chunk, 2 * sweep : 2 * sweep + 1, :] - drop[:n]
        imag = head_ref[chunk, 2 * sweep + 1 : 2 * sweep + 2, :] - drop[n:]
        if sweep < SWEEPS - 1:
            drops[chunk] = apply(matrix, scaled_volts(swing_ref[chunk], real, imag))
            return
        rows = slice(chunk * width, (chunk + 1) * width)
        for index, (part, to_ref) in enumerate(((real, real_ref), (imag, imag_ref))):
            out_ref[index, rows, :] = part.T
            copies.append(pltpu.make_async_copy(out_ref.at[index, rows, :], to_ref.at[rows, :], sems.at[index, chunk]))
            copies[-1].start()

    for turn in range(chunks + SWEEPS - 1):
        for sweep in reversed(range(SWEEPS)):
            if 0 <= turn - sweep < chunks:
                advance(turn - sweep, sweep)
    for copy in copies:
        copy.wait()


def after_kernel(*refs):
    del refs


def after(array, *others):
    return pl.pallas_call(
        after_kernel,
        out_shape=jax.ShapeDtypeStruct(array.shape, array.dtype),
        in_specs=[ANY] * (1 + len(others)),
        out_specs=ANY,
        input_output_aliases={0: 0},
        compiler_params=limit(0),
        name="after",
    )(array, *others)


def in_hbm(*arrays):
    return [pltpu.with_memory_space_constraint(array, pltpu.HBM) for array in arrays]


def limit(nbytes):
    return pltpu.CompilerParams(vmem_limit_bytes=min(60 << 20, int(nbytes) + (16 << 20)))


def local(feeders, nodes, factors, loadings, parents, load_base, lateral_z, trunk_z):
    node = lax.axis_index("node").astype(jnp.int32)
    feeder = lax.axis_index("feeder").astype(jnp.int32)
    rows, rank = factors.shape
    scen = rows * nodes
    n = loadings.shape[0]
    width = max(scen // feeders, LANES)
    share = feeders * width // scen
    f32, bf16 = jnp.float32, jnp.bfloat16
    matrix_shape = (2 * n + EXTRA, 4 * n)

    def trade(block, offset):
        return lax.ppermute(block, "node", [(i, i ^ offset) for i in range(nodes)])

    held = {0: factors}
    far = nodes // 2
    if far:
        held[far] = trade(factors, far)

    packed = pl.pallas_call(
        pack_kernel,
        out_shape=jax.ShapeDtypeStruct((n + EXTRA, rank), bf16),
        in_specs=[HBM] * 5,
        out_specs=VMEM,
        scratch_shapes=[
            pltpu.SMEM((2,), f32),
            pltpu.VMEM((n, rank), bf16),
            pltpu.VMEM((1, n), jnp.int32),
            pltpu.VMEM((2, 2, n), f32),
            pltpu.VMEM((EXTRA, rank), f32),
            pltpu.SemaphoreType.DMA((5,)),
        ],
        compiler_params=limit(2 * (n + EXTRA) * rank * 2),
        name="pack",
    )(*in_hbm(trunk_z.reshape(2), loadings, parents.reshape(1, n), load_base, lateral_z))

    def swap(block, offset):
        return lax.ppermute(block, "feeder", [(i, i ^ offset) for i in range(feeders)])

    every = {0: packed}
    for offset in sorted(range(2, feeders, 2), key=lambda o: -(o & -o)):
        every[offset] = swap(packed, offset)
    every[1] = swap(packed, 1)
    slots = list(every)
    early = len(slots)
    middle = [3] if 2 in every else []
    for offset in middle:
        every[offset] = swap(every[1], offset ^ 1)
    for offset in slots[1:-1]:
        if offset + 1 not in every:
            every[offset + 1] = swap(every[offset], 1)
    slots = list(every)

    if far:
        held[far] = after(held[far], *(every[slot] for slot in slots[:early]))
    step = far // 2
    while step >= 1:
        for offset in list(held):
            held[offset ^ step] = trade(held[offset], step)
        step //= 2
    pieces = [held[offset] for offset in range(nodes)]

    start = (feeder // share) * width
    place = jnp.stack([(start // rows) ^ node, start % rows, feeder])

    def states(count):
        return [
            ((count, *matrix_shape), bf16),
            ((count, n, width), f32),
            ((count, 2 * n, width), f32),
            ((count, EXTRA, width), f32),
        ]

    state_bytes = (2 * n + EXTRA) * 8 * n + (3 * n + EXTRA) * width * 4 + (n + EXTRA) * rank * 2
    block, own, kept, *started = pl.pallas_call(
        functools.partial(early_kernel, nodes),
        out_shape=[
            jax.ShapeDtypeStruct((width, rank), bf16),
            jax.ShapeDtypeStruct(matrix_shape, bf16),
            pltpu.HBM((nodes - 1, rows, rank), bf16),
        ]
        + [jax.ShapeDtypeStruct(*state) for state in states(early)],
        in_specs=[SMEM, HBM] + [ANY] * (nodes - 1) + [VMEM] * early,
        out_specs=[VMEM, VMEM, HBM] + [VMEM] * 4,
        scratch_shapes=[pltpu.SemaphoreType.DMA, pltpu.SemaphoreType.DMA((nodes - 1,))],
        compiler_params=limit(early * state_bytes),
        cost_estimate=pl.CostEstimate(flops=early * (1 << 29), bytes_accessed=early * state_bytes, transcendentals=early * n * width),
        name="early",
    )(place, *in_hbm(pieces[0]), *pieces[1:], *(every[slot] for slot in slots[:early]))
    counts = [early]
    if middle:
        counts.append(len(middle))
        started += pl.pallas_call(
            between_kernel,
            out_shape=[jax.ShapeDtypeStruct(*state) for state in states(len(middle))],
            in_specs=[VMEM] * (1 + len(middle)),
            out_specs=[VMEM] * 4,
            compiler_params=limit(len(middle) * state_bytes),
            cost_estimate=pl.CostEstimate(flops=1 << 20, bytes_accessed=1 << 10, transcendentals=0),
            name="between",
        )(block, *(every[slot] for slot in middle))
    late = feeders - sum(counts)
    heads = pl.pallas_call(
        functools.partial(heads_kernel, slots, counts),
        out_shape=pltpu.VMEM((feeders, 8, width), f32),
        in_specs=[SMEM] + [VMEM] * (1 + feeders + len(started)),
        out_specs=VMEM,
        scratch_shapes=[pltpu.VMEM(*state) for state in states(max(late, 1))[:3]]
        + [
            pltpu.VMEM((feeders, 2 * n, width), f32),
            pltpu.VMEM((feeders, 8, width), f32),
            pltpu.VMEM((feeders, 8, width), f32),
        ],
        compiler_params=limit(feeders * state_bytes + feeders * (2 * n + 16) * width * 4),
        name="heads",
    )(place, block, *(every[slot] for slot in slots), *started)
    given = lax.all_to_all(heads, "feeder", 0, 0, tiled=True)
    given = given[::share]

    chunks = scen // width
    swing, drop = pl.pallas_call(
        first_kernel,
        out_shape=(
            jax.ShapeDtypeStruct((chunks, n, width), f32),
            jax.ShapeDtypeStruct((chunks, 2 * n, width), f32),
        ),
        in_specs=[SMEM, VMEM, HBM, HBM, HBM],
        out_specs=(VMEM, VMEM),
        scratch_shapes=[
            pltpu.VMEM((n, rank), bf16),
            pltpu.VMEM((nodes, rows, rank), bf16),
            pltpu.SemaphoreType.DMA((nodes + 1,)),
        ],
        compiler_params=limit(3 * n * scen * 4 + scen * rank * 2),
        cost_estimate=pl.CostEstimate(flops=2 * scen * n * rank * 4, bytes_accessed=3 * n * scen * 4, transcendentals=scen * n),
        name="first",
    )(node.reshape(1), own, *in_hbm(loadings, factors, kept))
    return pl.pallas_call(
        volts_kernel,
        out_shape=(
            jax.ShapeDtypeStruct((scen, n), f32),
            jax.ShapeDtypeStruct((scen, n), f32),
        ),
        in_specs=[VMEM] * 4,
        out_specs=(HBM, HBM),
        scratch_shapes=[pltpu.VMEM((2, scen, n), f32), pltpu.SemaphoreType.DMA((2, chunks))],
        compiler_params=limit(5 * n * scen * 4),
        name="volts",
    )(own, swing, drop, given)


def solution(mesh):
    feeders = mesh.shape["feeder"]
    nodes = mesh.shape["node"]
    return jax.shard_map(
        functools.partial(local, feeders, nodes),
        mesh=mesh,
        in_specs=(
            P("node", None),
            P(("feeder", "node"), None),
            P(("feeder", "node")),
            P(None, ("feeder", "node")),
            P(None, ("feeder", "node")),
            P(None, "feeder", "node"),
        ),
        out_specs=(P(None, ("feeder", "node")), P(None, ("feeder", "node"))),
        check_vma=False,
    )
```

```python
import functools

import jax
import jax.numpy as jnp
from jax import lax
from jax.experimental import pallas as pl
from jax.experimental.pallas import tpu as pltpu
from jax.sharding import PartitionSpec as P

SWEEPS = 3
EXTRA = 16
LANES = 128

VMEM = pl.BlockSpec(memory_space=pltpu.VMEM)
SMEM = pl.BlockSpec(memory_space=pltpu.SMEM)
HBM = pl.BlockSpec(memory_space=pltpu.HBM)
ANY = pl.BlockSpec(memory_space=pl.ANY)


def split(x):
    high = x.astype(jnp.bfloat16)
    low = (x - high.astype(jnp.float32)).astype(jnp.bfloat16)
    return high, low


def product(left, right):
    return jnp.dot(left, right, preferred_element_type=jnp.float32)


def product_nt(left, right):
    return lax.dot_general(left, right, (((1,), (1,)), ((), ())), preferred_element_type=jnp.float32)


def wide(row, width):
    n = row.shape[1]
    if width <= n:
        return row[:, :width]
    return jnp.concatenate([row] * (width // n), axis=1)


def pack_kernel(
    trunk_ref, loadings_ref, parents_ref, base_ref, z_ref, out_ref, trunk, loads, owners, rows_ref, meta_ref, sems
):
    n = loadings_ref.shape[0]
    copies = [
        pltpu.make_async_copy(loadings_ref, loads, sems.at[0]),
        pltpu.make_async_copy(parents_ref, owners, sems.at[1]),
        pltpu.make_async_copy(base_ref, rows_ref.at[0], sems.at[2]),
        pltpu.make_async_copy(z_ref, rows_ref.at[1], sems.at[3]),
        pltpu.make_async_copy(trunk_ref, trunk, sems.at[4]),
    ]
    for copy in copies:
        copy.start()
    for copy in copies[1:]:
        copy.wait()
    pair_ids = lax.broadcasted_iota(jnp.int32, (2, n), 0)
    trunk_rows = jnp.where(pair_ids == 0, trunk[0], trunk[1])
    for index, rows in enumerate((rows_ref[0], rows_ref[1], trunk_rows)):
        high = rows.astype(jnp.bfloat16).astype(jnp.float32)
        middle = (rows - high).astype(jnp.bfloat16).astype(jnp.float32)
        meta_ref[2 * index : 2 * index + 2, 0:n] = high
        meta_ref[2 * index : 2 * index + 2, n : 2 * n] = middle
        meta_ref[8 + 2 * index : 10 + 2 * index, 0:n] = rows - high - middle
    meta_ref[6:8, 0:n] = jnp.broadcast_to(owners[...].astype(jnp.float32), (2, n))
    meta_ref[6:8, n : 2 * n] = jnp.zeros((2, n), jnp.float32)
    meta_ref[14:16, 0:n] = jnp.zeros((2, n), jnp.float32)
    meta_ref[8:16, n : 2 * n] = jnp.zeros((8, n), jnp.float32)
    meta = meta_ref[...].astype(jnp.bfloat16)
    copies[0].wait()
    out_ref[0:n, :] = loads[...]
    out_ref[n : n + EXTRA, :] = meta


def constants(section_ref, n):
    meta = section_ref[n : n + EXTRA, :].astype(jnp.float32)
    high, middle = meta[0:8, 0:n], meta[0:8, n : 2 * n]
    return high, middle, high + middle + meta[8:16, 0:n]


def matrix_steps(sections, n):
    highs, middles, rows = zip(*(constants(section, n) for section in sections))
    row_ids = lax.broadcasted_iota(jnp.int32, (n, n), 0)
    lane_ids = lax.broadcasted_iota(jnp.int32, (n, n), 1)
    section_ids = lax.broadcasted_iota(jnp.int32, (max(8, len(sections)), n), 0)
    stacked = jnp.full(section_ids.shape, -1, jnp.int32)
    for index, row in enumerate(rows):
        stacked = jnp.where(section_ids == index, row[6:7].astype(jnp.int32), stacked)
    known = {1: stacked}

    def ancestor(distance):
        if distance not in known:
            step = 1 << (distance.bit_length() - 1)
            if step == distance:
                step //= 2
            far, near = ancestor(step), ancestor(distance - step)
            known[distance] = jnp.where(near < 0, -1, jnp.take_along_axis(far, jnp.maximum(near, 0), axis=1))
        return known[distance]

    digits = []
    unit = 1
    while unit < n:
        digits.append([ancestor(unit * digit).astype(jnp.float32) for digit in range(1, 8) if unit * digit < n])
        unit *= 8
    last = [found.T for found in digits.pop()]
    yield None

    rows_b, lanes_b = (ids.astype(jnp.float32).astype(jnp.bfloat16) for ids in (row_ids, lane_ids))
    one, zero = jnp.ones((n, n), jnp.bfloat16), jnp.zeros((n, n), jnp.bfloat16)
    identity = jnp.where(rows_b == lanes_b, one, zero)
    products = [None] * len(sections)
    for index in range(len(sections)):
        for digit in digits:
            factor = identity
            for found in digit:
                row = jnp.broadcast_to(found[index : index + 1, :].astype(jnp.bfloat16), (n, n))
                factor = jnp.where(rows_b == row, one, factor)
            done = products[index]
            products[index] = factor if done is None else product(done, factor).astype(jnp.bfloat16)
    yield None

    paths = []
    for index in range(len(sections)):
        factor = identity
        for found in last:
            column = jnp.broadcast_to(found[:, index : index + 1], (n, n)).astype(jnp.bfloat16)
            factor = jnp.where(lanes_b == column, one, factor)
        paths.append(product_nt(factor, products[index]).astype(jnp.bfloat16))
    yield None

    shared = []
    for path, high, middle in zip(paths, highs, middles):
        wide_path = path.astype(jnp.float32)

        def scaled(index):
            return jnp.concatenate([wide_path * high[index : index + 1], wide_path * middle[index : index + 1]], axis=1)

        left = jnp.concatenate([scaled(2), scaled(3)], axis=0).astype(jnp.bfloat16)
        shared.append(product_nt(left, jnp.concatenate([path, path], axis=1)))
    yield None

    pad_ids = lax.broadcasted_iota(jnp.int32, (EXTRA, 2 * n), 0)
    out = []
    for both, row in zip(shared, rows):
        resist, react = both[:n], both[n:]
        base_active, base_reactive = row[0:1], row[1:2]
        real_high, real_low = split(resist * base_active + react * base_reactive)
        imag_high, imag_low = split(react * base_active - resist * base_reactive)
        row_real = jnp.concatenate([base_active, base_reactive], axis=1)
        row_imag = jnp.concatenate([-base_reactive, base_active], axis=1)
        sums_high, sums_low = split(jnp.where(pad_ids == 0, row_real, jnp.where(pad_ids == 1, row_imag, 0.0)))

        def whole(real_part, imag_part, sums_part):
            top = jnp.concatenate([real_part, -imag_part], axis=1)
            bottom = jnp.concatenate([imag_part, real_part], axis=1)
            return jnp.concatenate([top, bottom, sums_part], axis=0)

        out.append(
            jnp.concatenate(
                [whole(real_high, imag_high, sums_high), whole(real_low, imag_low, sums_low)], axis=1
            )
        )
    yield out


def swing_of(loadings, factors):
    level = product_nt(loadings, factors).astype(jnp.bfloat16).astype(jnp.float32)
    return 1.0 + 0.5 * jnp.tanh(level)


def apply(matrix, u):
    span = matrix.shape[1] // 2
    high, low = split(u)
    left = jnp.concatenate([matrix, matrix[:, :span]], axis=1)
    return product(left, jnp.concatenate([high, high, low], axis=0))


def apply_first(matrix, swing):
    n = matrix.shape[1] // 4
    high, low = split(swing)
    high_part, low_part = matrix[:, :n], matrix[:, 2 * n : 3 * n]
    return product(
        jnp.concatenate([high_part, low_part, high_part], axis=1), jnp.concatenate([high, high, low], axis=0)
    )


def inverse_of(swing, real, imag):
    return swing * pltpu.reciprocal(real * real + imag * imag, approx=True)


def scaled_volts(swing, real, imag):
    inverse = inverse_of(swing, real, imag)
    return jnp.concatenate([real * inverse, imag * inverse], axis=0)


def first_sweep(sections, factors_ref, matrix_ref, swing_ref, drop_ref, inject_ref, arrived=None):
    n = swing_ref.shape[1]
    for start in range(0, len(sections), 8):
        group = list(enumerate(sections))[start : start + 8]
        steps = matrix_steps([section for _, section in group], n)
        next(steps)
        if start == 0 and arrived is not None:
            arrived()
        for slot, section in group:
            swing_ref[slot] = swing_of(section[0:n, :], factors_ref[...])
        *_, matrices = steps
        for (slot, _), matrix in zip(group, matrices):
            matrix_ref[slot] = matrix
            out = apply_first(matrix_ref[slot], swing_ref[slot])
            drop_ref[slot] = out[: 2 * n]
            inject_ref[slot] = out[2 * n :]


def between_kernel(factors_ref, *refs):
    first_sweep(refs[:-4], factors_ref, *refs[-4:])


def early_kernel(pieces, place_ref, *refs):
    piece_refs, sections = refs[:pieces], refs[pieces:-9]
    factors_ref, own_ref, kept_ref, matrix_ref, swing_ref, drop_ref, inject_ref, sem, keep_sems = refs[-9:]
    width = factors_ref.shape[0]
    piece, offset = place_ref[0], place_ref[1]
    keeps = [
        pltpu.make_async_copy(piece_ref, kept_ref.at[index], keep_sems.at[index])
        for index, piece_ref in enumerate(piece_refs[1:])
    ]
    for copy in keeps:
        copy.start()
    for index, piece_ref in enumerate(piece_refs):
        @pl.when(piece == index)
        def _(piece_ref=piece_ref):
            rows = piece_ref.at[pl.ds(pl.multiple_of(offset, width), width), :]
            pltpu.make_async_copy(rows, factors_ref, sem).start()

    def arrived():
        pltpu.make_async_copy(piece_refs[0].at[0:width, :], factors_ref, sem).wait()

    first_sweep(sections, factors_ref, matrix_ref, swing_ref, drop_ref, inject_ref, arrived)
    own_ref[...] = matrix_ref[0]
    for copy in keeps:
        copy.wait()


def heads_kernel(slots, counts, place_ref, factors_ref, *refs):
    feeders, early = len(slots), sum(counts)
    sections, refs = refs[:feeders], refs[feeders:]
    done = []
    for count in counts:
        done += [[ref.at[index] for ref in refs[:4]] for index in range(count)]
        refs = refs[4:]
    head_ref, matrix_ref, swing_ref, drop_ref, again_ref, flow_ref, trunk_ref = refs
    width = factors_ref.shape[0]
    n = swing_ref.shape[1]
    place = [jnp.bitwise_xor(place_ref[2], slot) for slot in slots]
    late_refs = (matrix_ref, swing_ref, drop_ref)

    def of(index, which):
        return done[index][which] if index < early else late_refs[which].at[index - early]

    def flow_of(index, real, imag):
        base = constants(sections[index], n)[2].T
        active, reactive = base[:, 0:1], base[:, 1:2]
        if imag is None:
            parts = (active * real, -reactive * real)
        else:
            parts = (active * real + reactive * imag, active * imag - reactive * real)
        return [jnp.sum(part, axis=0, keepdims=True) for part in parts]

    groups = [list(range(start, min(start + 8, feeders))) for start in range(early, feeders, 8)]
    steps = [matrix_steps([sections[index] for index in group], n) for group in groups]
    if steps:
        next(steps[0])
    for index in range(feeders):
        row = constants(sections[index], n)[2]
        trunk_ref[place[index], 0:2, :] = wide(row[4:6], width)
        if index < early:
            flow_ref[place[index]] = of(index, 3)[0:8, :]
        else:
            swing = swing_of(sections[index][0:n, :], factors_ref[...])
            of(index, 1)[...] = swing
            for part, total in enumerate(flow_of(index, swing, None)):
                flow_ref[place[index], part : part + 1, :] = total

    def heads(sweep):
        flows = [None] * feeders
        real = jnp.zeros((1, width), jnp.float32)
        imag = real
        for g in reversed(range(feeders)):
            real = real + flow_ref[g, 0:1, :]
            imag = imag + flow_ref[g, 1:2, :]
            flows[g] = (real, imag)
        head_real = jnp.ones((1, width), jnp.float32)
        head_imag = jnp.zeros((1, width), jnp.float32)
        for g in range(feeders):
            r, x = trunk_ref[g, 0:1, :], trunk_ref[g, 1:2, :]
            real, imag = flows[g]
            head_real = head_real - (r * real - x * imag)
            head_imag = head_imag - (r * imag + x * real)
            head_ref[feeders - 1 - g, 2 * sweep : 2 * sweep + 1, :] = head_real
            head_ref[feeders - 1 - g, 2 * sweep + 1 : 2 * sweep + 2, :] = head_imag

    def volts(index, sweep):
        drop = of(index, 2) if sweep == 1 else again_ref.at[index]
        rank = feeders - 1 - place[index]
        real = head_ref[rank, 2 * sweep - 2 : 2 * sweep - 1, :] - drop[0:n, :]
        imag = head_ref[rank, 2 * sweep - 1 : 2 * sweep, :] - drop[n : 2 * n, :]
        return real, imag

    def middle(index, sweep):
        out = apply(of(index, 0)[...], scaled_volts(of(index, 1)[...], *volts(index, sweep)))
        again_ref[index] = out[: 2 * n]
        flow_ref[place[index]] = out[2 * n : 2 * n + 8]

    heads(0)
    ready = list(range(early))
    for group, step in zip(groups, steps):
        for matrices in step:
            if ready:
                middle(ready.pop(0), 1)
        for index, matrix in zip(group, matrices):
            of(index, 0)[...] = matrix
            of(index, 2)[...] = apply_first(matrix, of(index, 1)[...])[: 2 * n]
    for index in ready + list(range(early, feeders)):
        middle(index, 1)
    heads(1)
    for sweep in range(2, SWEEPS):
        for index in range(feeders):
            if sweep < SWEEPS - 1:
                middle(index, sweep)
            else:
                real, imag = volts(index, sweep)
                inverse = inverse_of(of(index, 1)[...], real, imag)
                for part, total in enumerate(flow_of(index, real * inverse, imag * inverse)):
                    flow_ref[place[index], part : part + 1, :] = total
        heads(sweep)
    for g in range(feeders):
        head_ref[g, 2 * SWEEPS :, :] = jnp.zeros((head_ref.shape[1] - 2 * SWEEPS, width), jnp.float32)


def first_kernel(
    node_ref, matrix_ref, loadings_ref, rows_ref, kept_ref, swing_ref, drop_ref, loads, factors_ref, sems
):
    n = loadings_ref.shape[0]
    width = swing_ref.shape[2]
    pieces = 1 + kept_ref.shape[0]
    chunks = rows_ref.shape[0] // width
    copies = [pltpu.make_async_copy(loadings_ref, loads, sems.at[pieces])]
    for index in range(pieces):
        piece_ref = kept_ref.at[index - 1] if index else rows_ref
        copies.append(pltpu.make_async_copy(piece_ref, factors_ref.at[index], sems.at[index]))
    for copy in copies:
        copy.start()
    matrix = matrix_ref[0 : 2 * n, :]
    for copy in copies:
        copy.wait()
    loadings = loads[...]
    together = 4 // chunks if chunks < 4 else 1

    @pl.loop(0, pieces // together)
    def _(outer):
        for inner in range(together):
            index = outer * together + inner
            for part in range(chunks):
                chunk = jnp.bitwise_xor(node_ref[0], index) * chunks + part
                swing = swing_of(loadings, factors_ref[index, part * width : (part + 1) * width, :])
                swing_ref[chunk] = swing
                drop_ref[chunk] = apply_first(matrix, swing)


def volts_kernel(share, matrix_ref, swing_ref, drop_ref, head_ref, real_ref, imag_ref, out_ref, sems):
    n = swing_ref.shape[1]
    chunks, width = swing_ref.shape[0], swing_ref.shape[2]
    matrix = matrix_ref[0 : 2 * n, :]
    drops = [None] * chunks
    copies = []

    def advance(chunk, sweep):
        drop = drop_ref[chunk] if sweep == 0 else drops[chunk]
        giver = head_ref.shape[0] - 1 - chunk * share
        real = head_ref[giver, 2 * sweep : 2 * sweep + 1, :] - drop[:n]
        imag = head_ref[giver, 2 * sweep + 1 : 2 * sweep + 2, :] - drop[n:]
        if sweep < SWEEPS - 1:
            drops[chunk] = apply(matrix, scaled_volts(swing_ref[chunk], real, imag))
            return
        rows = slice(chunk * width, (chunk + 1) * width)
        for index, (part, to_ref) in enumerate(((real, real_ref), (imag, imag_ref))):
            out_ref[index, rows, :] = part.T
            copies.append(pltpu.make_async_copy(out_ref.at[index, rows, :], to_ref.at[rows, :], sems.at[index, chunk]))
            copies[-1].start()

    for turn in range(chunks + SWEEPS - 1):
        for sweep in reversed(range(SWEEPS)):
            if 0 <= turn - sweep < chunks:
                advance(turn - sweep, sweep)
    for copy in copies:
        copy.wait()


def after_kernel(*refs):
    del refs


def after(array, *others):
    return pl.pallas_call(
        after_kernel,
        out_shape=jax.ShapeDtypeStruct(array.shape, array.dtype),
        in_specs=[ANY] * (1 + len(others)),
        out_specs=ANY,
        input_output_aliases={0: 0},
        compiler_params=limit(0),
        name="after",
    )(array, *others)


def in_hbm(*arrays):
    return [pltpu.with_memory_space_constraint(array, pltpu.HBM) for array in arrays]


def limit(nbytes):
    return pltpu.CompilerParams(vmem_limit_bytes=min(60 << 20, int(nbytes) + (16 << 20)))


def local(feeders, nodes, factors, loadings, parents, load_base, lateral_z, trunk_z):
    node = lax.axis_index("node").astype(jnp.int32)
    feeder = lax.axis_index("feeder").astype(jnp.int32)
    rows, rank = factors.shape
    scen = rows * nodes
    n = loadings.shape[0]
    width = max(scen // feeders, LANES)
    share = feeders * width // scen
    f32, bf16 = jnp.float32, jnp.bfloat16
    matrix_shape = (2 * n + EXTRA, 4 * n)

    def trade(block, offset):
        return lax.ppermute(block, "node", [(i, i ^ offset) for i in range(nodes)])

    held = {0: factors}
    far = nodes // 2
    if far:
        held[far] = trade(factors, far)

    packed = pl.pallas_call(
        pack_kernel,
        out_shape=jax.ShapeDtypeStruct((n + EXTRA, rank), bf16),
        in_specs=[HBM] * 5,
        out_specs=VMEM,
        scratch_shapes=[
            pltpu.SMEM((2,), f32),
            pltpu.VMEM((n, rank), bf16),
            pltpu.VMEM((1, n), jnp.int32),
            pltpu.VMEM((2, 2, n), f32),
            pltpu.VMEM((EXTRA, rank), f32),
            pltpu.SemaphoreType.DMA((5,)),
        ],
        compiler_params=limit(2 * (n + EXTRA) * rank * 2),
        name="pack",
    )(*in_hbm(trunk_z.reshape(2), loadings, parents.reshape(1, n), load_base, lateral_z))

    def swap(block, offset):
        return lax.ppermute(block, "feeder", [(i, i ^ offset) for i in range(feeders)])

    every = {0: packed}
    for offset in sorted(range(2, feeders, 2), key=lambda o: -(o & -o)):
        every[offset] = swap(packed, offset)
    every[1] = swap(packed, 1)
    slots = list(every)
    early = len(slots)
    middle = [3] if 2 in every else []
    for offset in middle:
        every[offset] = swap(every[1], offset ^ 1)
    for offset in slots[1:-1]:
        if offset + 1 not in every:
            every[offset + 1] = swap(every[offset], 1)
    slots = list(every)

    if far:
        held[far] = after(held[far], *(every[slot] for slot in slots[:early]))
    step = far // 2
    while step >= 1:
        for offset in list(held):
            held[offset ^ step] = trade(held[offset], step)
        step //= 2
    pieces = [held[offset] for offset in range(nodes)]

    start = (feeder // share) * width
    place = jnp.stack([(start // rows) ^ node, start % rows, feeder])

    def states(count):
        return [
            ((count, *matrix_shape), bf16),
            ((count, n, width), f32),
            ((count, 2 * n, width), f32),
            ((count, EXTRA, width), f32),
        ]

    state_bytes = (2 * n + EXTRA) * 8 * n + (3 * n + EXTRA) * width * 4 + (n + EXTRA) * rank * 2
    block, own, kept, *started = pl.pallas_call(
        functools.partial(early_kernel, nodes),
        out_shape=[
            jax.ShapeDtypeStruct((width, rank), bf16),
            jax.ShapeDtypeStruct(matrix_shape, bf16),
            pltpu.HBM((nodes - 1, rows, rank), bf16),
        ]
        + [jax.ShapeDtypeStruct(*state) for state in states(early)],
        in_specs=[SMEM, HBM] + [ANY] * (nodes - 1) + [VMEM] * early,
        out_specs=[VMEM, VMEM, HBM] + [VMEM] * 4,
        scratch_shapes=[pltpu.SemaphoreType.DMA, pltpu.SemaphoreType.DMA((nodes - 1,))],
        compiler_params=limit(early * state_bytes),
        cost_estimate=pl.CostEstimate(flops=early * (1 << 29), bytes_accessed=early * state_bytes, transcendentals=early * n * width),
        name="early",
    )(place, *in_hbm(pieces[0]), *pieces[1:], *(every[slot] for slot in slots[:early]))
    counts = [early]
    if middle:
        counts.append(len(middle))
        started += pl.pallas_call(
            between_kernel,
            out_shape=[jax.ShapeDtypeStruct(*state) for state in states(len(middle))],
            in_specs=[VMEM] * (1 + len(middle)),
            out_specs=[VMEM] * 4,
            compiler_params=limit(len(middle) * state_bytes),
            cost_estimate=pl.CostEstimate(flops=1 << 20, bytes_accessed=1 << 10, transcendentals=0),
            name="between",
        )(block, *(every[slot] for slot in middle))
    late = feeders - sum(counts)
    heads = pl.pallas_call(
        functools.partial(heads_kernel, slots, counts),
        out_shape=jax.ShapeDtypeStruct((feeders, 8, width), f32),
        in_specs=[SMEM] + [VMEM] * (1 + feeders + len(started)),
        out_specs=VMEM,
        scratch_shapes=[pltpu.VMEM(*state) for state in states(max(late, 1))[:3]]
        + [
            pltpu.VMEM((feeders, 2 * n, width), f32),
            pltpu.VMEM((feeders, 8, width), f32),
            pltpu.VMEM((feeders, 8, width), f32),
        ],
        compiler_params=limit(feeders * state_bytes + feeders * (2 * n + 16) * width * 4),
        name="heads",
    )(place, block, *(every[slot] for slot in slots), *started)
    given = lax.all_to_all(heads, "feeder", 0, 0, axis_index_groups=[list(range(feeders))[::-1]], tiled=True)

    chunks = scen // width
    swing, drop = pl.pallas_call(
        first_kernel,
        out_shape=(
            jax.ShapeDtypeStruct((chunks, n, width), f32),
            jax.ShapeDtypeStruct((chunks, 2 * n, width), f32),
        ),
        in_specs=[SMEM, VMEM, HBM, HBM, HBM],
        out_specs=(VMEM, VMEM),
        scratch_shapes=[
            pltpu.VMEM((n, rank), bf16),
            pltpu.VMEM((nodes, rows, rank), bf16),
            pltpu.SemaphoreType.DMA((nodes + 1,)),
        ],
        compiler_params=limit(3 * n * scen * 4 + scen * rank * 2),
        cost_estimate=pl.CostEstimate(flops=2 * scen * n * rank * 4, bytes_accessed=3 * n * scen * 4, transcendentals=scen * n),
        name="first",
    )(node.reshape(1), own, *in_hbm(loadings, factors, kept))
    return pl.pallas_call(
        functools.partial(volts_kernel, share),
        out_shape=(
            jax.ShapeDtypeStruct((scen, n), f32),
            jax.ShapeDtypeStruct((scen, n), f32),
        ),
        in_specs=[VMEM] * 4,
        out_specs=(HBM, HBM),
        scratch_shapes=[pltpu.VMEM((2, scen, n), f32), pltpu.SemaphoreType.DMA((2, chunks))],
        compiler_params=limit(5 * n * scen * 4),
        name="volts",
    )(own, swing, drop, given)


def solution(mesh):
    feeders = mesh.shape["feeder"]
    nodes = mesh.shape["node"]
    return jax.shard_map(
        functools.partial(local, feeders, nodes),
        mesh=mesh,
        in_specs=(
            P("node", None),
            P(("feeder", "node"), None),
            P(("feeder", "node")),
            P(None, ("feeder", "node")),
            P(None, ("feeder", "node")),
            P(None, "feeder", "node"),
        ),
        out_specs=(P(None, ("feeder", "node")), P(None, ("feeder", "node"))),
        check_vma=False,
    )
```

```python
import functools

import jax
import jax.numpy as jnp
from jax import lax
from jax.experimental import pallas as pl
from jax.experimental.pallas import tpu as pltpu
from jax.sharding import PartitionSpec as P

SWEEPS = 3
EXTRA = 16
LANES = 128

VMEM = pl.BlockSpec(memory_space=pltpu.VMEM)
SMEM = pl.BlockSpec(memory_space=pltpu.SMEM)
HBM = pl.BlockSpec(memory_space=pltpu.HBM)
ANY = pl.BlockSpec(memory_space=pl.ANY)


def split(x):
    high = x.astype(jnp.bfloat16)
    low = (x - high.astype(jnp.float32)).astype(jnp.bfloat16)
    return high, low


def product(left, right):
    return jnp.dot(left, right, preferred_element_type=jnp.float32)


def product_nt(left, right):
    return lax.dot_general(left, right, (((1,), (1,)), ((), ())), preferred_element_type=jnp.float32)


def wide(row, width):
    n = row.shape[1]
    if width <= n:
        return row[:, :width]
    return jnp.concatenate([row] * (width // n), axis=1)


def pack_kernel(
    trunk_ref, loadings_ref, parents_ref, base_ref, z_ref, out_ref, trunk, loads, owners, rows_ref, meta_ref, sems
):
    n = loadings_ref.shape[0]
    copies = [
        pltpu.make_async_copy(loadings_ref, loads, sems.at[0]),
        pltpu.make_async_copy(parents_ref, owners, sems.at[1]),
        pltpu.make_async_copy(base_ref, rows_ref.at[0], sems.at[2]),
        pltpu.make_async_copy(z_ref, rows_ref.at[1], sems.at[3]),
        pltpu.make_async_copy(trunk_ref, trunk, sems.at[4]),
    ]
    for copy in copies:
        copy.start()
    for copy in copies[1:]:
        copy.wait()
    pair_ids = lax.broadcasted_iota(jnp.int32, (2, n), 0)
    trunk_rows = jnp.where(pair_ids == 0, trunk[0], trunk[1])
    for index, rows in enumerate((rows_ref[0], rows_ref[1], trunk_rows)):
        high = rows.astype(jnp.bfloat16).astype(jnp.float32)
        middle = (rows - high).astype(jnp.bfloat16).astype(jnp.float32)
        meta_ref[2 * index : 2 * index + 2, 0:n] = high
        meta_ref[2 * index : 2 * index + 2, n : 2 * n] = middle
        meta_ref[8 + 2 * index : 10 + 2 * index, 0:n] = rows - high - middle
    meta_ref[6:8, 0:n] = jnp.broadcast_to(owners[...].astype(jnp.float32), (2, n))
    meta_ref[6:8, n : 2 * n] = jnp.zeros((2, n), jnp.float32)
    meta_ref[14:16, 0:n] = jnp.zeros((2, n), jnp.float32)
    meta_ref[8:16, n : 2 * n] = jnp.zeros((8, n), jnp.float32)
    meta = meta_ref[...].astype(jnp.bfloat16)
    copies[0].wait()
    out_ref[0:n, :] = loads[...]
    out_ref[n : n + EXTRA, :] = meta


def constants(section_ref, n):
    meta = section_ref[n : n + EXTRA, :].astype(jnp.float32)
    high, middle = meta[0:8, 0:n], meta[0:8, n : 2 * n]
    return high, middle, high + middle + meta[8:16, 0:n]


def matrix_steps(sections, n):
    highs, middles, rows = zip(*(constants(section, n) for section in sections))
    row_ids = lax.broadcasted_iota(jnp.int32, (n, n), 0)
    lane_ids = lax.broadcasted_iota(jnp.int32, (n, n), 1)
    section_ids = lax.broadcasted_iota(jnp.int32, (max(8, len(sections)), n), 0)
    stacked = jnp.full(section_ids.shape, -1, jnp.int32)
    for index, row in enumerate(rows):
        stacked = jnp.where(section_ids == index, row[6:7].astype(jnp.int32), stacked)
    known = {1: stacked}

    def ancestor(distance):
        if distance not in known:
            step = 1 << (distance.bit_length() - 1)
            if step == distance:
                step //= 2
            far, near = ancestor(step), ancestor(distance - step)
            known[distance] = jnp.where(near < 0, -1, jnp.take_along_axis(far, jnp.maximum(near, 0), axis=1))
        return known[distance]

    digits = []
    unit = 1
    while unit < n:
        digits.append([ancestor(unit * digit).astype(jnp.float32) for digit in range(1, 8) if unit * digit < n])
        unit *= 8
    last = [found.T for found in digits.pop()]
    yield None

    rows_b, lanes_b = (ids.astype(jnp.float32).astype(jnp.bfloat16) for ids in (row_ids, lane_ids))
    one, zero = jnp.ones((n, n), jnp.bfloat16), jnp.zeros((n, n), jnp.bfloat16)
    identity = jnp.where(rows_b == lanes_b, one, zero)
    products = [None] * len(sections)
    for index in range(len(sections)):
        for digit in digits:
            factor = identity
            for found in digit:
                row = jnp.broadcast_to(found[index : index + 1, :].astype(jnp.bfloat16), (n, n))
                factor = jnp.where(rows_b == row, one, factor)
            done = products[index]
            products[index] = factor if done is None else product(done, factor).astype(jnp.bfloat16)
    yield None

    paths = []
    for index in range(len(sections)):
        factor = identity
        for found in last:
            column = jnp.broadcast_to(found[:, index : index + 1], (n, n)).astype(jnp.bfloat16)
            factor = jnp.where(lanes_b == column, one, factor)
        paths.append(product_nt(factor, products[index]).astype(jnp.bfloat16))
    yield None

    shared = []
    for path, high, middle in zip(paths, highs, middles):
        wide_path = path.astype(jnp.float32)

        def scaled(index):
            return jnp.concatenate([wide_path * high[index : index + 1], wide_path * middle[index : index + 1]], axis=1)

        left = jnp.concatenate([scaled(2), scaled(3)], axis=0).astype(jnp.bfloat16)
        shared.append(product_nt(left, jnp.concatenate([path, path], axis=1)))
    yield None

    pad_ids = lax.broadcasted_iota(jnp.int32, (EXTRA, 2 * n), 0)
    out = []
    for both, row in zip(shared, rows):
        resist, react = both[:n], both[n:]
        base_active, base_reactive = row[0:1], row[1:2]
        real_high, real_low = split(resist * base_active + react * base_reactive)
        imag_high, imag_low = split(react * base_active - resist * base_reactive)
        row_real = jnp.concatenate([base_active, base_reactive], axis=1)
        row_imag = jnp.concatenate([-base_reactive, base_active], axis=1)
        sums_high, sums_low = split(jnp.where(pad_ids == 0, row_real, jnp.where(pad_ids == 1, row_imag, 0.0)))

        def whole(real_part, imag_part, sums_part):
            top = jnp.concatenate([real_part, -imag_part], axis=1)
            bottom = jnp.concatenate([imag_part, real_part], axis=1)
            return jnp.concatenate([top, bottom, sums_part], axis=0)

        out.append(
            jnp.concatenate(
                [whole(real_high, imag_high, sums_high), whole(real_low, imag_low, sums_low)], axis=1
            )
        )
    yield out


def stagger(count, steps):
    for turn in range(count + len(steps) - 1):
        for depth in reversed(range(len(steps))):
            if 0 <= turn - depth < count:
                steps[depth](turn - depth)


def swing_of(loadings, factors):
    level = product_nt(loadings, factors).astype(jnp.bfloat16).astype(jnp.float32)
    return 1.0 + 0.5 * jnp.tanh(level)


def apply(matrix, u):
    span = matrix.shape[1] // 2
    high, low = split(u)
    left = jnp.concatenate([matrix, matrix[:, :span]], axis=1)
    return product(left, jnp.concatenate([high, high, low], axis=0))


def apply_first(matrix, swing):
    n = matrix.shape[1] // 4
    high, low = split(swing)
    high_part, low_part = matrix[:, :n], matrix[:, 2 * n : 3 * n]
    return product(
        jnp.concatenate([high_part, low_part, high_part], axis=1), jnp.concatenate([high, high, low], axis=0)
    )


def inverse_of(swing, real, imag):
    return swing * pltpu.reciprocal(real * real + imag * imag, approx=True)


def scaled_volts(swing, real, imag):
    inverse = inverse_of(swing, real, imag)
    return jnp.concatenate([real * inverse, imag * inverse], axis=0)


def first_sweep(sections, factors_ref, matrix_ref, swing_ref, drop_ref, inject_ref, arrived=None):
    n = swing_ref.shape[1]
    for start in range(0, len(sections), 8):
        group = list(enumerate(sections))[start : start + 8]
        steps = matrix_steps([section for _, section in group], n)
        next(steps)
        if start == 0 and arrived is not None:
            arrived()
        for slot, section in group:
            swing_ref[slot] = swing_of(section[0:n, :], factors_ref[...])
        *_, matrices = steps
        for (slot, _), matrix in zip(group, matrices):
            matrix_ref[slot] = matrix
            out = apply_first(matrix_ref[slot], swing_ref[slot])
            drop_ref[slot] = out[: 2 * n]
            inject_ref[slot] = out[2 * n :]


def between_kernel(factors_ref, *refs):
    first_sweep(refs[:-4], factors_ref, *refs[-4:])


def early_kernel(pieces, place_ref, *refs):
    piece_refs, sections = refs[:pieces], refs[pieces:-9]
    factors_ref, own_ref, kept_ref, matrix_ref, swing_ref, drop_ref, inject_ref, sem, keep_sems = refs[-9:]
    width = factors_ref.shape[0]
    piece, offset = place_ref[0], place_ref[1]
    keeps = [
        pltpu.make_async_copy(piece_ref, kept_ref.at[index], keep_sems.at[index])
        for index, piece_ref in enumerate(piece_refs[1:])
    ]
    for copy in keeps:
        copy.start()
    for index, piece_ref in enumerate(piece_refs):
        @pl.when(piece == index)
        def _(piece_ref=piece_ref):
            rows = piece_ref.at[pl.ds(pl.multiple_of(offset, width), width), :]
            pltpu.make_async_copy(rows, factors_ref, sem).start()

    def arrived():
        pltpu.make_async_copy(piece_refs[0].at[0:width, :], factors_ref, sem).wait()

    first_sweep(sections, factors_ref, matrix_ref, swing_ref, drop_ref, inject_ref, arrived)
    own_ref[...] = matrix_ref[0]
    for copy in keeps:
        copy.wait()


def heads_kernel(slots, counts, place_ref, factors_ref, *refs):
    feeders, early = len(slots), sum(counts)
    sections, refs = refs[:feeders], refs[feeders:]
    done = []
    for count in counts:
        done += [[ref.at[index] for ref in refs[:4]] for index in range(count)]
        refs = refs[4:]
    head_ref, matrix_ref, swing_ref, drop_ref, again_ref, flow_ref, trunk_ref = refs
    width = factors_ref.shape[0]
    n = swing_ref.shape[1]
    place = [jnp.bitwise_xor(place_ref[2], slot) for slot in slots]
    late_refs = (matrix_ref, swing_ref, drop_ref)

    def of(index, which):
        return done[index][which] if index < early else late_refs[which].at[index - early]

    def flow_of(index, real, imag):
        base = constants(sections[index], n)[2].T
        active, reactive = base[:, 0:1], base[:, 1:2]
        if imag is None:
            parts = (active * real, -reactive * real)
        else:
            parts = (active * real + reactive * imag, active * imag - reactive * real)
        return [jnp.sum(part, axis=0, keepdims=True) for part in parts]

    groups = [list(range(start, min(start + 8, feeders))) for start in range(early, feeders, 8)]
    steps = [matrix_steps([sections[index] for index in group], n) for group in groups]
    if steps:
        next(steps[0])
    for index in range(feeders):
        row = constants(sections[index], n)[2]
        trunk_ref[place[index], 0:2, :] = wide(row[4:6], width)
        if index < early:
            flow_ref[place[index]] = of(index, 3)[0:8, :]
        else:
            swing = swing_of(sections[index][0:n, :], factors_ref[...])
            of(index, 1)[...] = swing
            for part, total in enumerate(flow_of(index, swing, None)):
                flow_ref[place[index], part : part + 1, :] = total

    def heads(sweep):
        flows = [None] * feeders
        real = jnp.zeros((1, width), jnp.float32)
        imag = real
        for g in reversed(range(feeders)):
            real = real + flow_ref[g, 0:1, :]
            imag = imag + flow_ref[g, 1:2, :]
            flows[g] = (real, imag)
        head_real = jnp.ones((1, width), jnp.float32)
        head_imag = jnp.zeros((1, width), jnp.float32)
        for g in range(feeders):
            r, x = trunk_ref[g, 0:1, :], trunk_ref[g, 1:2, :]
            real, imag = flows[g]
            head_real = head_real - (r * real - x * imag)
            head_imag = head_imag - (r * imag + x * real)
            head_ref[feeders - 1 - g, 2 * sweep : 2 * sweep + 1, :] = head_real
            head_ref[feeders - 1 - g, 2 * sweep + 1 : 2 * sweep + 2, :] = head_imag

    def volts(index, sweep):
        drop = of(index, 2) if sweep == 1 else again_ref.at[index]
        rank = feeders - 1 - place[index]
        real = head_ref[rank, 2 * sweep - 2 : 2 * sweep - 1, :] - drop[0:n, :]
        imag = head_ref[rank, 2 * sweep - 1 : 2 * sweep, :] - drop[n : 2 * n, :]
        return real, imag

    def middle(index, sweep):
        out = apply(of(index, 0)[...], scaled_volts(of(index, 1)[...], *volts(index, sweep)))
        again_ref[index] = out[: 2 * n]
        flow_ref[place[index]] = out[2 * n : 2 * n + 8]

    heads(0)
    ready = list(range(early))
    for group, step in zip(groups, steps):
        for matrices in step:
            if ready:
                middle(ready.pop(0), 1)
        for index, matrix in zip(group, matrices):
            of(index, 0)[...] = matrix
            of(index, 2)[...] = apply_first(matrix, of(index, 1)[...])[: 2 * n]
    for index in ready + list(range(early, feeders)):
        middle(index, 1)
    heads(1)
    for sweep in range(2, SWEEPS):
        for index in range(feeders):
            if sweep < SWEEPS - 1:
                middle(index, sweep)
            else:
                real, imag = volts(index, sweep)
                inverse = inverse_of(of(index, 1)[...], real, imag)
                for part, total in enumerate(flow_of(index, real * inverse, imag * inverse)):
                    flow_ref[place[index], part : part + 1, :] = total
        heads(sweep)
    for g in range(feeders):
        head_ref[g, 2 * SWEEPS :, :] = jnp.zeros((head_ref.shape[1] - 2 * SWEEPS, width), jnp.float32)


def first_kernel(
    node_ref, matrix_ref, loadings_ref, rows_ref, kept_ref, swing_ref, drop_ref, loads, factors_ref, sems
):
    n = loadings_ref.shape[0]
    width = swing_ref.shape[2]
    pieces = 1 + kept_ref.shape[0]
    chunks = rows_ref.shape[0] // width
    copies = [pltpu.make_async_copy(loadings_ref, loads, sems.at[pieces])]
    for index in range(pieces):
        piece_ref = kept_ref.at[index - 1] if index else rows_ref
        copies.append(pltpu.make_async_copy(piece_ref, factors_ref.at[index], sems.at[index]))
    for copy in copies:
        copy.start()
    matrix = matrix_ref[0 : 2 * n, :]
    copies[0].wait()
    loadings = loads[...]

    def place(item):
        return jnp.bitwise_xor(node_ref[0], item // chunks) * chunks + item % chunks

    def swing_step(item):
        index, part = divmod(item, chunks)
        if part == 0:
            copies[1 + index].wait()
        swing_ref[place(item)] = swing_of(loadings, factors_ref[index, part * width : (part + 1) * width, :])

    def drop_step(item):
        drop_ref[place(item)] = apply_first(matrix, swing_ref[place(item)])

    stagger(pieces * chunks, [swing_step, drop_step])


def volts_kernel(share, matrix_ref, swing_ref, drop_ref, head_ref, real_ref, imag_ref, out_ref, sems):
    n = swing_ref.shape[1]
    chunks, width = swing_ref.shape[0], swing_ref.shape[2]
    matrix = matrix_ref[0 : 2 * n, :]
    drops = [None] * chunks
    copies = []

    def advance(chunk, sweep):
        drop = drop_ref[chunk] if sweep == 0 else drops[chunk]
        giver = head_ref.shape[0] - 1 - chunk * share
        real = head_ref[giver, 2 * sweep : 2 * sweep + 1, :] - drop[:n]
        imag = head_ref[giver, 2 * sweep + 1 : 2 * sweep + 2, :] - drop[n:]
        if sweep < SWEEPS - 1:
            drops[chunk] = apply(matrix, scaled_volts(swing_ref[chunk], real, imag))
            return
        rows = slice(chunk * width, (chunk + 1) * width)
        for index, (part, to_ref) in enumerate(((real, real_ref), (imag, imag_ref))):
            out_ref[index, rows, :] = part.T
            copies.append(pltpu.make_async_copy(out_ref.at[index, rows, :], to_ref.at[rows, :], sems.at[index, chunk]))
            copies[-1].start()

    stagger(chunks, [functools.partial(advance, sweep=sweep) for sweep in range(SWEEPS)])
    for copy in copies:
        copy.wait()


def after_kernel(*refs):
    del refs


def after(array, *others):
    return pl.pallas_call(
        after_kernel,
        out_shape=jax.ShapeDtypeStruct(array.shape, array.dtype),
        in_specs=[ANY] * (1 + len(others)),
        out_specs=ANY,
        input_output_aliases={0: 0},
        compiler_params=limit(0),
        name="after",
    )(array, *others)


def in_hbm(*arrays):
    return [pltpu.with_memory_space_constraint(array, pltpu.HBM) for array in arrays]


def limit(nbytes):
    return pltpu.CompilerParams(vmem_limit_bytes=min(60 << 20, int(nbytes) + (16 << 20)))


def local(feeders, nodes, factors, loadings, parents, load_base, lateral_z, trunk_z):
    node = lax.axis_index("node").astype(jnp.int32)
    feeder = lax.axis_index("feeder").astype(jnp.int32)
    rows, rank = factors.shape
    scen = rows * nodes
    n = loadings.shape[0]
    width = max(scen // feeders, LANES)
    share = feeders * width // scen
    f32, bf16 = jnp.float32, jnp.bfloat16
    matrix_shape = (2 * n + EXTRA, 4 * n)

    def trade(block, offset):
        return lax.ppermute(block, "node", [(i, i ^ offset) for i in range(nodes)])

    held = {0: factors}
    far = nodes // 2
    if far:
        held[far] = trade(factors, far)

    packed = pl.pallas_call(
        pack_kernel,
        out_shape=jax.ShapeDtypeStruct((n + EXTRA, rank), bf16),
        in_specs=[HBM] * 5,
        out_specs=VMEM,
        scratch_shapes=[
            pltpu.SMEM((2,), f32),
            pltpu.VMEM((n, rank), bf16),
            pltpu.VMEM((1, n), jnp.int32),
            pltpu.VMEM((2, 2, n), f32),
            pltpu.VMEM((EXTRA, rank), f32),
            pltpu.SemaphoreType.DMA((5,)),
        ],
        compiler_params=limit(2 * (n + EXTRA) * rank * 2),
        name="pack",
    )(*in_hbm(trunk_z.reshape(2), loadings, parents.reshape(1, n), load_base, lateral_z))

    def swap(block, offset):
        return lax.ppermute(block, "feeder", [(i, i ^ offset) for i in range(feeders)])

    every = {0: packed}
    for offset in sorted(range(2, feeders, 2), key=lambda o: -(o & -o)):
        every[offset] = swap(packed, offset)
    every[1] = swap(packed, 1)
    slots = list(every)
    early = len(slots)
    middle = [3] if 2 in every else []
    for offset in middle:
        every[offset] = swap(every[1], offset ^ 1)
    for offset in slots[1:-1]:
        if offset + 1 not in every:
            every[offset + 1] = swap(every[offset], 1)
    slots = list(every)

    if far:
        held[far] = after(held[far], *(every[slot] for slot in slots[:early]))
    step = far // 2
    while step >= 1:
        for offset in list(held):
            held[offset ^ step] = trade(held[offset], step)
        step //= 2
    pieces = [held[offset] for offset in range(nodes)]

    start = (feeder // share) * width
    place = jnp.stack([(start // rows) ^ node, start % rows, feeder])

    def states(count):
        return [
            ((count, *matrix_shape), bf16),
            ((count, n, width), f32),
            ((count, 2 * n, width), f32),
            ((count, EXTRA, width), f32),
        ]

    state_bytes = (2 * n + EXTRA) * 8 * n + (3 * n + EXTRA) * width * 4 + (n + EXTRA) * rank * 2
    block, own, kept, *started = pl.pallas_call(
        functools.partial(early_kernel, nodes),
        out_shape=[
            jax.ShapeDtypeStruct((width, rank), bf16),
            jax.ShapeDtypeStruct(matrix_shape, bf16),
            pltpu.HBM((nodes - 1, rows, rank), bf16),
        ]
        + [jax.ShapeDtypeStruct(*state) for state in states(early)],
        in_specs=[SMEM, HBM] + [ANY] * (nodes - 1) + [VMEM] * early,
        out_specs=[VMEM, VMEM, HBM] + [VMEM] * 4,
        scratch_shapes=[pltpu.SemaphoreType.DMA, pltpu.SemaphoreType.DMA((nodes - 1,))],
        compiler_params=limit(early * state_bytes),
        cost_estimate=pl.CostEstimate(flops=early * (1 << 29), bytes_accessed=early * state_bytes, transcendentals=early * n * width),
        name="early",
    )(place, *in_hbm(pieces[0]), *pieces[1:], *(every[slot] for slot in slots[:early]))
    counts = [early]
    if middle:
        counts.append(len(middle))
        started += pl.pallas_call(
            between_kernel,
            out_shape=[jax.ShapeDtypeStruct(*state) for state in states(len(middle))],
            in_specs=[VMEM] * (1 + len(middle)),
            out_specs=[VMEM] * 4,
            compiler_params=limit(len(middle) * state_bytes),
            cost_estimate=pl.CostEstimate(flops=1 << 20, bytes_accessed=1 << 10, transcendentals=0),
            name="between",
        )(block, *(every[slot] for slot in middle))
    late = feeders - sum(counts)
    heads = pl.pallas_call(
        functools.partial(heads_kernel, slots, counts),
        out_shape=jax.ShapeDtypeStruct((feeders, 8, width), f32),
        in_specs=[SMEM] + [VMEM] * (1 + feeders + len(started)),
        out_specs=VMEM,
        scratch_shapes=[pltpu.VMEM(*state) for state in states(max(late, 1))[:3]]
        + [
            pltpu.VMEM((feeders, 2 * n, width), f32),
            pltpu.VMEM((feeders, 8, width), f32),
            pltpu.VMEM((feeders, 8, width), f32),
        ],
        compiler_params=limit(feeders * state_bytes + feeders * (2 * n + 16) * width * 4),
        name="heads",
    )(place, block, *(every[slot] for slot in slots), *started)
    given = lax.all_to_all(heads, "feeder", 0, 0, axis_index_groups=[list(range(feeders))[::-1]], tiled=True)

    chunks = scen // width
    swing, drop = pl.pallas_call(
        first_kernel,
        out_shape=(
            jax.ShapeDtypeStruct((chunks, n, width), f32),
            jax.ShapeDtypeStruct((chunks, 2 * n, width), f32),
        ),
        in_specs=[SMEM, VMEM, HBM, HBM, HBM],
        out_specs=(VMEM, VMEM),
        scratch_shapes=[
            pltpu.VMEM((n, rank), bf16),
            pltpu.VMEM((nodes, rows, rank), bf16),
            pltpu.SemaphoreType.DMA((nodes + 1,)),
        ],
        compiler_params=limit(3 * n * scen * 4 + scen * rank * 2),
        cost_estimate=pl.CostEstimate(flops=2 * scen * n * rank * 4, bytes_accessed=3 * n * scen * 4, transcendentals=scen * n),
        name="first",
    )(node.reshape(1), own, *in_hbm(loadings, factors, kept))
    return pl.pallas_call(
        functools.partial(volts_kernel, share),
        out_shape=(
            jax.ShapeDtypeStruct((scen, n), f32),
            jax.ShapeDtypeStruct((scen, n), f32),
        ),
        in_specs=[VMEM] * 4,
        out_specs=(HBM, HBM),
        scratch_shapes=[pltpu.VMEM((2, scen, n), f32), pltpu.SemaphoreType.DMA((2, chunks))],
        compiler_params=limit(5 * n * scen * 4),
        name="volts",
    )(own, swing, drop, given)


def solution(mesh):
    feeders = mesh.shape["feeder"]
    nodes = mesh.shape["node"]
    return jax.shard_map(
        functools.partial(local, feeders, nodes),
        mesh=mesh,
        in_specs=(
            P("node", None),
            P(("feeder", "node"), None),
            P(("feeder", "node")),
            P(None, ("feeder", "node")),
            P(None, ("feeder", "node")),
            P(None, "feeder", "node"),
        ),
        out_specs=(P(None, ("feeder", "node")), P(None, ("feeder", "node"))),
        check_vma=False,
    )
```

```python
import functools

import jax
import jax.numpy as jnp
from jax import lax
from jax.experimental import pallas as pl
from jax.experimental.pallas import tpu as pltpu
from jax.sharding import PartitionSpec as P

SWEEPS = 3
EXTRA = 16
LANES = 128

VMEM = pl.BlockSpec(memory_space=pltpu.VMEM)
SMEM = pl.BlockSpec(memory_space=pltpu.SMEM)
HBM = pl.BlockSpec(memory_space=pltpu.HBM)
ANY = pl.BlockSpec(memory_space=pl.ANY)


def split(x):
    high = x.astype(jnp.bfloat16)
    low = (x - high.astype(jnp.float32)).astype(jnp.bfloat16)
    return high, low


def product(left, right):
    return jnp.dot(left, right, preferred_element_type=jnp.float32)


def product_nt(left, right):
    return lax.dot_general(left, right, (((1,), (1,)), ((), ())), preferred_element_type=jnp.float32)


def wide(row, width):
    n = row.shape[1]
    if width <= n:
        return row[:, :width]
    return jnp.concatenate([row] * (width // n), axis=1)


def pack_kernel(
    place_ref, trunk_ref, loadings_ref, parents_ref, base_ref, z_ref, factors_ref, out_ref, block_ref,
    trunk, loads, owners, rows_ref, meta_ref, sems,
):
    n = loadings_ref.shape[0]
    width = block_ref.shape[0]
    offset = pl.multiple_of(place_ref[1], width)
    copies = [
        pltpu.make_async_copy(loadings_ref, loads, sems.at[0]),
        pltpu.make_async_copy(parents_ref, owners, sems.at[1]),
        pltpu.make_async_copy(base_ref, rows_ref.at[0], sems.at[2]),
        pltpu.make_async_copy(z_ref, rows_ref.at[1], sems.at[3]),
        pltpu.make_async_copy(trunk_ref, trunk, sems.at[4]),
        pltpu.make_async_copy(factors_ref.at[pl.ds(offset, width), :], block_ref, sems.at[5]),
    ]
    for copy in copies:
        copy.start()
    for copy in copies[1:5]:
        copy.wait()
    pair_ids = lax.broadcasted_iota(jnp.int32, (2, n), 0)
    trunk_rows = jnp.where(pair_ids == 0, trunk[0], trunk[1])
    for index, rows in enumerate((rows_ref[0], rows_ref[1], trunk_rows)):
        high = rows.astype(jnp.bfloat16).astype(jnp.float32)
        middle = (rows - high).astype(jnp.bfloat16).astype(jnp.float32)
        meta_ref[2 * index : 2 * index + 2, 0:n] = high
        meta_ref[2 * index : 2 * index + 2, n : 2 * n] = middle
        meta_ref[8 + 2 * index : 10 + 2 * index, 0:n] = rows - high - middle
    meta_ref[6:8, 0:n] = jnp.broadcast_to(owners[...].astype(jnp.float32), (2, n))
    meta_ref[6:8, n : 2 * n] = jnp.zeros((2, n), jnp.float32)
    meta_ref[14:16, 0:n] = jnp.zeros((2, n), jnp.float32)
    meta_ref[8:16, n : 2 * n] = jnp.zeros((8, n), jnp.float32)
    meta = meta_ref[...].astype(jnp.bfloat16)
    copies[0].wait()
    out_ref[0:n, :] = loads[...]
    out_ref[n : n + EXTRA, :] = meta
    copies[5].wait()


def constants(section_ref, n):
    meta = section_ref[n : n + EXTRA, :].astype(jnp.float32)
    high, middle = meta[0:8, 0:n], meta[0:8, n : 2 * n]
    return high, middle, high + middle + meta[8:16, 0:n]


def matrix_steps(sections, n):
    highs, middles, rows = zip(*(constants(section, n) for section in sections))
    row_ids = lax.broadcasted_iota(jnp.int32, (n, n), 0)
    lane_ids = lax.broadcasted_iota(jnp.int32, (n, n), 1)
    section_ids = lax.broadcasted_iota(jnp.int32, (max(8, len(sections)), n), 0)
    stacked = jnp.full(section_ids.shape, -1, jnp.int32)
    for index, row in enumerate(rows):
        stacked = jnp.where(section_ids == index, row[6:7].astype(jnp.int32), stacked)
    known = {1: stacked}

    def ancestor(distance):
        if distance not in known:
            step = 1 << (distance.bit_length() - 1)
            if step == distance:
                step //= 2
            far, near = ancestor(step), ancestor(distance - step)
            known[distance] = jnp.where(near < 0, -1, jnp.take_along_axis(far, jnp.maximum(near, 0), axis=1))
        return known[distance]

    digits = []
    unit = 1
    while unit < n:
        digits.append([ancestor(unit * digit).astype(jnp.float32) for digit in range(1, 8) if unit * digit < n])
        unit *= 8
    last = [found.T for found in digits.pop()]
    yield None

    rows_b, lanes_b = (ids.astype(jnp.float32).astype(jnp.bfloat16) for ids in (row_ids, lane_ids))
    one, zero = jnp.ones((n, n), jnp.bfloat16), jnp.zeros((n, n), jnp.bfloat16)
    identity = jnp.where(rows_b == lanes_b, one, zero)
    products = [None] * len(sections)
    for index in range(len(sections)):
        for digit in digits:
            factor = identity
            for found in digit:
                row = jnp.broadcast_to(found[index : index + 1, :].astype(jnp.bfloat16), (n, n))
                factor = jnp.where(rows_b == row, one, factor)
            done = products[index]
            products[index] = factor if done is None else product(done, factor).astype(jnp.bfloat16)
    yield None

    paths = []
    for index in range(len(sections)):
        factor = identity
        for found in last:
            column = jnp.broadcast_to(found[:, index : index + 1], (n, n)).astype(jnp.bfloat16)
            factor = jnp.where(lanes_b == column, one, factor)
        paths.append(product_nt(factor, products[index]).astype(jnp.bfloat16))
    yield None

    shared = []
    for path, high, middle in zip(paths, highs, middles):
        wide_path = path.astype(jnp.float32)

        def scaled(index):
            return jnp.concatenate([wide_path * high[index : index + 1], wide_path * middle[index : index + 1]], axis=1)

        left = jnp.concatenate([scaled(2), scaled(3)], axis=0).astype(jnp.bfloat16)
        shared.append(product_nt(left, jnp.concatenate([path, path], axis=1)))
    yield None

    pad_ids = lax.broadcasted_iota(jnp.int32, (EXTRA, 2 * n), 0)
    out = []
    for both, row in zip(shared, rows):
        resist, react = both[:n], both[n:]
        base_active, base_reactive = row[0:1], row[1:2]
        real_high, real_low = split(resist * base_active + react * base_reactive)
        imag_high, imag_low = split(react * base_active - resist * base_reactive)
        row_real = jnp.concatenate([base_active, base_reactive], axis=1)
        row_imag = jnp.concatenate([-base_reactive, base_active], axis=1)
        sums_high, sums_low = split(jnp.where(pad_ids == 0, row_real, jnp.where(pad_ids == 1, row_imag, 0.0)))

        def whole(real_part, imag_part, sums_part):
            top = jnp.concatenate([real_part, -imag_part], axis=1)
            bottom = jnp.concatenate([imag_part, real_part], axis=1)
            return jnp.concatenate([top, bottom, sums_part], axis=0)

        out.append(
            jnp.concatenate(
                [whole(real_high, imag_high, sums_high), whole(real_low, imag_low, sums_low)], axis=1
            )
        )
    yield out


def swing_of(loadings, factors):
    level = product_nt(loadings, factors).astype(jnp.bfloat16).astype(jnp.float32)
    return 1.0 + 0.5 * jnp.tanh(level)


def apply(matrix, u):
    span = matrix.shape[1] // 2
    high, low = split(u)
    left = jnp.concatenate([matrix, matrix[:, :span]], axis=1)
    return product(left, jnp.concatenate([high, high, low], axis=0))


def apply_first(matrix, swing):
    n = matrix.shape[1] // 4
    high, low = split(swing)
    high_part, low_part = matrix[:, :n], matrix[:, 2 * n : 3 * n]
    return product(
        jnp.concatenate([high_part, low_part, high_part], axis=1), jnp.concatenate([high, high, low], axis=0)
    )


def inverse_of(swing, real, imag):
    return swing * pltpu.reciprocal(real * real + imag * imag, approx=True)


def scaled_volts(swing, real, imag):
    inverse = inverse_of(swing, real, imag)
    return jnp.concatenate([real * inverse, imag * inverse], axis=0)


def first_sweep(sections, factors_ref, matrix_ref, swing_ref, drop_ref, inject_ref, arrived=None):
    n = swing_ref.shape[1]
    for start in range(0, len(sections), 8):
        group = list(enumerate(sections))[start : start + 8]
        steps = matrix_steps([section for _, section in group], n)
        next(steps)
        if start == 0 and arrived is not None:
            arrived()
        for slot, section in group:
            swing_ref[slot] = swing_of(section[0:n, :], factors_ref[...])
        *_, matrices = steps
        for (slot, _), matrix in zip(group, matrices):
            matrix_ref[slot] = matrix
            out = apply_first(matrix_ref[slot], swing_ref[slot])
            drop_ref[slot] = out[: 2 * n]
            inject_ref[slot] = out[2 * n :]


def between_kernel(factors_ref, *refs):
    first_sweep(refs[:-4], factors_ref, *refs[-4:])


def early_kernel(pieces, place_ref, *refs):
    piece_refs, sections = refs[:pieces], refs[pieces:-9]
    factors_ref, own_ref, kept_ref, matrix_ref, swing_ref, drop_ref, inject_ref, sem, keep_sems = refs[-9:]
    width = factors_ref.shape[0]
    piece, offset = place_ref[0], place_ref[1]
    keeps = [
        pltpu.make_async_copy(piece_ref, kept_ref.at[index], keep_sems.at[index])
        for index, piece_ref in enumerate(piece_refs[1:])
    ]
    for copy in keeps:
        copy.start()
    for index, piece_ref in enumerate(piece_refs):
        @pl.when(piece == index)
        def _(piece_ref=piece_ref, index=index):
            rows = piece_ref.at[pl.ds(pl.multiple_of(offset, width), width), :] if index else piece_ref
            pltpu.make_async_copy(rows, factors_ref, sem).start()

    def arrived():
        pltpu.make_async_copy(piece_refs[0], factors_ref, sem).wait()

    first_sweep(sections, factors_ref, matrix_ref, swing_ref, drop_ref, inject_ref, arrived)
    own_ref[...] = matrix_ref[0]
    for copy in keeps:
        copy.wait()


def heads_kernel(slots, counts, place_ref, factors_ref, *refs):
    feeders, early = len(slots), sum(counts)
    sections, refs = refs[:feeders], refs[feeders:]
    done = []
    for count in counts:
        done += [[ref.at[index] for ref in refs[:4]] for index in range(count)]
        refs = refs[4:]
    head_ref, matrix_ref, swing_ref, drop_ref, again_ref, flow_ref, trunk_ref = refs
    width = factors_ref.shape[0]
    n = swing_ref.shape[1]
    place = [jnp.bitwise_xor(place_ref[2], slot) for slot in slots]
    late_refs = (matrix_ref, swing_ref, drop_ref)

    def of(index, which):
        return done[index][which] if index < early else late_refs[which].at[index - early]

    def flow_of(index, real, imag):
        base = constants(sections[index], n)[2].T
        active, reactive = base[:, 0:1], base[:, 1:2]
        if imag is None:
            parts = (active * real, -reactive * real)
        else:
            parts = (active * real + reactive * imag, active * imag - reactive * real)
        return [jnp.sum(part, axis=0, keepdims=True) for part in parts]

    groups = [list(range(start, min(start + 8, feeders))) for start in range(early, feeders, 8)]
    steps = [matrix_steps([sections[index] for index in group], n) for group in groups]
    if steps:
        next(steps[0])
    for index in range(feeders):
        row = constants(sections[index], n)[2]
        trunk_ref[place[index], 0:2, :] = wide(row[4:6], width)
        if index < early:
            flow_ref[place[index]] = of(index, 3)[0:8, :]
        else:
            swing = swing_of(sections[index][0:n, :], factors_ref[...])
            of(index, 1)[...] = swing
            for part, total in enumerate(flow_of(index, swing, None)):
                flow_ref[place[index], part : part + 1, :] = total

    def heads(sweep):
        flows = [None] * feeders
        real = jnp.zeros((1, width), jnp.float32)
        imag = real
        for g in reversed(range(feeders)):
            real = real + flow_ref[g, 0:1, :]
            imag = imag + flow_ref[g, 1:2, :]
            flows[g] = (real, imag)
        head_real = jnp.ones((1, width), jnp.float32)
        head_imag = jnp.zeros((1, width), jnp.float32)
        for g in range(feeders):
            r, x = trunk_ref[g, 0:1, :], trunk_ref[g, 1:2, :]
            real, imag = flows[g]
            head_real = head_real - (r * real - x * imag)
            head_imag = head_imag - (r * imag + x * real)
            head_ref[feeders - 1 - g, 2 * sweep : 2 * sweep + 1, :] = head_real
            head_ref[feeders - 1 - g, 2 * sweep + 1 : 2 * sweep + 2, :] = head_imag

    def volts(index, sweep):
        drop = of(index, 2) if sweep == 1 else again_ref.at[index]
        rank = feeders - 1 - place[index]
        real = head_ref[rank, 2 * sweep - 2 : 2 * sweep - 1, :] - drop[0:n, :]
        imag = head_ref[rank, 2 * sweep - 1 : 2 * sweep, :] - drop[n : 2 * n, :]
        return real, imag

    def middle(index, sweep):
        out = apply(of(index, 0)[...], scaled_volts(of(index, 1)[...], *volts(index, sweep)))
        again_ref[index] = out[: 2 * n]
        flow_ref[place[index]] = out[2 * n : 2 * n + 8]

    heads(0)
    ready = list(range(early))
    for group, step in zip(groups, steps):
        for matrices in step:
            if ready:
                middle(ready.pop(0), 1)
        for index, matrix in zip(group, matrices):
            of(index, 0)[...] = matrix
            of(index, 2)[...] = apply_first(matrix, of(index, 1)[...])[: 2 * n]
    for index in ready + list(range(early, feeders)):
        middle(index, 1)
    heads(1)
    for sweep in range(2, SWEEPS):
        for index in range(feeders):
            if sweep < SWEEPS - 1:
                middle(index, sweep)
            else:
                real, imag = volts(index, sweep)
                inverse = inverse_of(of(index, 1)[...], real, imag)
                for part, total in enumerate(flow_of(index, real * inverse, imag * inverse)):
                    flow_ref[place[index], part : part + 1, :] = total
        heads(sweep)
    for g in range(feeders):
        head_ref[g, 2 * SWEEPS :, :] = jnp.zeros((head_ref.shape[1] - 2 * SWEEPS, width), jnp.float32)


def first_kernel(
    node_ref, matrix_ref, loadings_ref, rows_ref, kept_ref, swing_ref, drop_ref, loads, factors_ref, sems
):
    n = loadings_ref.shape[0]
    width = swing_ref.shape[2]
    pieces = 1 + kept_ref.shape[0]
    chunks = rows_ref.shape[0] // width
    copies = [pltpu.make_async_copy(loadings_ref, loads, sems.at[pieces])]
    for index in range(pieces):
        piece_ref = kept_ref.at[index - 1] if index else rows_ref
        copies.append(pltpu.make_async_copy(piece_ref, factors_ref.at[index], sems.at[index]))
    for copy in copies:
        copy.start()
    matrix = matrix_ref[0 : 2 * n, :]
    for copy in copies:
        copy.wait()
    loadings = loads[...]
    together = 4 // chunks if chunks < 4 else 1

    @pl.loop(0, pieces // together)
    def _(outer):
        for inner in range(together):
            index = outer * together + inner
            for part in range(chunks):
                chunk = jnp.bitwise_xor(node_ref[0], index) * chunks + part
                swing = swing_of(loadings, factors_ref[index, part * width : (part + 1) * width, :])
                swing_ref[chunk] = swing
                drop_ref[chunk] = apply_first(matrix, swing)


def volts_kernel(share, matrix_ref, swing_ref, drop_ref, head_ref, real_ref, imag_ref, out_ref, sems):
    n = swing_ref.shape[1]
    chunks, width = swing_ref.shape[0], swing_ref.shape[2]
    matrix = matrix_ref[0 : 2 * n, :]
    drops = [None] * chunks
    copies = []

    def advance(chunk, sweep):
        drop = drop_ref[chunk] if sweep == 0 else drops[chunk]
        giver = head_ref.shape[0] - 1 - chunk * share
        real = head_ref[giver, 2 * sweep : 2 * sweep + 1, :] - drop[:n]
        imag = head_ref[giver, 2 * sweep + 1 : 2 * sweep + 2, :] - drop[n:]
        if sweep < SWEEPS - 1:
            drops[chunk] = apply(matrix, scaled_volts(swing_ref[chunk], real, imag))
            return
        rows = slice(chunk * width, (chunk + 1) * width)
        for index, (part, to_ref) in enumerate(((real, real_ref), (imag, imag_ref))):
            out_ref[index, rows, :] = part.T
            copies.append(pltpu.make_async_copy(out_ref.at[index, rows, :], to_ref.at[rows, :], sems.at[index, chunk]))
            copies[-1].start()

    for turn in range(chunks + SWEEPS - 1):
        for sweep in reversed(range(SWEEPS)):
            if 0 <= turn - sweep < chunks:
                advance(turn - sweep, sweep)
    for copy in copies:
        copy.wait()


def after_kernel(*refs):
    del refs


def after(array, *others):
    return pl.pallas_call(
        after_kernel,
        out_shape=jax.ShapeDtypeStruct(array.shape, array.dtype),
        in_specs=[ANY] * (1 + len(others)),
        out_specs=ANY,
        input_output_aliases={0: 0},
        compiler_params=limit(0),
        name="after",
    )(array, *others)


def in_hbm(*arrays):
    return [pltpu.with_memory_space_constraint(array, pltpu.HBM) for array in arrays]


def limit(nbytes):
    return pltpu.CompilerParams(vmem_limit_bytes=min(60 << 20, int(nbytes) + (16 << 20)))


def local(feeders, nodes, factors, loadings, parents, load_base, lateral_z, trunk_z):
    node = lax.axis_index("node").astype(jnp.int32)
    feeder = lax.axis_index("feeder").astype(jnp.int32)
    rows, rank = factors.shape
    scen = rows * nodes
    n = loadings.shape[0]
    width = max(scen // feeders, LANES)
    share = feeders * width // scen
    f32, bf16 = jnp.float32, jnp.bfloat16
    matrix_shape = (2 * n + EXTRA, 4 * n)

    def trade(block, offset):
        return lax.ppermute(block, "node", [(i, i ^ offset) for i in range(nodes)])

    held = {0: factors}
    far = nodes // 2
    if far:
        held[far] = trade(factors, far)

    start = (feeder // share) * width
    place = jnp.stack([(start // rows) ^ node, start % rows, feeder])

    packed, own_rows = pl.pallas_call(
        pack_kernel,
        out_shape=(jax.ShapeDtypeStruct((n + EXTRA, rank), bf16), jax.ShapeDtypeStruct((width, rank), bf16)),
        in_specs=[SMEM] + [HBM] * 6,
        out_specs=(VMEM, VMEM),
        scratch_shapes=[
            pltpu.SMEM((2,), f32),
            pltpu.VMEM((n, rank), bf16),
            pltpu.VMEM((1, n), jnp.int32),
            pltpu.VMEM((2, 2, n), f32),
            pltpu.VMEM((EXTRA, rank), f32),
            pltpu.SemaphoreType.DMA((6,)),
        ],
        compiler_params=limit(2 * (n + EXTRA) * rank * 2),
        name="pack",
    )(place, *in_hbm(trunk_z.reshape(2), loadings, parents.reshape(1, n), load_base, lateral_z, factors))

    def swap(block, offset):
        return lax.ppermute(block, "feeder", [(i, i ^ offset) for i in range(feeders)])

    every = {0: packed}
    for offset in sorted(range(2, feeders, 2), key=lambda o: -(o & -o)):
        every[offset] = swap(packed, offset)
    every[1] = swap(packed, 1)
    slots = list(every)
    early = len(slots)
    middle = [3] if 2 in every else []
    for offset in middle:
        every[offset] = swap(every[1], offset ^ 1)
    for offset in slots[1:-1]:
        if offset + 1 not in every:
            every[offset + 1] = swap(every[offset], 1)
    slots = list(every)

    if far:
        held[far] = after(held[far], *(every[slot] for slot in slots[:early]))
    step = far // 2
    while step >= 1:
        for offset in list(held):
            held[offset ^ step] = trade(held[offset], step)
        step //= 2
    pieces = [held[offset] for offset in range(nodes)]

    def states(count):
        return [
            ((count, *matrix_shape), bf16),
            ((count, n, width), f32),
            ((count, 2 * n, width), f32),
            ((count, EXTRA, width), f32),
        ]

    state_bytes = (2 * n + EXTRA) * 8 * n + (3 * n + EXTRA) * width * 4 + (n + EXTRA) * rank * 2
    block, own, kept, *started = pl.pallas_call(
        functools.partial(early_kernel, nodes),
        out_shape=[
            jax.ShapeDtypeStruct((width, rank), bf16),
            jax.ShapeDtypeStruct(matrix_shape, bf16),
            pltpu.HBM((nodes - 1, rows, rank), bf16),
        ]
        + [jax.ShapeDtypeStruct(*state) for state in states(early)],
        in_specs=[SMEM, VMEM] + [ANY] * (nodes - 1) + [VMEM] * early,
        out_specs=[VMEM, VMEM, HBM] + [VMEM] * 4,
        scratch_shapes=[pltpu.SemaphoreType.DMA, pltpu.SemaphoreType.DMA((nodes - 1,))],
        compiler_params=limit(early * state_bytes),
        cost_estimate=pl.CostEstimate(flops=early * (1 << 29), bytes_accessed=early * state_bytes, transcendentals=early * n * width),
        name="early",
    )(place, own_rows, *pieces[1:], *(every[slot] for slot in slots[:early]))
    counts = [early]
    if middle:
        counts.append(len(middle))
        started += pl.pallas_call(
            between_kernel,
            out_shape=[jax.ShapeDtypeStruct(*state) for state in states(len(middle))],
            in_specs=[VMEM] * (1 + len(middle)),
            out_specs=[VMEM] * 4,
            compiler_params=limit(len(middle) * state_bytes),
            cost_estimate=pl.CostEstimate(flops=1 << 20, bytes_accessed=1 << 10, transcendentals=0),
            name="between",
        )(block, *(every[slot] for slot in middle))
    late = feeders - sum(counts)
    heads = pl.pallas_call(
        functools.partial(heads_kernel, slots, counts),
        out_shape=jax.ShapeDtypeStruct((feeders, 8, width), f32),
        in_specs=[SMEM] + [VMEM] * (1 + feeders + len(started)),
        out_specs=VMEM,
        scratch_shapes=[pltpu.VMEM(*state) for state in states(max(late, 1))[:3]]
        + [
            pltpu.VMEM((feeders, 2 * n, width), f32),
            pltpu.VMEM((feeders, 8, width), f32),
            pltpu.VMEM((feeders, 8, width), f32),
        ],
        compiler_params=limit(feeders * state_bytes + feeders * (2 * n + 16) * width * 4),
        name="heads",
    )(place, block, *(every[slot] for slot in slots), *started)
    given = lax.all_to_all(heads, "feeder", 0, 0, axis_index_groups=[list(range(feeders))[::-1]], tiled=True)

    chunks = scen // width
    swing, drop = pl.pallas_call(
        first_kernel,
        out_shape=(
            jax.ShapeDtypeStruct((chunks, n, width), f32),
            jax.ShapeDtypeStruct((chunks, 2 * n, width), f32),
        ),
        in_specs=[SMEM, VMEM, HBM, HBM, HBM],
        out_specs=(VMEM, VMEM),
        scratch_shapes=[
            pltpu.VMEM((n, rank), bf16),
            pltpu.VMEM((nodes, rows, rank), bf16),
            pltpu.SemaphoreType.DMA((nodes + 1,)),
        ],
        compiler_params=limit(3 * n * scen * 4 + scen * rank * 2),
        cost_estimate=pl.CostEstimate(flops=2 * scen * n * rank * 4, bytes_accessed=3 * n * scen * 4, transcendentals=scen * n),
        name="first",
    )(node.reshape(1), own, *in_hbm(loadings, factors, kept))
    return pl.pallas_call(
        functools.partial(volts_kernel, share),
        out_shape=(
            jax.ShapeDtypeStruct((scen, n), f32),
            jax.ShapeDtypeStruct((scen, n), f32),
        ),
        in_specs=[VMEM] * 4,
        out_specs=(HBM, HBM),
        scratch_shapes=[pltpu.VMEM((2, scen, n), f32), pltpu.SemaphoreType.DMA((2, chunks))],
        compiler_params=limit(5 * n * scen * 4),
        name="volts",
    )(own, swing, drop, given)


def solution(mesh):
    feeders = mesh.shape["feeder"]
    nodes = mesh.shape["node"]
    return jax.shard_map(
        functools.partial(local, feeders, nodes),
        mesh=mesh,
        in_specs=(
            P("node", None),
            P(("feeder", "node"), None),
            P(("feeder", "node")),
            P(None, ("feeder", "node")),
            P(None, ("feeder", "node")),
            P(None, "feeder", "node"),
        ),
        out_specs=(P(None, ("feeder", "node")), P(None, ("feeder", "node"))),
        check_vma=False,
    )
```
